32 devices in a mesh: groups: 2 (over y), ep: 4 (over z), tp: 2 (over x), sub: 2 (over core).
Axes of the slice: x: 2, y: 2, z: 4, core: 2. Of those that a mesh axis runs over, the one named last changes fastest.
Arguments:
- queries: bfloat16 [2048, 4096], P(('groups', 'ep', 'sub'), 'tp'), parts along dimension 0, may hold values from -8 to 8
- key_rows: bfloat16 [2048, 512], P(('groups', 'ep', 'sub'), 'tp'), parts along dimension 0, may hold values from -5 to 5
- value_rows: bfloat16 [2048, 512], P(('groups', 'ep', 'sub'), 'tp'), parts along dimension 0, may hold values from -12 to 12
- sink_logits: float32 [64], P('tp'), may hold values from 2 to 6
- out_weight: bfloat16 [4096, 2880], P('tp', 'ep'), may hold values from -0.09375 to 0.09375
- residual: bfloat16 [2048, 2880], P(('groups', 'ep', 'sub')), parts along dimension 0, may hold values from -12 to 12
- norm_gain: float32 [2880], replicated, may hold values from 0.1 to 1.9
- expert_in: bfloat16 [8, 2, 2880, 1440], P(('ep', 'sub'), None, None, 'tp'), may hold values from -0.109375 to 0.109375
- expert_out: bfloat16 [8, 1440, 2880], P(('ep', 'sub'), None, 'tp'), may hold values from -0.15625 to 0.15625
- routes: int32 [2048, 4], P(('groups', 'ep', 'sub')), parts along dimension 0, may hold values from 0 to 7, all different within a row; in each aligned block of 128 rows (0 to 127, 128 to 255, ...) at most 128 rows name the same one
- route_scores: int32 [2048, 4], P(('groups', 'ep', 'sub')), parts along dimension 0, may hold values from 1 to 1023
Outputs:
- mixed_out: bfloat16 [2048, 2880], P(('groups', 'ep', 'sub'), 'tp'), parts along dimension 0
The draws below stay inside these ranges and needn't reach their ends.
There are 2 independent parts, one for each index of `groups`. The reference program is written for one: setup_inputs(seed, part) draws one part's arguments, and reference() takes and returns one part's arrays. A program takes and returns all parts, laid end to end along the dimension named above; an argument that names none is the same for every part. Nothing has to cross between parts.
Inputs may be any that keep to these rules, and one draw needn't show every extreme that they name: `routes`: each row names 4 different experts. Within the 128 rows of one index of ep+sub no expert is named by more than 128 rows, a bound that some block reaches of them.
All inputs are finite; a program needn't handle non-finite values.
Results may differ from the reference program's by a relative error of at most 0.0044.
Values may be sent and summed in bfloat16 or wider, within the bound.
No kernel may reach another device: no remote copies, remote signals or barrier semaphores. Data moves between devices by JAX's collectives and lax.ppermute only.
A program may use at most 128 MiB of HBM per device.

```python
import math
import jax
import jax.numpy as jnp
import numpy as np
from jax import lax

D = 2880
HEADS = 64
KVH = 8
HD = 64
WIN = 128
TOP = 4
FFW = 1440
TOK_DEV = 128
TOKENS = 1024
EXPERTS = 8
CAP = 128


def draw_queries(key, part):
    key = jax.random.fold_in(key, 5)
    draw_base = jnp.clip(jax.random.normal(key, (TOKENS, HEADS, HD)), -4.0, 4.0)
    return draw_base.reshape(TOKENS, HEADS * HD).astype(jnp.bfloat16)


def draw_key_rows(key, part):
    key = jax.random.fold_in(key, 9)
    draw_base = jnp.clip(jax.random.normal(key, (TOKENS, KVH, HD)), -4.0, 4.0)
    return draw_base.reshape(TOKENS, KVH * HD).astype(jnp.bfloat16)


def draw_residual(key, part):
    key = jax.random.fold_in(key, 23)
    column = jnp.arange(D, dtype=jnp.float32) / (D - 1)
    rising = 1.0 + 2.0 * column
    result = jnp.clip(jax.random.normal(key, (TOKENS, D)), -4.0, 4.0) * rising[None, :]
    return result.astype(jnp.bfloat16)


def place_ends(drawn, rng, low, high):
    shape = drawn.shape
    index_at = [jax.random.randint(jax.random.fold_in(rng, axis), (), 0, shape[axis]) for axis in range(len(shape))]
    drawn = drawn.at[tuple(index_at)].set(low)
    longest = shape.index(max(shape))
    index_at[longest] = (index_at[longest] + 1) % shape[longest]
    return drawn.at[tuple(index_at)].set(high)


def steps_of(rng, extent, cuts, smallest, high):
    level = 1.0
    for dim, parts in cuts:
        steps = jax.random.uniform(jax.random.fold_in(jax.random.fold_in(rng, 6), dim), (parts,), jnp.float32, smallest / len(cuts), high / len(cuts))
        level = level * jnp.repeat(jnp.exp(steps), extent[dim] // parts).reshape((-1,) + (1,) * (len(extent) - 1 - dim))
    return level


def assign_block(rng, own, number, rows, number_of, top, reach, slope):
    ranking = jax.random.permutation(rng, number_of)
    crowded, common = shares(number_of, rows * top, reach, slope, True), shares(number_of, rows * top, reach, slope, False)
    places = jnp.arange(number_of)

    def named(lengths, offset_by):
        used = int((lengths > 0).sum())
        fixed = max(1, used // 4)
        passed = fixed + (places - fixed + offset_by * (used - fixed)) % max(1, number_of - fixed)
        return jnp.zeros((number_of,), jnp.int32).at[ranking[jnp.where(places < fixed, places, passed)]].set(jnp.asarray(lengths, jnp.int32))

    lengths = jnp.where(number % 4 == 0, named(crowded, number // 4), named(common, number - number // 4 - 1))
    mixed = jax.random.permutation(jax.random.fold_in(own, 3), number_of)
    source_of, sink = mixed[0:number_of // 2 * 2:2], mixed[1:number_of // 2 * 2:2]
    slack = jnp.minimum(lengths[source_of] - 1, reach - lengths[sink]) // 2
    slack = jnp.where((source_of == ranking[0]) | (sink == ranking[0]) | (lengths[sink] == 0), 0, jnp.maximum(slack, 0))
    passed = jax.random.randint(jax.random.fold_in(own, 4), (number_of // 2,), 0, 1 << 20) % (slack + 1)
    lengths = lengths.at[source_of].add(-passed).at[sink].add(passed)
    members = jnp.searchsorted(jnp.cumsum(lengths), jnp.arange(rows * top), side="right").astype(jnp.int32)
    table = members.reshape(top, rows).T
    table = table[jax.random.permutation(jax.random.fold_in(own, 1), rows)]
    offset_by = jax.random.randint(jax.random.fold_in(own, 2), (rows, 1), 0, top)
    return jnp.take_along_axis(table, (jnp.arange(top)[None, :] + offset_by) % top, axis=1)


def shares(count, total, limit, slope, full):
    loads = [(1 << 20) // math.isqrt(standing ** slope) + 1 for standing in range(1, count + 1)]
    largest = limit if full else min(limit, max(-(-total // count), total * loads[0] // sum(loads)))
    least = 1 if total - largest >= count - 1 else 0
    holding, spare = [largest] + [least] * (count - 1), total - largest - least * (count - 1)
    while spare > 0:
        movable = [i for i in range(1, count) if holding[i] < largest] or [i for i in range(1, count) if holding[i] < limit]
        whole, remaining = sum([loads[i] for i in movable]), spare
        for i in movable:
            addition = min(limit - holding[i], max(1, remaining * loads[i] // whole), spare)
            holding[i] = holding[i] + addition
            spare = spare - addition
    return np.array(holding)


def noise(rng, extent, deviation, reach, pieces=(), held_as=jnp.bfloat16):
    factor_of = steps_of(rng, extent, pieces, -0.22, 0.18) if pieces else 1.0
    values = jax.random.normal(rng, extent, jnp.float32) * deviation * factor_of
    return jnp.minimum(jnp.maximum(values, -reach), reach).astype(held_as)


def setup_inputs(seed: int = 0, part: int = 0) -> dict:
    splits = jax.random.split(jax.random.key(seed), 12)
    part_keys = jax.random.split(jax.random.fold_in(splits[11], part), 12)
    queries = draw_queries(jax.random.fold_in(jax.random.fold_in(splits[11], part), 71), part)
    key_rows = draw_key_rows(jax.random.fold_in(jax.random.fold_in(splits[11], part), 71), part)
    value_rows = noise(part_keys[2], (TOKENS, KVH * HD), 3.0, 12.0, ((0, 8), (1, 2)))
    sink_logits = jnp.clip(2.0 + 4.0 * jax.random.uniform(splits[3], (HEADS,), jnp.float32) ** steps_of(splits[3], (HEADS,), ((0, 2),), -0.2, 0.2), 2.0, 6.0)
    out_weight = noise(splits[4], (HEADS * HD, D), (HEADS * HD) ** -0.5, 0.09375, ((0, 2), (1, 4)))
    residual = draw_residual(jax.random.fold_in(jax.random.fold_in(splits[11], part), 71), part)
    norm_gain = jnp.clip(1.0 + 0.18 * jax.random.normal(splits[6], (D,), jnp.float32), 0.1, 1.9)
    expert_in = noise(splits[7], (EXPERTS, 2, D, FFW), D ** -0.5, 0.109375, ((0, 8), (3, 2)))
    expert_out = noise(splits[8], (EXPERTS, FFW, D), FFW ** -0.5, 0.15625, ((0, 8), (2, 2)))
    routes_keys = jax.random.split(jax.random.fold_in(part_keys[9], 1), TOKENS // TOK_DEV)
    routes_turns = jax.random.permutation(jax.random.fold_in(part_keys[9], 3), TOKENS // TOK_DEV)
    routes = jax.vmap(lambda own, number: assign_block(jax.random.fold_in(part_keys[9], 2), own, number, TOK_DEV, EXPERTS, TOP, CAP, 2))(routes_keys, routes_turns).reshape((TOKENS, TOP))
    route_scores = place_ends(jax.random.randint(part_keys[10], (TOKENS, TOP), 1, 1024), jax.random.fold_in(part_keys[10], 1), 1, 1023).astype(jnp.int32)
    return {"queries": queries, "key_rows": key_rows, "value_rows": value_rows, "sink_logits": sink_logits, "out_weight": out_weight, "residual": residual, "norm_gain": norm_gain, "expert_in": expert_in, "expert_out": expert_out, "routes": routes, "route_scores": route_scores}


def sink_attention(queries, key_rows, value_rows, sink_logits):
    group_size = HEADS // KVH
    block_rows = TOK_DEV
    block_count = TOKENS // block_rows
    window_reach = WIN - 1
    padded_keys = jnp.concatenate([jnp.zeros((window_reach, KVH * HD), key_rows.dtype), key_rows], axis=0)
    padded_values = jnp.concatenate([jnp.zeros((window_reach, KVH * HD), value_rows.dtype), value_rows], axis=0)
    sink_table = sink_logits.reshape(KVH, group_size)

    def one_block(block_index):
        start = block_index * block_rows
        query_rows = lax.dynamic_slice_in_dim(queries, start, block_rows, 0).reshape(block_rows, KVH, group_size, HD).astype(jnp.float32)
        key_part = lax.dynamic_slice_in_dim(padded_keys, start, block_rows + window_reach, 0).reshape(block_rows + window_reach, KVH, HD).astype(jnp.float32)
        value_part = lax.dynamic_slice_in_dim(padded_values, start, block_rows + window_reach, 0).reshape(block_rows + window_reach, KVH, HD).astype(jnp.float32)
        scores = jnp.einsum('pgqd,jgd->gqpj', query_rows, key_part) * HD ** (-0.5)
        query_pos = jnp.arange(block_rows, dtype=jnp.int32)[:, None]
        key_pos = jnp.arange(block_rows + window_reach, dtype=jnp.int32)[None, :]
        allowed = (key_pos >= query_pos) & (key_pos <= query_pos + window_reach) & (start + key_pos >= window_reach)
        masked = jnp.where(allowed, scores, -1e+30)
        largest = jnp.maximum(lax.optimization_barrier(jnp.max(masked, axis=3)), sink_table[:, :, None])
        numerator = jnp.where(allowed, jnp.exp(masked - largest[..., None]), 0.0)
        denominator = lax.optimization_barrier(jnp.sum(numerator, axis=3)) + jnp.exp(sink_table[:, :, None] - largest)
        weights = (numerator / denominator[..., None]).astype(jnp.bfloat16)
        attended = jnp.einsum('gqpj,jgd->pgqd', weights.astype(jnp.float32), value_part)
        return attended.reshape(block_rows, HEADS * HD).astype(jnp.bfloat16)
    blocks = lax.map(one_block, jnp.arange(block_count, dtype=jnp.int32))
    return blocks.reshape(TOKENS, HEADS * HD)

def reference(queries, key_rows, value_rows, sink_logits, out_weight, residual, norm_gain, expert_in, expert_out, routes, route_scores):
    attended = sink_attention(queries, key_rows, value_rows, sink_logits)
    hidden = residual.astype(jnp.float32) + jnp.dot(attended, out_weight, preferred_element_type=jnp.float32)
    square = lax.optimization_barrier(jnp.sum(hidden * hidden, axis=1, keepdims=True))
    normed = (hidden * lax.rsqrt(square / D + 1e-05) * norm_gain).astype(jnp.bfloat16)
    slot_count = EXPERTS * CAP
    flat_routes = routes.reshape(-1).astype(jnp.int32)
    one_hot = (flat_routes[:, None] == jnp.arange(EXPERTS, dtype=jnp.int32)[None, :]).astype(jnp.int32)
    before = jnp.cumsum(one_hot, axis=0) - one_hot
    placed = (lax.optimization_barrier(jnp.sum(before * one_hot, axis=1)) + flat_routes * slot_count).astype(jnp.int32)
    owner_row = jnp.arange(TOKENS * TOP, dtype=jnp.int32) // TOP
    source = jnp.zeros((EXPERTS * slot_count,), jnp.int32).at[placed].set(owner_row)

    def one_expert(expert_index):
        picks = lax.dynamic_slice_in_dim(source, expert_index * slot_count, slot_count, 0)
        picked_rows = jnp.take(normed, picks, axis=0)
        weights_in = expert_in[expert_index]
        gate_part = jnp.dot(picked_rows, weights_in[0], preferred_element_type=jnp.float32)
        up_part = jnp.dot(picked_rows, weights_in[1], preferred_element_type=jnp.float32)
        activated = ((up_part + 1.0) * gate_part * jax.nn.sigmoid(1.702 * gate_part)).astype(jnp.bfloat16)
        return jnp.dot(activated, expert_out[expert_index], preferred_element_type=jnp.float32).astype(jnp.bfloat16)
    results = lax.map(one_expert, jnp.arange(EXPERTS, dtype=jnp.int32))
    flat_results = results.reshape(EXPERTS * slot_count, D)
    picked = jnp.take(flat_results, placed, axis=0).astype(jnp.float32).reshape(TOKENS, TOP, D)
    scores = route_scores.astype(jnp.float32)
    mix_share = scores / lax.optimization_barrier(jnp.sum(scores, axis=1, keepdims=True))
    expert_sum = jnp.einsum('tk,tkd->td', mix_share, picked)
    return (hidden + expert_sum).astype(jnp.bfloat16)
```

```python
import jax
import jax.numpy as jnp
from jax import lax
from jax.sharding import PartitionSpec as P

D = 2880
HD = 64
WIN = 128
TOP = 4


def shifted(block, axis, distance):
    devices = range(lax.axis_size(axis))
    route = [(i - distance, i) for i in devices if i - distance in devices]
    return lax.ppermute(block, axis, route)


def rotated(block, axis, distance):
    count = lax.axis_size(axis)
    return lax.ppermute(block, axis, [(i, (i + distance) % count) for i in range(count)])


def picked(blocks, index, axis):
    return lax.dynamic_index_in_dim(blocks, index, axis, keepdims=False)


def attention(queries, key_rows, value_rows, sink_logits):
    row_count = queries.shape[0]
    head_count = queries.shape[1] // HD
    kv_count = key_rows.shape[1] // HD
    group_size = head_count // kv_count
    window_reach = WIN - 1
    kv_width = kv_count * HD
    paired = jnp.concatenate([key_rows, value_rows], axis=1)
    earlier = shifted(paired[row_count - window_reach :], ("ep", "sub"), 1)
    context = jnp.concatenate([earlier, paired], axis=0)
    key_part = context[:, :kv_width].reshape(row_count + window_reach, kv_count, HD)
    value_part = context[:, kv_width:].reshape(row_count + window_reach, kv_count, HD)
    query_rows = queries.reshape(row_count, kv_count, group_size, HD)
    scores = jnp.einsum(
        "pgqd,jgd->gqpj", query_rows, key_part, preferred_element_type=jnp.float32
    ) * HD ** (-0.5)
    query_pos = jnp.arange(row_count, dtype=jnp.int32)[:, None]
    key_pos = jnp.arange(row_count + window_reach, dtype=jnp.int32)[None, :]
    first_device = lax.axis_index(("ep", "sub")) == 0
    allowed = (key_pos >= query_pos) & (key_pos <= query_pos + window_reach)
    allowed = allowed & jnp.logical_or(jnp.logical_not(first_device), key_pos >= window_reach)
    sink_table = sink_logits.reshape(kv_count, group_size)
    masked = jnp.where(allowed, scores, -1e30)
    largest = jnp.maximum(jnp.max(masked, axis=3), sink_table[:, :, None])
    numerator = jnp.where(allowed, jnp.exp(masked - largest[..., None]), 0.0)
    denominator = jnp.sum(numerator, axis=3) + jnp.exp(sink_table[:, :, None] - largest)
    weights = (numerator / denominator[..., None]).astype(jnp.bfloat16)
    attended = jnp.einsum("gqpj,jgd->pgqd", weights, value_part, preferred_element_type=jnp.float32)
    return attended.reshape(row_count, head_count * HD).astype(jnp.bfloat16)


def activation(rows, scale, expert_in):
    gate = jnp.dot(rows, expert_in[0, 0], preferred_element_type=jnp.float32) * scale
    up = jnp.dot(rows, expert_in[0, 1], preferred_element_type=jnp.float32) * scale
    return ((up + 1.0) * gate * jax.nn.sigmoid(1.702 * gate)).astype(jnp.bfloat16)


def local(
    queries,
    key_rows,
    value_rows,
    sink_logits,
    out_weight,
    residual,
    norm_gain,
    expert_in,
    expert_out,
    routes,
    route_scores,
):
    row_count = queries.shape[0]
    z_count, t_count, s_count = lax.axis_size("ep"), lax.axis_size("tp"), lax.axis_size("sub")
    z, t, s = lax.axis_index("ep"), lax.axis_index("tp"), lax.axis_index("sub")
    part_rows = row_count // t_count
    columns = out_weight.shape[1]
    units = expert_in.shape[3]
    width = expert_out.shape[2]

    experts_in = [expert_in] + [rotated(expert_in, "sub", k) for k in range(1, s_count)]
    experts_out = [expert_out] + [rotated(expert_out, "sub", k) for k in range(1, s_count)]
    experts_out = [
        [lax.dynamic_slice_in_dim(w[0], ((t - m) % t_count) * units, units, 0) for m in range(t_count)]
        for w in experts_out
    ]

    own_residual = picked(residual.reshape(t_count, part_rows, z_count, columns), t, 0)
    residual_parts = [picked(own_residual, z, 1)] + [
        rotated(picked(own_residual, (z + k) % z_count, 1), "ep", k) for k in range(1, z_count)
    ]
    order = (z - jnp.arange(z_count, dtype=jnp.int32)) % z_count
    residual_part = jnp.take(jnp.stack(residual_parts), order, axis=0)

    expert_count = z_count * s_count
    route_float = route_scores.astype(jnp.float32)
    mix_share = route_float / jnp.sum(route_float, axis=1, keepdims=True)
    named = routes[:, :, None] == jnp.arange(expert_count, dtype=jnp.int32)[None, None, :]
    share_table = jnp.sum(jnp.where(named, mix_share[:, :, None], 0.0), axis=1)
    share_table = lax.all_gather(share_table, "ep", axis=0)
    share_table = share_table.reshape(z_count, t_count, part_rows, z_count, s_count)
    share_table = picked(share_table, z, 3)

    attended = attention(queries, key_rows, value_rows, sink_logits)
    gathered = lax.all_gather(attended, "ep", axis=0, tiled=True)
    partial_value = jnp.dot(gathered, out_weight, preferred_element_type=jnp.float32)
    partial_value = partial_value.reshape(z_count, t_count, part_rows, columns)
    hidden = residual_part.astype(jnp.float32) + picked(partial_value, t, 1)
    for m in range(1, t_count):
        sent = picked(partial_value, (t + m) % t_count, 1).astype(jnp.bfloat16)
        hidden = hidden + rotated(sent, "tp", m).astype(jnp.float32)

    gain_part = lax.dynamic_slice_in_dim(norm_gain, z * columns, columns, 0)
    scaled = (hidden * gain_part).astype(jnp.bfloat16).reshape(z_count * part_rows, columns)
    rows = lax.all_gather(scaled, "ep", axis=1, tiled=True)
    row_sets = [rows] + [rotated(rows, "tp", m) for m in range(1, t_count)]

    inverse_gain = 1.0 / norm_gain
    activated = []
    for rows in row_sets:
        plain = rows.astype(jnp.float32) * inverse_gain
        square = jnp.sum(plain * plain, axis=1, keepdims=True)
        scale = lax.rsqrt(square / D + 1e-05)
        activated.append([activation(rows, scale, w) for w in experts_in])

    outputs = []
    for k in range(t_count):
        total = 0.0
        for e in range(s_count):
            result = 0.0
            for m in range(t_count):
                block = activated[(k - m) % t_count][e]
                if m:
                    block = rotated(block, "tp", m)
                result = result + jnp.dot(
                    block, experts_out[e][m], preferred_element_type=jnp.float32
                )
            share = picked(picked(share_table, (t - k) % t_count, 1), (s - e) % s_count, 2)
            result = result.astype(jnp.bfloat16).astype(jnp.float32)
            total = total + share.reshape(-1, 1) * result
        total = total.astype(jnp.bfloat16).reshape(z_count, part_rows, width)
        final = picked(total, z, 0).astype(jnp.float32)
        for n in range(1, z_count):
            final = final + rotated(picked(total, (z + n) % z_count, 0), "ep", n).astype(jnp.float32)
        own = picked(row_sets[k].reshape(z_count, part_rows, D), z, 0)
        own = lax.dynamic_slice_in_dim(own, t * width, width, 1).astype(jnp.float32)
        own = own * lax.dynamic_slice_in_dim(inverse_gain, t * width, width, 0)
        outputs.append((own + final).astype(jnp.bfloat16))
    order = (t - jnp.arange(t_count, dtype=jnp.int32)) % t_count
    return jnp.take(jnp.stack(outputs), order, axis=0).reshape(row_count, width)


def solution(mesh):
    in_specs = (
        P(("groups", "ep", "sub"), "tp"),
        P(("groups", "ep", "sub"), "tp"),
        P(("groups", "ep", "sub"), "tp"),
        P("tp"),
        P("tp", "ep"),
        P(("groups", "ep", "sub"), None),
        P(),
        P(("ep", "sub"), None, None, "tp"),
        P(("ep", "sub"), None, "tp"),
        P(("groups", "ep", "sub"), None),
        P(("groups", "ep", "sub"), None),
    )
    out_specs = P(("groups", "ep", "sub"), "tp")
    return jax.shard_map(local, mesh=mesh, in_specs=in_specs, out_specs=out_specs, check_vma=False)
```

```python
import jax
import jax.numpy as jnp
from jax import lax
from jax.experimental import pallas as pl
from jax.experimental.pallas import tpu as pltpu
from jax.sharding import PartitionSpec as P

D = 2880
HD = 64
WIN = 128
TOP = 4
PAIR = 2
VMEM_BYTES = 48 * 1024 * 1024


def shifted(block, axis, distance):
    devices = range(lax.axis_size(axis))
    route = [(i - distance, i) for i in devices if i - distance in devices]
    return lax.ppermute(block, axis, route)


def swapped(block, axis, distance):
    return lax.ppermute(block, axis, [(i, i ^ distance) for i in range(lax.axis_size(axis))])


def picked(blocks, index, axis):
    return lax.dynamic_index_in_dim(blocks, index, axis, keepdims=False)


def in_vmem(count):
    return [pl.BlockSpec(memory_space=pltpu.VMEM)] * count


def cost(flops, bytes_accessed):
    return pl.CostEstimate(flops=flops, bytes_accessed=bytes_accessed, transcendentals=0)


def dot(left, right):
    return jnp.dot(left, right, preferred_element_type=jnp.float32)


def attention_kernel(first_ref, sink_ref, q_ref, kp_ref, k_ref, vp_ref, v_ref, out_ref):
    rows = q_ref.shape[0]
    kv_count = k_ref.shape[1] // HD
    pairs = q_ref.shape[1] // (2 * HD * kv_count)
    lane = lax.broadcasted_iota(jnp.int32, (rows, 2 * HD), 1)
    low = lane < HD
    row = lax.broadcasted_iota(jnp.int32, (rows, rows), 0)
    col = lax.broadcasted_iota(jnp.int32, (rows, rows), 1)
    before = col > row
    shut = before & (first_ref[0] == 1)
    zero = jnp.zeros((), jnp.bfloat16)

    def twice(ref, g):
        part = ref[:, g * HD : (g + 1) * HD]
        return jnp.concatenate([part, part], axis=1)

    def scores_of(q, keys):
        return lax.dot_general(q, keys, (((1,), (1,)), ((), ())), preferred_element_type=jnp.float32)

    for g in range(kv_count):
        keys_before, keys_own = twice(kp_ref, g), twice(k_ref, g)
        values_before, values_own = twice(vp_ref, g), twice(v_ref, g)
        for i in range(pairs):
            start = (g * pairs + i) * 2 * HD
            both = q_ref[:, start : start + 2 * HD]
            results = []
            for side in range(2):
                q = jnp.where(low if side == 0 else ~low, both, zero)
                sink = sink_ref[(g * pairs + i) * 2 + side]
                scores = jnp.where(before, scores_of(q, keys_before), scores_of(q, keys_own)) * HD ** (-0.5)
                scores = jnp.where(shut, -1e30, scores)
                largest = jnp.maximum(jnp.max(scores, axis=1, keepdims=True), sink)
                numerator = jnp.exp(scores - largest)
                denominator = jnp.sum(numerator, axis=1, keepdims=True) + jnp.exp(sink - largest)
                weights = (numerator * (1.0 / denominator)).astype(jnp.bfloat16)
                results.append(
                    dot(jnp.where(before, weights, zero), values_before)
                    + dot(jnp.where(before, zero, weights), values_own)
                )
            out_ref[:, start : start + 2 * HD] = jnp.where(low, results[0], results[1]).astype(jnp.bfloat16)


def attention(queries, key_rows, value_rows, sink_logits, first):
    rows, width = queries.shape
    earlier_keys = shifted(key_rows, ("ep", "sub"), 1)
    earlier_values = shifted(value_rows, ("ep", "sub"), 1)
    smem = pl.BlockSpec(memory_space=pltpu.SMEM)
    return pl.pallas_call(
        attention_kernel,
        out_shape=jax.ShapeDtypeStruct((rows, width), jnp.bfloat16),
        in_specs=[smem, smem] + in_vmem(5),
        out_specs=in_vmem(1)[0],
        compiler_params=pltpu.CompilerParams(vmem_limit_bytes=VMEM_BYTES),
        cost_estimate=cost(8 * rows * rows * width, 6 * rows * width),
        name="attention",
    )(first, sink_logits, queries, earlier_keys, key_rows, earlier_values, value_rows)


def project(attended, out_weight, near_weights, t, z, s, t_count):
    slots = len(attended)
    rows, width = attended[0].shape
    columns = out_weight.shape[1]
    half = rows // t_count
    shares = len(near_weights)
    depth = width // shares

    def kernel(place_ref, *refs):
        attended_refs = refs[:slots]
        weight_ref = refs[slots]
        near_refs = refs[slots + 1 : slots + 1 + shares]
        kept_ref, sent_ref, total = refs[slots + 1 + shares :]
        t, member, s = place_ref[0], place_ref[1], place_ref[2]
        for jr in range(slots):
            for i in range(PAIR):
                if i == 0:
                    result = dot(attended_refs[jr][...], weight_ref[...])
                else:
                    result = 0.0
                    for u in range(shares):
                        start = pl.multiple_of((s ^ u) * depth, 128)
                        result = result + dot(attended_refs[jr][:, pl.ds(start, depth)], near_refs[u][...])
                total[...] = result
                for m in range(t_count):
                    block = total[pl.ds(pl.multiple_of((t ^ m) * half, half), half), :]
                    if m == 0:
                        kept_ref[member ^ i, jr] = block
                    else:
                        sent_ref[m - 1, member ^ i, jr] = block.astype(jnp.bfloat16)

    place = jnp.stack([t, z % PAIR, s]).astype(jnp.int32)
    return pl.pallas_call(
        kernel,
        out_shape=(
            jax.ShapeDtypeStruct((PAIR, slots, half, columns), jnp.float32),
            jax.ShapeDtypeStruct((t_count - 1, PAIR, slots, half, columns), jnp.bfloat16),
        ),
        in_specs=[pl.BlockSpec(memory_space=pltpu.SMEM)] + in_vmem(slots + 1 + shares),
        out_specs=tuple(in_vmem(2)),
        scratch_shapes=[pltpu.VMEM((rows, columns), jnp.float32)],
        compiler_params=pltpu.CompilerParams(vmem_limit_bytes=VMEM_BYTES),
        cost_estimate=cost(4 * slots * rows * width * columns, 4 * width * columns),
        name="project",
    )(place, *attended, out_weight, *near_weights)


def activate(pieces, inverse_gain, experts_in, pair):
    t_count, slots = len(pieces), len(pieces[0])
    _, _, half, columns = pieces[0][0].shape
    chunks = slots * PAIR
    row_count = t_count * slots * half
    experts = len(experts_in)
    units = experts_in[0].shape[3]
    tile = min(256, units)
    tiles = -(-units // tile)
    weights = [w.reshape(2, chunks, columns, units) for w in experts_in]

    def kernel(pair_ref, *refs):
        piece_refs = refs[: t_count * slots]
        gain_ref = refs[t_count * slots]
        weight_refs = refs[t_count * slots + 1 : t_count * slots + 1 + experts]
        out_ref, rows_ref, scale_ref = refs[t_count * slots + 1 + experts :]
        e, step = pl.program_id(0), pl.program_id(1)

        @pl.when((e == 0) & (step == 0))
        def _():
            for m in range(t_count):
                for j in range(slots):
                    start = (m * slots + j) * half
                    square = jnp.zeros((half, 1), jnp.float32)
                    for r in range(slots):
                        for i in range(PAIR):
                            chunk = (pair_ref[0] ^ r) * PAIR + i
                            block = piece_refs[m * slots + r][i, j ^ r]
                            rows_ref[chunk, start : start + half, :] = block
                            plain = block.astype(jnp.float32) * gain_ref[chunk]
                            square = square + jnp.sum(plain * plain, axis=1, keepdims=True)
                    scale_ref[start : start + half, :] = lax.rsqrt(square / D + 1e-05)

        for index in range(experts):

            @pl.when(e == index)
            def _():
                gate = jnp.zeros((row_count, tile), jnp.float32)
                up = jnp.zeros((row_count, tile), jnp.float32)
                for c in range(chunks):
                    gate = gate + dot(rows_ref[c], weight_refs[index][0, c])
                    up = up + dot(rows_ref[c], weight_refs[index][1, c])
                gate = gate * scale_ref[...]
                up = up * scale_ref[...]
                out_ref[0] = ((up + 1.0) * gate * jax.nn.sigmoid(1.702 * gate)).astype(jnp.bfloat16)

    def weight_spec(index):
        def place(e, step):
            return (0, 0, 0, jnp.where(e == index, step, jnp.where(e < index, 0, tiles - 1)))

        return pl.BlockSpec((2, chunks, columns, tile), place)

    flat = [piece for part in pieces for piece in part]
    return pl.pallas_call(
        kernel,
        grid=(experts, tiles),
        out_shape=jax.ShapeDtypeStruct((experts, row_count, units), jnp.bfloat16),
        in_specs=[pl.BlockSpec(memory_space=pltpu.SMEM)]
        + in_vmem(len(flat) + 1)
        + [weight_spec(index) for index in range(experts)],
        out_specs=pl.BlockSpec((1, row_count, tile), lambda e, step: (e, 0, step)),
        scratch_shapes=[
            pltpu.VMEM((chunks, row_count, columns), jnp.bfloat16),
            pltpu.VMEM((row_count, 1), jnp.float32),
        ],
        compiler_params=pltpu.CompilerParams(vmem_limit_bytes=VMEM_BYTES),
        cost_estimate=cost(4 * experts * row_count * D * units, 4 * experts * D * units),
        name="activate",
    )(pair.reshape(1), *flat, inverse_gain.reshape(chunks, 1, columns), *weights)


def combine(activated, share, experts_out, t, slots):
    t_count = len(activated)
    experts, row_count, units = activated[0].shape
    width = experts_out[0].shape[2]
    half = row_count // (t_count * slots)
    tile = min(256, width)
    tiles = -(-width // tile)
    weights = [w.reshape(t_count, units, width) for w in experts_out]

    def kernel(t_ref, *refs):
        activated_refs = refs[:t_count]
        share_ref = refs[t_count]
        weight_refs = refs[t_count + 1 : t_count + 1 + experts]
        out_refs = refs[t_count + 1 + experts :]
        t = t_ref[0]
        for m in range(t_count):
            start = m * slots * half
            total = jnp.zeros((slots * half, tile), jnp.float32)
            for e in range(experts):
                result = jnp.zeros((slots * half, tile), jnp.float32)
                for u in range(t_count):
                    first = (m ^ u) * slots * half
                    result = result + dot(
                        activated_refs[u][e, first : first + slots * half, :], weight_refs[e][t ^ u]
                    )
                result = result.astype(jnp.bfloat16).astype(jnp.float32)
                total = total + share_ref[start : start + slots * half, e : e + 1] * result
            for j in range(slots):
                out_refs[j][m] = total[j * half : (j + 1) * half].astype(jnp.bfloat16)

    weight_spec = pl.BlockSpec((t_count, units, tile), lambda step: (0, 0, step))
    return pl.pallas_call(
        kernel,
        grid=(tiles,),
        out_shape=tuple(jax.ShapeDtypeStruct((t_count, half, width), jnp.bfloat16) for _ in range(slots)),
        in_specs=[pl.BlockSpec(memory_space=pltpu.SMEM)] + in_vmem(t_count + 1) + [weight_spec] * experts,
        out_specs=tuple(
            pl.BlockSpec((t_count, half, tile), lambda step: (0, 0, step)) for _ in range(slots)
        ),
        compiler_params=pltpu.CompilerParams(vmem_limit_bytes=VMEM_BYTES),
        cost_estimate=cost(
            2 * experts * row_count * t_count * units * width, 2 * experts * t_count * units * width
        ),
        name="combine",
    )(t.reshape(1), *activated, share, *weights)


def finish(own, returned, t):
    t_count, half, width = own.shape

    def kernel(t_ref, own_ref, *refs):
        *parts, out_ref = refs
        for m in range(t_count):
            total = own_ref[m]
            for part in parts:
                total = total + part[m].astype(jnp.float32)
            start = pl.multiple_of((t_ref[0] ^ m) * half, half)
            out_ref[pl.ds(start, half), :] = total.astype(jnp.bfloat16)

    return pl.pallas_call(
        kernel,
        out_shape=jax.ShapeDtypeStruct((t_count * half, width), jnp.bfloat16),
        in_specs=[pl.BlockSpec(memory_space=pltpu.SMEM)] + in_vmem(1 + len(returned)),
        out_specs=in_vmem(1)[0],
        compiler_params=pltpu.CompilerParams(vmem_limit_bytes=VMEM_BYTES),
        name="finish",
    )(t.reshape(1), own, *returned)


def local(
    queries,
    key_rows,
    value_rows,
    sink_logits,
    out_weight,
    residual,
    norm_gain,
    expert_in,
    expert_out,
    routes,
    route_scores,
):
    row_count = queries.shape[0]
    z_count, t_count, s_count = lax.axis_size("ep"), lax.axis_size("tp"), lax.axis_size("sub")
    z, t, s = lax.axis_index("ep"), lax.axis_index("tp"), lax.axis_index("sub")
    half = row_count // t_count
    columns = out_weight.shape[1]
    width = expert_out.shape[2]
    slots = z_count // PAIR
    pair = (z // PAIR).astype(jnp.int32)

    first = (lax.axis_index(("ep", "sub")) == 0).astype(jnp.int32).reshape(1)
    attended = attention(queries, key_rows, value_rows, sink_logits, first)

    near = picked(out_weight.reshape(s_count, out_weight.shape[0] // s_count, columns), s, 0)
    near = swapped(near, "ep", 1)
    near_weights = [near] + [swapped(near, "sub", u) for u in range(1, s_count)]

    experts_in = [expert_in] + [swapped(expert_in, "sub", e) for e in range(1, s_count)]
    experts_out = [expert_out] + [swapped(expert_out, "sub", e) for e in range(1, s_count)]

    own_residual = picked(residual.reshape(t_count, half, slots, PAIR * columns), t, 0)
    residual_part = [
        picked(own_residual, pair ^ j, 1) if j == 0 else swapped(picked(own_residual, pair ^ j, 1), "ep", PAIR * j)
        for j in range(slots)
    ]
    residual_part = jnp.stack([part.reshape(half, PAIR, columns) for part in residual_part])
    residual_part = residual_part.transpose(2, 0, 1, 3).astype(jnp.float32)

    expert_count = z_count * s_count
    route_float = route_scores.astype(jnp.float32)
    mix_share = route_float / jnp.sum(route_float, axis=1, keepdims=True)
    experts = jnp.arange(expert_count, dtype=jnp.int32)
    named = routes[:, :, None] == experts[None, None, :]
    table = jnp.sum(jnp.where(named, mix_share[:, :, None], 0.0), axis=1)
    tables = jnp.stack([table] + [swapped(table, "ep", d) for d in range(1, z_count)])
    chosen = jnp.stack([z * s_count + (s ^ e) for e in range(s_count)])
    tables = jnp.sum(
        jnp.where(experts[None, None, None, :] == chosen[None, None, :, None], tables[:, :, None, :], 0.0), axis=3
    )
    tables = tables.reshape(slots, PAIR, t_count, half, s_count)
    tables = jnp.take(tables, t ^ jnp.arange(t_count, dtype=jnp.int32), axis=2)

    gathered = [attended] + [swapped(attended, "ep", PAIR * j) for j in range(1, slots)]
    hidden, sent = project(gathered, out_weight, near_weights, t, z, s, t_count)
    hidden = hidden + residual_part
    for m in range(1, t_count):
        hidden = hidden + swapped(sent[m - 1], "tp", m).astype(jnp.float32)
    gain_part = picked(norm_gain.reshape(slots, PAIR, 1, 1, columns), pair, 0)
    scaled = (hidden * gain_part).astype(jnp.bfloat16)

    own = {0: scaled}
    distance = z_count // 2
    while distance:
        own.update({d + distance: swapped(own[d], "ep", distance) for d in list(own)})
        distance //= 2
    pieces = [own] + [{d: swapped(own[d], "tp", m) for d in own} for m in range(1, t_count)]

    inverse_gain = 1.0 / norm_gain
    own_rows = []
    for m in range(t_count):
        rows = jnp.stack([pieces[m][PAIR * r][:, r] for r in range(slots)])
        rows = jnp.take(rows, pair ^ jnp.arange(slots, dtype=jnp.int32), axis=0)
        own_rows.append(rows.reshape(z_count, half, columns).transpose(1, 0, 2).reshape(half, D))
    own_rows = lax.dynamic_slice_in_dim(jnp.stack(own_rows), t * width, width, 2).astype(jnp.float32)
    own_rows = own_rows * lax.dynamic_slice_in_dim(inverse_gain, t * width, width, 0)

    returned = []
    for p in range(PAIR):
        part = [[pieces[m][PAIR * r + p] for r in range(slots)] for m in range(t_count)]
        activated = activate(part, inverse_gain, experts_in, pair)
        activated = [activated] + [swapped(activated, "tp", m) for m in range(1, t_count)]
        share = tables[:, p].transpose(1, 0, 2, 3).reshape(row_count * slots, s_count)
        for j, result in enumerate(combine(activated, share, experts_out, t, slots)):
            distance = PAIR * j + p
            returned.append(swapped(result, "ep", distance) if distance else result)
    return finish(own_rows, returned, t)


def solution(mesh):
    in_specs = (
        P(("groups", "ep", "sub"), "tp"),
        P(("groups", "ep", "sub"), "tp"),
        P(("groups", "ep", "sub"), "tp"),
        P("tp"),
        P("tp", "ep"),
        P(("groups", "ep", "sub"), None),
        P(),
        P(("ep", "sub"), None, None, "tp"),
        P(("ep", "sub"), None, "tp"),
        P(("groups", "ep", "sub"), None),
        P(("groups", "ep", "sub"), None),
    )
    out_specs = P(("groups", "ep", "sub"), "tp")
    return jax.shard_map(local, mesh=mesh, in_specs=in_specs, out_specs=out_specs, check_vma=False)
```

```python
import jax
import jax.numpy as jnp
from jax import lax
from jax.experimental import pallas as pl
from jax.experimental.pallas import tpu as pltpu
from jax.sharding import PartitionSpec as P

D = 2880
HD = 64
WIN = 128
TOP = 4
VMEM_BYTES = 48 * 1024 * 1024


def shifted(block, axis, distance):
    devices = range(lax.axis_size(axis))
    route = [(i - distance, i) for i in devices if i - distance in devices]
    return lax.ppermute(block, axis, route)


def swapped(block, axis, distance):
    return lax.ppermute(block, axis, [(i, i ^ distance) for i in range(lax.axis_size(axis))])


def picked(blocks, index, axis):
    return lax.dynamic_index_in_dim(blocks, index, axis, keepdims=False)


def in_vmem(count):
    return [pl.BlockSpec(memory_space=pltpu.VMEM)] * count


def in_smem():
    return pl.BlockSpec(memory_space=pltpu.SMEM)


def cost(flops, bytes_accessed):
    return pl.CostEstimate(flops=flops, bytes_accessed=bytes_accessed, transcendentals=0)


def dot(left, right):
    return jnp.dot(left, right, preferred_element_type=jnp.float32)


def tile_of(size):
    return size // 3 if size % 48 == 0 else size


def aligned(size):
    return size % 16 == 0


def params():
    return pltpu.CompilerParams(vmem_limit_bytes=VMEM_BYTES)


def attention_kernel(first_ref, sink_ref, q_ref, kp_ref, k_ref, vp_ref, v_ref, out_ref):
    rows = q_ref.shape[0]
    kv_count = k_ref.shape[1] // HD
    pairs = q_ref.shape[1] // (2 * HD * kv_count)
    key = lax.broadcasted_iota(jnp.int32, (rows, rows), 0)
    query = lax.broadcasted_iota(jnp.int32, (rows, rows), 1)
    before = key > query
    shut = before & (first_ref[0] == 1)
    blank = jnp.zeros((2 * rows, HD), jnp.bfloat16)
    values = jnp.concatenate(
        [ref[...].astype(jnp.float32).T.astype(jnp.bfloat16) for ref in (vp_ref, v_ref)], axis=1
    )
    for g in range(kv_count):
        head = slice(g * HD, (g + 1) * HD)
        keys = jnp.concatenate([kp_ref[:, head], k_ref[:, head]], axis=0) * jnp.bfloat16(HD ** (-0.5))
        keys = jnp.concatenate(
            [jnp.concatenate([keys, blank], axis=1), jnp.concatenate([blank, keys], axis=1)], axis=0
        )
        for i in range(pairs):
            start = (g * pairs + i) * 2 * HD
            products = lax.dot_general(
                keys,
                q_ref[:, start : start + 2 * HD],
                (((1,), (1,)), ((), ())),
                preferred_element_type=jnp.float32,
            )
            weights = []
            for side in range(2):
                sink = sink_ref[(g * pairs + i) * 2 + side]
                part = products[side * 2 * rows : (side + 1) * 2 * rows]
                scores = jnp.where(before, part[:rows], part[rows:])
                scores = jnp.where(shut, -1e30, scores)
                largest = jnp.maximum(jnp.max(scores, axis=0, keepdims=True), sink)
                numerator = jnp.exp(scores - largest)
                denominator = jnp.sum(numerator, axis=0, keepdims=True) + jnp.exp(sink - largest)
                numerator = numerator * (1.0 / denominator)
                weights.append(
                    jnp.concatenate(
                        [
                            jnp.where(before, numerator, 0.0).astype(jnp.bfloat16),
                            jnp.where(before, 0.0, numerator).astype(jnp.bfloat16),
                        ],
                        axis=0,
                    )
                )
            result = dot(values[head], jnp.concatenate(weights, axis=1)).astype(jnp.bfloat16)
            out_ref[start : start + HD, :] = result[:, :rows]
            out_ref[start + HD : start + 2 * HD, :] = result[:, rows:]


def attention(queries, key_rows, value_rows, sink_logits, first):
    rows, width = queries.shape
    earlier_keys = shifted(key_rows, ("ep", "sub"), 1)
    earlier_values = shifted(value_rows, ("ep", "sub"), 1)
    return pl.pallas_call(
        attention_kernel,
        out_shape=jax.ShapeDtypeStruct((width, rows), jnp.bfloat16),
        in_specs=[in_smem(), in_smem()] + in_vmem(5),
        out_specs=in_vmem(1)[0],
        compiler_params=params(),
        cost_estimate=cost(8 * rows * rows * width, 6 * rows * width),
        name="attention",
    )(first, sink_logits, queries, earlier_keys, key_rows, earlier_values, value_rows)


def project(attended, out_weight, near_weights, t, member, s, t_count):
    slots = len(attended)
    width, rows = attended[0].shape
    columns = out_weight.shape[0]
    shares = len(near_weights)
    pair = 2
    depth = width // shares

    def kernel(place_ref, *refs):
        attended_refs = refs[:slots]
        weight_ref = refs[slots]
        near_refs = refs[slots + 1 : slots + 1 + shares]
        kept_ref, sent_ref, total = refs[slots + 1 + shares :]
        t, member, s = place_ref[0], place_ref[1], place_ref[2]
        for i in range(pair):
            if i == 0:
                result = dot(weight_ref[...], jnp.concatenate([ref[...] for ref in attended_refs], axis=1))
            else:
                result = 0.0
                for u in range(shares):
                    span = pl.ds(pl.multiple_of((s ^ u) * depth, 128), depth)
                    block = jnp.concatenate([ref[span, :] for ref in attended_refs], axis=1)
                    result = result + dot(near_refs[u][...], block)
            total[...] = result
            for m in range(t_count):
                block = total[:, pl.ds(pl.multiple_of((t ^ m) * rows, 128), rows)]
                if m == 0:
                    kept_ref[member ^ i] = block
                else:
                    sent_ref[m - 1, member ^ i] = block.astype(jnp.bfloat16)

    return pl.pallas_call(
        kernel,
        out_shape=(
            jax.ShapeDtypeStruct((pair, columns, rows), jnp.float32),
            jax.ShapeDtypeStruct((t_count - 1, pair, columns, rows), jnp.bfloat16),
        ),
        in_specs=[in_smem()] + in_vmem(slots + 1 + shares),
        out_specs=tuple(in_vmem(2)),
        scratch_shapes=[pltpu.VMEM((columns, slots * rows), jnp.float32)],
        compiler_params=params(),
        cost_estimate=cost(4 * slots * rows * width * columns, 4 * width * columns),
        name="project",
    )(jnp.stack([t, member, s]).astype(jnp.int32), *attended, out_weight, *near_weights)


def activate(pieces, gain_table, weights, pair, t):
    slots = len(pieces)
    depth, rows = pieces[0][0].shape
    lanes = slots * rows
    experts = len(weights)
    units = weights[0].shape[1]
    tile = tile_of(units)
    tiles = units // tile

    def kernel(place_ref, *refs):
        piece_refs = refs[: slots * slots]
        table_ref = refs[slots * slots]
        weight_refs = refs[slots * slots + 1 : slots * slots + 1 + experts]
        out_ref, rows_ref, scale_ref, stage_ref = refs[slots * slots + 1 + experts :]
        e, step = pl.program_id(0), pl.program_id(1)

        @pl.when((e == 0) & (step == 0))
        def _():
            for m in range(slots):
                for r in range(slots):
                    lane = pl.ds(pl.multiple_of((place_ref[1] ^ r ^ m) * rows, 128), rows)
                    index = place_ref[0] ^ r
                    block = piece_refs[m * slots + r][...]
                    if aligned(depth):
                        rows_ref[pl.ds(pl.multiple_of(index * depth, 16), depth), lane] = block
                    else:
                        stage_ref[index, :, lane] = block
            if not aligned(depth):
                for index in range(slots):
                    rows_ref[index * depth : (index + 1) * depth, :] = stage_ref[index]
            plain = rows_ref[...].astype(jnp.float32)
            square = jnp.sum(dot(table_ref[...], (plain * plain).astype(jnp.bfloat16)), axis=0, keepdims=True)
            scale_ref[...] = lax.rsqrt(square / D + 1e-05)

        for index in range(experts):

            @pl.when(e == index)
            def _():
                gate = dot(weight_refs[index][0], rows_ref[...]) * scale_ref[...]
                up = dot(weight_refs[index][1], rows_ref[...]) * scale_ref[...]
                out_ref[0] = ((up + 1.0) * gate * jax.nn.sigmoid(1.702 * gate)).astype(jnp.bfloat16)

    def weight_spec(index):
        def place(e, step):
            return (0, jnp.where(e == index, step, jnp.where(e < index, 0, tiles - 1)), 0)

        return pl.BlockSpec((2, tile, D), place)

    flat = [piece for part in pieces for piece in part]
    return pl.pallas_call(
        kernel,
        grid=(experts, tiles),
        out_shape=jax.ShapeDtypeStruct((experts, units, lanes), jnp.bfloat16),
        in_specs=[in_smem()] + in_vmem(len(flat) + 1) + [weight_spec(index) for index in range(experts)],
        out_specs=pl.BlockSpec((1, tile, lanes), lambda e, step: (e, step, 0)),
        scratch_shapes=[
            pltpu.VMEM((D, lanes), jnp.bfloat16),
            pltpu.VMEM((1, lanes), jnp.float32),
            pltpu.VMEM((1, 16, 128) if aligned(depth) else (slots, depth, lanes), jnp.bfloat16),
        ],
        compiler_params=params(),
        cost_estimate=cost(4 * experts * lanes * D * units, 4 * experts * D * units),
        name="activate",
    )(jnp.stack([pair, t]).astype(jnp.int32), *flat, gain_table, *weights)


def combine(activated, share, weights, t, slots):
    t_count = len(activated)
    experts, units, lanes = activated[0].shape
    width = weights[0].shape[0]
    rows = lanes // slots
    tile = tile_of(width)
    tiles = width // tile

    def kernel(t_ref, *refs):
        activated_refs = refs[:t_count]
        share_ref = refs[t_count]
        weight_refs = refs[t_count + 1 : t_count + 1 + experts]
        *out_refs, all_ref, stage_ref = refs[t_count + 1 + experts :]

        @pl.when(pl.program_id(0) == 0)
        def _():
            for u in range(t_count):
                index = t_ref[0] ^ u
                if aligned(units):
                    all_ref[:, pl.ds(pl.multiple_of(index * units, 16), units), :] = activated_refs[u][...]
                else:
                    stage_ref[index] = activated_refs[u][...]
            if not aligned(units):
                for index in range(t_count):
                    all_ref[:, index * units : (index + 1) * units, :] = stage_ref[index]

        total = 0.0
        for e in range(experts):
            result = dot(weight_refs[e][...], all_ref[e]).astype(jnp.bfloat16).astype(jnp.float32)
            total = total + share_ref[e : e + 1, :] * result
        for j in range(slots):
            out_refs[j][...] = total[:, j * rows : (j + 1) * rows].astype(jnp.bfloat16)

    return pl.pallas_call(
        kernel,
        grid=(tiles,),
        out_shape=tuple(jax.ShapeDtypeStruct((width, rows), jnp.bfloat16) for _ in range(slots)),
        in_specs=[in_smem()]
        + in_vmem(t_count + 1)
        + [pl.BlockSpec((tile, t_count * units), lambda step: (step, 0))] * experts,
        out_specs=tuple(pl.BlockSpec((tile, rows), lambda step: (step, 0)) for _ in range(slots)),
        scratch_shapes=[
            pltpu.VMEM((experts, t_count * units, lanes), jnp.bfloat16),
            pltpu.VMEM((1, 1, 16, 128) if aligned(units) else (t_count, experts, units, lanes), jnp.bfloat16),
        ],
        compiler_params=params(),
        cost_estimate=cost(
            2 * experts * lanes * t_count * units * width, 2 * experts * t_count * units * width
        ),
        name="combine",
    )(t.reshape(1), *activated, share, *weights)


def local(
    queries,
    key_rows,
    value_rows,
    sink_logits,
    out_weight,
    residual,
    norm_gain,
    expert_in,
    expert_out,
    routes,
    route_scores,
):
    rows = queries.shape[0]
    z_count, t_count, s_count = lax.axis_size("ep"), lax.axis_size("tp"), lax.axis_size("sub")
    z, t, s = (lax.axis_index(name).astype(jnp.int32) for name in ("ep", "tp", "sub"))
    columns = out_weight.shape[1]
    width = expert_out.shape[2]
    slots = t_count
    group = z_count // slots
    pair = z // group

    first = (lax.axis_index(("ep", "sub")) == 0).astype(jnp.int32).reshape(1)
    attended = attention(queries, key_rows, value_rows, sink_logits, first)

    out_weight = out_weight.T
    depth = out_weight.shape[1] // s_count
    near = swapped(lax.dynamic_slice_in_dim(out_weight, s * depth, depth, 1), "ep", 1)
    near, attended = lax.optimization_barrier((near, attended))
    near_weights = [near] + [swapped(near, "sub", u) for u in range(1, s_count)]

    expert_in = expert_in[0].transpose(0, 2, 1)
    expert_out = expert_out[0].T
    experts_in = [expert_in] + [swapped(expert_in, "sub", e) for e in range(1, s_count)]
    experts_out = [expert_out] + [swapped(expert_out, "sub", e) for e in range(1, s_count)]

    residual = residual.T.reshape(slots, group * columns, rows)
    route = [
        (i * t_count + k, (i ^ (group * k)) * t_count + k) for i in range(z_count) for k in range(t_count)
    ]
    residual = lax.ppermute(picked(residual, pair ^ t, 0), ("ep", "tp"), route)

    expert_count = z_count * s_count
    route_float = route_scores.T.astype(jnp.float32)
    mix_share = route_float / jnp.sum(route_float, axis=0, keepdims=True)
    experts = jnp.arange(expert_count, dtype=jnp.int32)
    named = routes.T[:, None, :] == experts[None, :, None]
    table = jnp.sum(jnp.where(named, mix_share[:, None, :], 0.0), axis=0)
    tables = jnp.stack([table] + [swapped(table, "ep", d) for d in range(1, z_count)])
    tables = jnp.take(tables, jnp.stack([z * s_count + (s ^ e) for e in range(s_count)]), axis=1)
    tables = tables.reshape(slots, group, s_count, rows)

    gathered = [attended] + [swapped(attended, "ep", group * j) for j in range(1, slots)]
    hidden, sent = project(gathered, out_weight, near_weights, t, z % group, s, t_count)
    hidden = hidden.reshape(group * columns, rows) + residual.astype(jnp.float32)
    for m in range(1, t_count):
        received = swapped(sent[m - 1].reshape(group * columns, rows), "tp", m)
        hidden = hidden + received.astype(jnp.float32)
    gain_part = picked(norm_gain.reshape(slots, group * columns), pair, 0)
    scaled = (hidden * gain_part[:, None]).astype(jnp.bfloat16)

    own = {0: scaled}
    distance = z_count // 2
    while distance:
        own.update({d + distance: swapped(own[d], "ep", distance) for d in list(own)})
        distance //= 2
    pieces = [own] + [{d: swapped(own[d], "tp", m) for d in own} for m in range(1, t_count)]

    inverse_gain = 1.0 / norm_gain
    inverse_square = inverse_gain * inverse_gain
    coarse = inverse_square.astype(jnp.bfloat16)
    fine = (inverse_square - coarse.astype(jnp.float32)).astype(jnp.bfloat16)
    gain_table = jnp.concatenate([coarse[None], fine[None], jnp.zeros((14, D), jnp.bfloat16)], axis=0)

    total = 0.0
    for m in range(t_count):
        for r in range(slots):
            here = (pair == m) & ((pair ^ t) == r)
            total = total + jnp.where(here, pieces[m][group * r].astype(jnp.float32), 0.0)
    total = total * lax.dynamic_slice_in_dim(inverse_gain, t * width, width, 0)[:, None]

    for p in range(group):
        part = [[pieces[m][group * r + p] for r in range(slots)] for m in range(t_count)]
        activated = activate(part, gain_table, experts_in, pair, t)
        activated = [activated] + [swapped(activated, "tp", m) for m in range(1, t_count)]
        share = tables[:, p].transpose(1, 0, 2).reshape(s_count, slots * rows)
        for j, result in enumerate(combine(activated, share, experts_out, t, slots)):
            distance = group * j + p
            result = swapped(result, "ep", distance) if distance else result
            total = total + result.astype(jnp.float32)
    return total.astype(jnp.bfloat16).T


def solution(mesh):
    in_specs = (
        P(("groups", "ep", "sub"), "tp"),
        P(("groups", "ep", "sub"), "tp"),
        P(("groups", "ep", "sub"), "tp"),
        P("tp"),
        P("tp", "ep"),
        P(("groups", "ep", "sub"), None),
        P(),
        P(("ep", "sub"), None, None, "tp"),
        P(("ep", "sub"), None, "tp"),
        P(("groups", "ep", "sub"), None),
        P(("groups", "ep", "sub"), None),
    )
    out_specs = P(("groups", "ep", "sub"), "tp")
    return jax.shard_map(local, mesh=mesh, in_specs=in_specs, out_specs=out_specs, check_vma=False)
```

```python
import jax
import jax.numpy as jnp
from jax import lax
from jax.experimental import pallas as pl
from jax.experimental.pallas import tpu as pltpu
from jax.sharding import PartitionSpec as P

D = 2880
HD = 64
WIN = 128
TOP = 4
VMEM_BYTES = 16 * 1024 * 1024


def shifted(block, axis, distance):
    devices = range(lax.axis_size(axis))
    route = [(i - distance, i) for i in devices if i - distance in devices]
    return lax.ppermute(block, axis, route)


def swapped(block, axis, distance):
    return lax.ppermute(block, axis, [(i, i ^ distance) for i in range(lax.axis_size(axis))])


def picked(blocks, index, axis):
    return lax.dynamic_index_in_dim(blocks, index, axis, keepdims=False)


def in_vmem(count):
    return [pl.BlockSpec(memory_space=pltpu.VMEM)] * count


def in_smem():
    return pl.BlockSpec(memory_space=pltpu.SMEM)


def cost(flops, bytes_accessed):
    return pl.CostEstimate(flops=flops, bytes_accessed=bytes_accessed, transcendentals=0)


def dot(left, right):
    return jnp.dot(left, right, preferred_element_type=jnp.float32)


def aligned(size):
    return size % 16 == 0


def params():
    return pltpu.CompilerParams(vmem_limit_bytes=VMEM_BYTES)


def attention_kernel(first_ref, sink_ref, q_ref, kp_ref, k_ref, vp_ref, v_ref, out_ref):
    rows = q_ref.shape[0]
    kv_count = k_ref.shape[1] // HD
    pairs = q_ref.shape[1] // (2 * HD * kv_count)
    key = lax.broadcasted_iota(jnp.int32, (rows, rows), 0)
    query = lax.broadcasted_iota(jnp.int32, (rows, rows), 1)
    before = key > query
    shut = before & (first_ref[0] == 1)
    blank = jnp.zeros((2 * rows, HD), jnp.bfloat16)
    values = jnp.concatenate(
        [ref[...].astype(jnp.float32).T.astype(jnp.bfloat16) for ref in (vp_ref, v_ref)], axis=1
    )
    for g in range(kv_count):
        head = slice(g * HD, (g + 1) * HD)
        keys = jnp.concatenate([kp_ref[:, head], k_ref[:, head]], axis=0) * jnp.bfloat16(HD ** (-0.5))
        keys = jnp.concatenate(
            [jnp.concatenate([keys, blank], axis=1), jnp.concatenate([blank, keys], axis=1)], axis=0
        )
        for i in range(pairs):
            start = (g * pairs + i) * 2 * HD
            products = lax.dot_general(
                keys,
                q_ref[:, start : start + 2 * HD],
                (((1,), (1,)), ((), ())),
                preferred_element_type=jnp.float32,
            )
            weights = []
            for side in range(2):
                sink = sink_ref[(g * pairs + i) * 2 + side]
                part = products[side * 2 * rows : (side + 1) * 2 * rows]
                scores = jnp.where(before, part[:rows], part[rows:])
                scores = jnp.where(shut, -1e30, scores)
                largest = jnp.maximum(jnp.max(scores, axis=0, keepdims=True), sink)
                numerator = jnp.exp(scores - largest)
                denominator = jnp.sum(numerator, axis=0, keepdims=True) + jnp.exp(sink - largest)
                numerator = numerator * (1.0 / denominator)
                weights.append(
                    jnp.concatenate(
                        [
                            jnp.where(before, numerator, 0.0).astype(jnp.bfloat16),
                            jnp.where(before, 0.0, numerator).astype(jnp.bfloat16),
                        ],
                        axis=0,
                    )
                )
            result = dot(values[head], jnp.concatenate(weights, axis=1)).astype(jnp.bfloat16)
            out_ref[start : start + HD, :] = result[:, :rows]
            out_ref[start + HD : start + 2 * HD, :] = result[:, rows:]


def attention(queries, earlier_keys, key_rows, earlier_values, value_rows, sink_logits, first):
    rows, width = queries.shape
    return pl.pallas_call(
        attention_kernel,
        out_shape=jax.ShapeDtypeStruct((width, rows), jnp.bfloat16),
        in_specs=[in_smem(), in_smem()] + in_vmem(5),
        out_specs=in_vmem(1)[0],
        compiler_params=params(),
        cost_estimate=cost(8 * rows * rows * width, 6 * rows * width),
        name="attention",
    )(first, sink_logits, queries, earlier_keys, key_rows, earlier_values, value_rows)


def project(attended, out_weight, near_weights, t, member, s, t_count):
    slots = len(attended)
    width, rows = attended[0].shape
    columns = out_weight.shape[0]
    shares = len(near_weights)
    pair = 2
    depth = width // shares

    def kernel(place_ref, *refs):
        attended_refs = refs[:slots]
        weight_ref = refs[slots]
        near_refs = refs[slots + 1 : slots + 1 + shares]
        kept_ref, sent_ref, total = refs[slots + 1 + shares :]
        t, member, s = place_ref[0], place_ref[1], place_ref[2]
        for i in range(pair):
            if i == 0:
                result = dot(weight_ref[...], jnp.concatenate([ref[...] for ref in attended_refs], axis=1))
            else:
                result = 0.0
                for u in range(shares):
                    span = pl.ds(pl.multiple_of((s ^ u) * depth, 128), depth)
                    block = jnp.concatenate([ref[span, :] for ref in attended_refs], axis=1)
                    result = result + dot(near_refs[u][...], block)
            total[...] = result
            for m in range(t_count):
                block = total[:, pl.ds(pl.multiple_of((t ^ m) * rows, 128), rows)]
                if m == 0:
                    kept_ref[member ^ i] = block
                else:
                    sent_ref[m - 1, member ^ i] = block.astype(jnp.bfloat16)

    return pl.pallas_call(
        kernel,
        out_shape=(
            jax.ShapeDtypeStruct((pair, columns, rows), jnp.float32),
            jax.ShapeDtypeStruct((t_count - 1, pair, columns, rows), jnp.bfloat16),
        ),
        in_specs=[in_smem()] + in_vmem(slots + 1 + shares),
        out_specs=tuple(in_vmem(2)),
        scratch_shapes=[pltpu.VMEM((columns, slots * rows), jnp.float32)],
        compiler_params=params(),
        cost_estimate=cost(4 * slots * rows * width * columns, 4 * width * columns),
        name="project",
    )(jnp.stack([t, member, s]).astype(jnp.int32), *attended, out_weight, *near_weights)


def activate(pieces, gain_table, weights, pair, t):
    slots = len(pieces)
    depth, rows = pieces[0][0].shape
    lanes = slots * rows
    experts = len(weights)
    units = weights[0].shape[1]

    def kernel(place_ref, *refs):
        piece_refs = refs[: slots * slots]
        table_ref = refs[slots * slots]
        weight_refs = refs[slots * slots + 1 : slots * slots + 1 + experts]
        out_ref, rows_ref, stage_ref = refs[slots * slots + 1 + experts :]
        for m in range(slots):
            for r in range(slots):
                lane = pl.ds(pl.multiple_of((place_ref[1] ^ r ^ m) * rows, 128), rows)
                index = place_ref[0] ^ r
                block = piece_refs[m * slots + r][...]
                if aligned(depth):
                    rows_ref[pl.ds(pl.multiple_of(index * depth, 16), depth), lane] = block
                else:
                    stage_ref[index, :, lane] = block
        if not aligned(depth):
            for index in range(slots):
                rows_ref[index * depth : (index + 1) * depth, :] = stage_ref[index]
        plain = rows_ref[...].astype(jnp.float32)
        square = jnp.sum(dot(table_ref[...], (plain * plain).astype(jnp.bfloat16)), axis=0, keepdims=True)
        scale = lax.rsqrt(square / D + 1e-05)
        for e in range(experts):
            gate = dot(weight_refs[e][0], rows_ref[...]) * scale
            up = dot(weight_refs[e][1], rows_ref[...]) * scale
            out_ref[e] = ((up + 1.0) * gate * jax.nn.sigmoid(1.702 * gate)).astype(jnp.bfloat16)

    flat = [piece for part in pieces for piece in part]
    return pl.pallas_call(
        kernel,
        out_shape=jax.ShapeDtypeStruct((experts, units, lanes), jnp.bfloat16),
        in_specs=[in_smem()] + in_vmem(len(flat) + 1 + experts),
        out_specs=in_vmem(1)[0],
        scratch_shapes=[
            pltpu.VMEM((D, lanes), jnp.bfloat16),
            pltpu.VMEM((1, 16, 128) if aligned(depth) else (slots, depth, lanes), jnp.bfloat16),
        ],
        compiler_params=params(),
        cost_estimate=cost(4 * experts * lanes * D * units, 4 * experts * D * units),
        name="activate",
    )(jnp.stack([pair, t]).astype(jnp.int32), *flat, gain_table, *weights)


def combine(activated, share, weights, t, slots):
    t_count = len(activated)
    experts, units, lanes = activated[0].shape
    width = weights[0].shape[0]
    rows = lanes // slots

    def kernel(t_ref, *refs):
        activated_refs = refs[:t_count]
        share_ref = refs[t_count]
        weight_refs = refs[t_count + 1 : t_count + 1 + experts]
        *out_refs, all_ref, stage_ref = refs[t_count + 1 + experts :]
        for u in range(t_count):
            index = t_ref[0] ^ u
            if aligned(units):
                all_ref[:, pl.ds(pl.multiple_of(index * units, 16), units), :] = activated_refs[u][...]
            else:
                stage_ref[index] = activated_refs[u][...]
        if not aligned(units):
            for index in range(t_count):
                all_ref[:, index * units : (index + 1) * units, :] = stage_ref[index]
        total = 0.0
        for e in range(experts):
            result = dot(weight_refs[e][...], all_ref[e]).astype(jnp.bfloat16).astype(jnp.float32)
            total = total + share_ref[e : e + 1, :] * result
        for j in range(slots):
            out_refs[j][...] = total[:, j * rows : (j + 1) * rows].astype(jnp.bfloat16)

    return pl.pallas_call(
        kernel,
        out_shape=tuple(jax.ShapeDtypeStruct((width, rows), jnp.bfloat16) for _ in range(slots)),
        in_specs=[in_smem()] + in_vmem(t_count + 1 + experts),
        out_specs=tuple(in_vmem(slots)),
        scratch_shapes=[
            pltpu.VMEM((experts, t_count * units, lanes), jnp.bfloat16),
            pltpu.VMEM((1, 1, 16, 128) if aligned(units) else (t_count, experts, units, lanes), jnp.bfloat16),
        ],
        compiler_params=params(),
        cost_estimate=cost(
            2 * experts * lanes * t_count * units * width, 2 * experts * t_count * units * width
        ),
        name="combine",
    )(t.reshape(1), *activated, share, *weights)


def local(
    queries,
    key_rows,
    value_rows,
    sink_logits,
    out_weight,
    residual,
    norm_gain,
    expert_in,
    expert_out,
    routes,
    route_scores,
):
    rows = queries.shape[0]
    z_count, t_count, s_count = lax.axis_size("ep"), lax.axis_size("tp"), lax.axis_size("sub")
    z, t, s = (lax.axis_index(name).astype(jnp.int32) for name in ("ep", "tp", "sub"))
    columns = out_weight.shape[1]
    width = expert_out.shape[2]
    slots = t_count
    group = z_count // slots
    pair = z // group

    first = (lax.axis_index(("ep", "sub")) == 0).astype(jnp.int32).reshape(1)
    earlier_keys = shifted(key_rows, ("ep", "sub"), 1)
    earlier_values = shifted(value_rows, ("ep", "sub"), 1)
    attended = attention(
        queries, earlier_keys, key_rows, earlier_values, value_rows, sink_logits, first
    )

    out_weight = out_weight.T
    depth = out_weight.shape[1] // s_count
    near, _ = lax.optimization_barrier((out_weight, earlier_values))
    near = swapped(lax.dynamic_slice_in_dim(near, s * depth, depth, 1), "ep", 1)
    near, _ = lax.optimization_barrier((near, attended))
    near_weights = [near] + [swapped(near, "sub", u) for u in range(1, s_count)]

    expert_in = expert_in[0].transpose(0, 2, 1)
    expert_out = expert_out[0].T
    experts_in = [expert_in] + [swapped(expert_in, "sub", e) for e in range(1, s_count)]
    experts_out = [expert_out] + [swapped(expert_out, "sub", e) for e in range(1, s_count)]

    residual = residual.T.reshape(slots, group * columns, rows)
    route = [
        (i * t_count + k, (i ^ (group * k)) * t_count + k) for i in range(z_count) for k in range(t_count)
    ]
    residual = lax.ppermute(picked(residual, pair ^ t, 0), ("ep", "tp"), route)

    expert_count = z_count * s_count
    route_float = route_scores.T.astype(jnp.float32)
    mix_share = route_float / jnp.sum(route_float, axis=0, keepdims=True)
    experts = jnp.arange(expert_count, dtype=jnp.int32)
    named = routes.T[:, None, :] == experts[None, :, None]
    table = jnp.sum(jnp.where(named, mix_share[:, None, :], 0.0), axis=0)
    tables = jnp.stack([table] + [swapped(table, "ep", d) for d in range(1, z_count)])
    tables = jnp.take(tables, jnp.stack([z * s_count + (s ^ e) for e in range(s_count)]), axis=1)
    tables = tables.reshape(slots, group, s_count, rows)

    gathered = [attended] + [swapped(attended, "ep", group * j) for j in range(1, slots)]
    hidden, sent = project(gathered, out_weight, near_weights, t, z % group, s, t_count)
    hidden = hidden.reshape(group * columns, rows) + residual.astype(jnp.float32)
    for m in range(1, t_count):
        received = swapped(sent[m - 1].reshape(group * columns, rows), "tp", m)
        hidden = hidden + received.astype(jnp.float32)
    gain_part = picked(norm_gain.reshape(slots, group * columns), pair, 0)
    scaled = (hidden * gain_part[:, None]).astype(jnp.bfloat16)

    own = {0: scaled}
    distance = z_count // 2
    while distance:
        own.update({d + distance: swapped(own[d], "ep", distance) for d in list(own)})
        distance //= 2
    pieces = [own] + [{d: swapped(own[d], "tp", m) for d in own} for m in range(1, t_count)]

    inverse_gain = 1.0 / norm_gain
    inverse_square = inverse_gain * inverse_gain
    coarse = inverse_square.astype(jnp.bfloat16)
    fine = (inverse_square - coarse.astype(jnp.float32)).astype(jnp.bfloat16)
    gain_table = jnp.concatenate([coarse[None], fine[None], jnp.zeros((14, D), jnp.bfloat16)], axis=0)

    total = 0.0
    for m in range(t_count):
        for r in range(slots):
            here = (pair == m) & ((pair ^ t) == r)
            total = total + jnp.where(here, pieces[m][group * r].astype(jnp.float32), 0.0)
    total = total * lax.dynamic_slice_in_dim(inverse_gain, t * width, width, 0)[:, None]

    for p in range(group):
        part = [[pieces[m][group * r + p] for r in range(slots)] for m in range(t_count)]
        activated = activate(part, gain_table, experts_in, pair, t)
        activated = [activated] + [swapped(activated, "tp", m) for m in range(1, t_count)]
        share = tables[:, p].transpose(1, 0, 2).reshape(s_count, slots * rows)
        for j, result in enumerate(combine(activated, share, experts_out, t, slots)):
            distance = group * j + p
            result = swapped(result, "ep", distance) if distance else result
            total = total + result.astype(jnp.float32)
    return total.astype(jnp.bfloat16).T


def solution(mesh):
    in_specs = (
        P(("groups", "ep", "sub"), "tp"),
        P(("groups", "ep", "sub"), "tp"),
        P(("groups", "ep", "sub"), "tp"),
        P("tp"),
        P("tp", "ep"),
        P(("groups", "ep", "sub"), None),
        P(),
        P(("ep", "sub"), None, None, "tp"),
        P(("ep", "sub"), None, "tp"),
        P(("groups", "ep", "sub"), None),
        P(("groups", "ep", "sub"), None),
    )
    out_specs = P(("groups", "ep", "sub"), "tp")
    return jax.shard_map(local, mesh=mesh, in_specs=in_specs, out_specs=out_specs, check_vma=False)
```

```python
import jax
import jax.numpy as jnp
from jax import lax
from jax.experimental import pallas as pl
from jax.experimental.pallas import tpu as pltpu
from jax.sharding import PartitionSpec as P

D = 2880
HD = 64
WIN = 128
TOP = 4
VMEM_BYTES = 16 * 1024 * 1024


def shifted(block, axis, distance):
    devices = range(lax.axis_size(axis))
    route = [(i - distance, i) for i in devices if i - distance in devices]
    return lax.ppermute(block, axis, route)


def swapped(block, axis, distance):
    return lax.ppermute(block, axis, [(i, i ^ distance) for i in range(lax.axis_size(axis))])


def picked(blocks, index, axis):
    return lax.dynamic_index_in_dim(blocks, index, axis, keepdims=False)


def in_vmem(count):
    return [pl.BlockSpec(memory_space=pltpu.VMEM)] * count


def in_smem():
    return pl.BlockSpec(memory_space=pltpu.SMEM)


def cost(flops, bytes_accessed):
    return pl.CostEstimate(flops=flops, bytes_accessed=bytes_accessed, transcendentals=0)


def dot(left, right):
    return jnp.dot(left, right, preferred_element_type=jnp.float32)


def aligned(size):
    return size % 16 == 0


def params():
    return pltpu.CompilerParams(vmem_limit_bytes=VMEM_BYTES)


def attention_kernel(first_ref, sink_ref, q_ref, earlier_ref, k_ref, v_ref, out_ref):
    rows = q_ref.shape[0]
    kv_count = k_ref.shape[1] // HD
    pairs = q_ref.shape[1] // (2 * HD * kv_count)
    key = lax.broadcasted_iota(jnp.int32, (rows, rows), 0)
    query = lax.broadcasted_iota(jnp.int32, (rows, rows), 1)
    before = key > query
    shut = before & (first_ref[0] == 1)
    blank = jnp.zeros((2 * rows, HD), jnp.bfloat16)
    values = jnp.concatenate(
        [
            block.astype(jnp.float32).T.astype(jnp.bfloat16)
            for block in (earlier_ref[:, kv_count * HD :], v_ref[...])
        ],
        axis=1,
    )
    for g in range(kv_count):
        head = slice(g * HD, (g + 1) * HD)
        keys = jnp.concatenate([earlier_ref[:, head], k_ref[:, head]], axis=0) * jnp.bfloat16(HD ** (-0.5))
        keys = jnp.concatenate(
            [jnp.concatenate([keys, blank], axis=1), jnp.concatenate([blank, keys], axis=1)], axis=0
        )
        for i in range(pairs):
            start = (g * pairs + i) * 2 * HD
            products = lax.dot_general(
                keys,
                q_ref[:, start : start + 2 * HD],
                (((1,), (1,)), ((), ())),
                preferred_element_type=jnp.float32,
            )
            weights = []
            for side in range(2):
                sink = sink_ref[(g * pairs + i) * 2 + side]
                part = products[side * 2 * rows : (side + 1) * 2 * rows]
                scores = jnp.where(before, part[:rows], part[rows:])
                scores = jnp.where(shut, -1e30, scores)
                largest = jnp.maximum(jnp.max(scores, axis=0, keepdims=True), sink)
                numerator = jnp.exp(scores - largest)
                denominator = jnp.sum(numerator, axis=0, keepdims=True) + jnp.exp(sink - largest)
                numerator = numerator * (1.0 / denominator)
                weights.append(
                    jnp.concatenate(
                        [
                            jnp.where(before, numerator, 0.0).astype(jnp.bfloat16),
                            jnp.where(before, 0.0, numerator).astype(jnp.bfloat16),
                        ],
                        axis=0,
                    )
                )
            result = dot(values[head], jnp.concatenate(weights, axis=1)).astype(jnp.bfloat16)
            out_ref[start : start + HD, :] = result[:, :rows]
            out_ref[start + HD : start + 2 * HD, :] = result[:, rows:]


def attention(queries, earlier, key_rows, value_rows, sink_logits, first):
    rows, width = queries.shape
    return pl.pallas_call(
        attention_kernel,
        out_shape=jax.ShapeDtypeStruct((width, rows), jnp.bfloat16),
        in_specs=[in_smem(), in_smem()] + in_vmem(4),
        out_specs=in_vmem(1)[0],
        compiler_params=params(),
        cost_estimate=cost(8 * rows * rows * width, 6 * rows * width),
        name="attention",
    )(first, sink_logits, queries, earlier, key_rows, value_rows)


def project(attended, weights, t, s, t_count):
    slots = len(attended)
    width, rows = attended[0].shape
    columns = weights[0].shape[0]
    shares = len(weights)
    depth = width // shares

    def kernel(place_ref, *refs):
        attended_refs = refs[:slots]
        weight_refs = refs[slots : slots + shares]
        kept_ref, sent_ref, total = refs[slots + shares :]
        t, s = place_ref[0], place_ref[1]
        result = 0.0
        for u in range(shares):
            span = pl.ds(pl.multiple_of((s ^ u) * depth, 128), depth)
            block = jnp.concatenate([ref[span, :] for ref in attended_refs], axis=1)
            result = result + dot(weight_refs[u][...], block)
        total[...] = result
        for m in range(t_count):
            block = total[:, pl.ds(pl.multiple_of((t ^ m) * rows, 128), rows)]
            if m == 0:
                kept_ref[...] = block
            else:
                sent_ref[m - 1] = block.astype(jnp.bfloat16)

    return pl.pallas_call(
        kernel,
        out_shape=(
            jax.ShapeDtypeStruct((columns, rows), jnp.float32),
            jax.ShapeDtypeStruct((t_count - 1, columns, rows), jnp.bfloat16),
        ),
        in_specs=[in_smem()] + in_vmem(slots + shares),
        out_specs=tuple(in_vmem(2)),
        scratch_shapes=[pltpu.VMEM((columns, slots * rows), jnp.float32)],
        compiler_params=params(),
        cost_estimate=cost(2 * slots * rows * width * columns, 2 * width * columns),
        name="project",
    )(jnp.stack([t, s]).astype(jnp.int32), *attended, *weights)


def activate(pieces, gain_table, weights, pair, t):
    slots = len(pieces)
    depth, rows = pieces[0][0].shape
    lanes = slots * rows
    experts = len(weights)
    units = weights[0].shape[1]

    def kernel(place_ref, *refs):
        piece_refs = refs[: slots * slots]
        table_ref = refs[slots * slots]
        weight_refs = refs[slots * slots + 1 : slots * slots + 1 + experts]
        out_ref, rows_ref, stage_ref = refs[slots * slots + 1 + experts :]
        for m in range(slots):
            for r in range(slots):
                lane = pl.ds(pl.multiple_of((place_ref[1] ^ r ^ m) * rows, 128), rows)
                index = place_ref[0] ^ r
                block = piece_refs[m * slots + r][...]
                if aligned(depth):
                    rows_ref[pl.ds(pl.multiple_of(index * depth, 16), depth), lane] = block
                else:
                    stage_ref[index, :, lane] = block
        if not aligned(depth):
            for index in range(slots):
                rows_ref[index * depth : (index + 1) * depth, :] = stage_ref[index]
        plain = rows_ref[...].astype(jnp.float32)
        square = jnp.sum(dot(table_ref[...], (plain * plain).astype(jnp.bfloat16)), axis=0, keepdims=True)
        scale = lax.rsqrt(square / D + 1e-05)
        for e in range(experts):
            gate = dot(weight_refs[e][0], rows_ref[...]) * scale
            up = dot(weight_refs[e][1], rows_ref[...]) * scale
            out_ref[e] = ((up + 1.0) * gate * jax.nn.sigmoid(1.702 * gate)).astype(jnp.bfloat16)

    flat = [piece for part in pieces for piece in part]
    return pl.pallas_call(
        kernel,
        out_shape=jax.ShapeDtypeStruct((experts, units, lanes), jnp.bfloat16),
        in_specs=[in_smem()] + in_vmem(len(flat) + 1 + experts),
        out_specs=in_vmem(1)[0],
        scratch_shapes=[
            pltpu.VMEM((D, lanes), jnp.bfloat16),
            pltpu.VMEM((1, 16, 128) if aligned(depth) else (slots, depth, lanes), jnp.bfloat16),
        ],
        compiler_params=params(),
        cost_estimate=cost(4 * experts * lanes * D * units, 4 * experts * D * units),
        name="activate",
    )(jnp.stack([pair, t]).astype(jnp.int32), *flat, gain_table, *weights)


def combine(activated, share, weights, t, slots):
    t_count = len(activated)
    experts, units, lanes = activated[0].shape
    width = weights[0].shape[0]
    rows = lanes // slots

    def kernel(t_ref, *refs):
        activated_refs = refs[:t_count]
        share_ref = refs[t_count]
        weight_refs = refs[t_count + 1 : t_count + 1 + experts]
        *out_refs, all_ref, stage_ref = refs[t_count + 1 + experts :]
        for u in range(t_count):
            index = t_ref[0] ^ u
            if aligned(units):
                all_ref[:, pl.ds(pl.multiple_of(index * units, 16), units), :] = activated_refs[u][...]
            else:
                stage_ref[index] = activated_refs[u][...]
        if not aligned(units):
            for index in range(t_count):
                all_ref[:, index * units : (index + 1) * units, :] = stage_ref[index]
        total = 0.0
        for e in range(experts):
            result = dot(weight_refs[e][...], all_ref[e]).astype(jnp.bfloat16).astype(jnp.float32)
            total = total + share_ref[e : e + 1, :] * result
        for j in range(slots):
            out_refs[j][...] = total[:, j * rows : (j + 1) * rows].astype(jnp.bfloat16)

    return pl.pallas_call(
        kernel,
        out_shape=tuple(jax.ShapeDtypeStruct((width, rows), jnp.bfloat16) for _ in range(slots)),
        in_specs=[in_smem()] + in_vmem(t_count + 1 + experts),
        out_specs=tuple(in_vmem(slots)),
        scratch_shapes=[
            pltpu.VMEM((experts, t_count * units, lanes), jnp.bfloat16),
            pltpu.VMEM((1, 1, 16, 128) if aligned(units) else (t_count, experts, units, lanes), jnp.bfloat16),
        ],
        compiler_params=params(),
        cost_estimate=cost(
            2 * experts * lanes * t_count * units * width, 2 * experts * t_count * units * width
        ),
        name="combine",
    )(t.reshape(1), *activated, share, *weights)


def local(
    queries,
    key_rows,
    value_rows,
    sink_logits,
    out_weight,
    residual,
    norm_gain,
    expert_in,
    expert_out,
    routes,
    route_scores,
):
    rows = queries.shape[0]
    z_count, t_count, s_count = lax.axis_size("ep"), lax.axis_size("tp"), lax.axis_size("sub")
    z, t, s = (lax.axis_index(name).astype(jnp.int32) for name in ("ep", "tp", "sub"))
    columns = out_weight.shape[1]
    width = expert_out.shape[2]
    slots = t_count
    group = z_count // slots
    pair = z // group

    paired = jnp.concatenate([key_rows, value_rows], axis=1)
    earlier = shifted(paired, ("ep", "sub"), 1)
    out_weight = out_weight.T
    depth = out_weight.shape[1] // s_count
    near = lax.dynamic_slice_in_dim(out_weight, s * depth, depth, 1)
    residual = picked(residual.T.reshape(slots, group * columns, rows), pair ^ t, 0)
    earlier, near, residual, expert_in, expert_out = lax.optimization_barrier(
        (earlier, near, residual, expert_in, expert_out)
    )

    near = swapped(near, "ep", 1)

    route = [
        (i * t_count + k, (i ^ (group * k)) * t_count + k) for i in range(z_count) for k in range(t_count)
    ]
    residual = lax.ppermute(residual, ("ep", "tp"), route)

    expert_in = expert_in[0].transpose(0, 2, 1)
    expert_out = expert_out[0]
    experts_in = [expert_in] + [swapped(expert_in, "sub", e) for e in range(1, s_count)]
    experts_out = [expert_out.T] + [swapped(expert_out, "sub", e).T for e in range(1, s_count)]

    first = (lax.axis_index(("ep", "sub")) == 0).astype(jnp.int32).reshape(1)
    attended = attention(queries, earlier, key_rows, value_rows, sink_logits, first)

    expert_count = z_count * s_count
    route_float = route_scores.T.astype(jnp.float32)
    mix_share = route_float / jnp.sum(route_float, axis=0, keepdims=True)
    experts = jnp.arange(expert_count, dtype=jnp.int32)
    named = routes.T[:, None, :] == experts[None, :, None]
    table = jnp.sum(jnp.where(named, mix_share[:, None, :], 0.0), axis=0)
    tables = jnp.stack([table] + [swapped(table, "ep", d) for d in range(1, z_count)])
    tables = jnp.take(tables, jnp.stack([z * s_count + (s ^ e) for e in range(s_count)]), axis=1)
    tables = tables.reshape(slots, group, s_count, rows)

    gathered = [attended] + [swapped(attended, "ep", group * j) for j in range(1, slots)]
    near, *gathered = lax.optimization_barrier((near, *gathered))
    near_weights = [near] + [swapped(near, "sub", u) for u in range(1, s_count)]
    mine = project(gathered, [out_weight], t, s * 0, t_count)
    other = project(gathered, near_weights, t, s, t_count)
    first_member = z % group == 0

    def ordered(a, b):
        return jnp.concatenate([jnp.where(first_member, a, b), jnp.where(first_member, b, a)], axis=0)

    hidden = ordered(mine[0], other[0]) + residual.astype(jnp.float32)
    for m in range(1, t_count):
        received = swapped(ordered(mine[1][m - 1], other[1][m - 1]), "tp", m)
        hidden = hidden + received.astype(jnp.float32)
    gain_part = picked(norm_gain.reshape(slots, group * columns), pair, 0)
    scaled = (hidden * gain_part[:, None]).astype(jnp.bfloat16)

    own = {0: scaled}
    distance = z_count // 2
    while distance:
        own.update({d + distance: swapped(own[d], "ep", distance) for d in list(own)})
        distance //= 2
    pieces = [own] + [{d: swapped(own[d], "tp", m) for d in own} for m in range(1, t_count)]

    inverse_gain = 1.0 / norm_gain
    inverse_square = inverse_gain * inverse_gain
    coarse = inverse_square.astype(jnp.bfloat16)
    fine = (inverse_square - coarse.astype(jnp.float32)).astype(jnp.bfloat16)
    gain_table = jnp.concatenate([coarse[None], fine[None], jnp.zeros((14, D), jnp.bfloat16)], axis=0)

    total = 0.0
    for m in range(t_count):
        for r in range(slots):
            here = (pair == m) & ((pair ^ t) == r)
            total = total + jnp.where(here, pieces[m][group * r].astype(jnp.float32), 0.0)
    total = total * lax.dynamic_slice_in_dim(inverse_gain, t * width, width, 0)[:, None]
    total = lax.optimization_barrier(total)

    for p in range(group):
        part = [[pieces[m][group * r + p] for r in range(slots)] for m in range(t_count)]
        activated = activate(part, gain_table, experts_in, pair, t)
        activated = [activated] + [swapped(activated, "tp", m) for m in range(1, t_count)]
        share = tables[:, p].transpose(1, 0, 2).reshape(s_count, slots * rows)
        for j, result in enumerate(combine(activated, share, experts_out, t, slots)):
            distance = group * j + p
            result = swapped(result, "ep", distance) if distance else result
            total = total + result.astype(jnp.float32)
    return total.astype(jnp.bfloat16).T


def solution(mesh):
    in_specs = (
        P(("groups", "ep", "sub"), "tp"),
        P(("groups", "ep", "sub"), "tp"),
        P(("groups", "ep", "sub"), "tp"),
        P("tp"),
        P("tp", "ep"),
        P(("groups", "ep", "sub"), None),
        P(),
        P(("ep", "sub"), None, None, "tp"),
        P(("ep", "sub"), None, "tp"),
        P(("groups", "ep", "sub"), None),
        P(("groups", "ep", "sub"), None),
    )
    out_specs = P(("groups", "ep", "sub"), "tp")
    return jax.shard_map(local, mesh=mesh, in_specs=in_specs, out_specs=out_specs, check_vma=False)
```

```python
import jax
import jax.numpy as jnp
from jax import lax
from jax.experimental import pallas as pl
from jax.experimental.pallas import tpu as pltpu
from jax.sharding import PartitionSpec as P

D = 2880
HD = 64
WIN = 128
TOP = 4
VMEM_BYTES = 16 * 1024 * 1024
FETCH_BYTES = 32 * 1024 * 1024


def shifted(block, axis, distance):
    devices = range(lax.axis_size(axis))
    route = [(i - distance, i) for i in devices if i - distance in devices]
    return lax.ppermute(block, axis, route)


def swapped(block, axis, distance):
    return lax.ppermute(block, axis, [(i, i ^ distance) for i in range(lax.axis_size(axis))])


def picked(blocks, index, axis):
    return lax.dynamic_index_in_dim(blocks, index, axis, keepdims=False)


def in_vmem(count):
    return [pl.BlockSpec(memory_space=pltpu.VMEM)] * count


def in_smem():
    return pl.BlockSpec(memory_space=pltpu.SMEM)


def cost(flops, bytes_accessed):
    return pl.CostEstimate(flops=flops, bytes_accessed=bytes_accessed, transcendentals=0)


def dot(left, right):
    return jnp.dot(left, right, preferred_element_type=jnp.float32)


def aligned(size):
    return size % 16 == 0


def params(limit=VMEM_BYTES):
    return pltpu.CompilerParams(vmem_limit_bytes=limit)


def fetches(sources, held, arrived):
    return [
        pltpu.make_async_copy(source, held.at[index], arrived.at[index]) for index, source in enumerate(sources)
    ]


def attention_kernel(first_ref, sink_ref, q_ref, earlier_ref, k_ref, v_ref, out_ref):
    rows = q_ref.shape[0]
    kv_count = k_ref.shape[1] // HD
    pairs = q_ref.shape[1] // (2 * HD * kv_count)
    key = lax.broadcasted_iota(jnp.int32, (rows, rows), 0)
    query = lax.broadcasted_iota(jnp.int32, (rows, rows), 1)
    before = key > query
    shut = before & (first_ref[0] == 1)
    blank = jnp.zeros((2 * rows, HD), jnp.bfloat16)
    values = jnp.concatenate(
        [
            block.astype(jnp.float32).T.astype(jnp.bfloat16)
            for block in (earlier_ref[:, kv_count * HD :], v_ref[...])
        ],
        axis=1,
    )
    for g in range(kv_count):
        head = slice(g * HD, (g + 1) * HD)
        keys = jnp.concatenate([earlier_ref[:, head], k_ref[:, head]], axis=0) * jnp.bfloat16(HD ** (-0.5))
        keys = jnp.concatenate(
            [jnp.concatenate([keys, blank], axis=1), jnp.concatenate([blank, keys], axis=1)], axis=0
        )
        for i in range(pairs):
            start = (g * pairs + i) * 2 * HD
            products = lax.dot_general(
                keys,
                q_ref[:, start : start + 2 * HD],
                (((1,), (1,)), ((), ())),
                preferred_element_type=jnp.float32,
            )
            weights = []
            for side in range(2):
                sink = sink_ref[(g * pairs + i) * 2 + side]
                part = products[side * 2 * rows : (side + 1) * 2 * rows]
                scores = jnp.where(before, part[:rows], part[rows:])
                scores = jnp.where(shut, -1e30, scores)
                largest = jnp.maximum(jnp.max(scores, axis=0, keepdims=True), sink)
                numerator = jnp.exp(scores - largest)
                denominator = jnp.sum(numerator, axis=0, keepdims=True) + jnp.exp(sink - largest)
                numerator = numerator * (1.0 / denominator)
                weights.append(
                    jnp.concatenate(
                        [
                            jnp.where(before, numerator, 0.0).astype(jnp.bfloat16),
                            jnp.where(before, 0.0, numerator).astype(jnp.bfloat16),
                        ],
                        axis=0,
                    )
                )
            result = dot(values[head], jnp.concatenate(weights, axis=1)).astype(jnp.bfloat16)
            out_ref[start : start + HD, :] = result[:, :rows]
            out_ref[start + HD : start + 2 * HD, :] = result[:, rows:]


def attention(queries, earlier, key_rows, value_rows, sink_logits, first):
    rows, width = queries.shape
    return pl.pallas_call(
        attention_kernel,
        out_shape=jax.ShapeDtypeStruct((width, rows), jnp.bfloat16),
        in_specs=[in_smem(), in_smem()] + in_vmem(4),
        out_specs=in_vmem(1)[0],
        compiler_params=params(),
        cost_estimate=cost(8 * rows * rows * width, 6 * rows * width),
        name="attention",
    )(first, sink_logits, queries, earlier, key_rows, value_rows)


def project(attended, weights, t, s, t_count):
    slots = len(attended)
    width, rows = attended[0].shape
    columns = weights[0].shape[0]
    shares = len(weights)
    depth = width // shares

    def kernel(place_ref, *refs):
        attended_refs = refs[:slots]
        weight_refs = refs[slots : slots + shares]
        kept_ref, sent_ref, total = refs[slots + shares :]
        t, s = place_ref[0], place_ref[1]
        result = 0.0
        for u in range(shares):
            span = pl.ds(pl.multiple_of((s ^ u) * depth, 128), depth)
            block = jnp.concatenate([ref[span, :] for ref in attended_refs], axis=1)
            result = result + dot(weight_refs[u][...], block)
        total[...] = result
        for m in range(t_count):
            block = total[:, pl.ds(pl.multiple_of((t ^ m) * rows, 128), rows)]
            if m == 0:
                kept_ref[...] = block
            else:
                sent_ref[m - 1] = block.astype(jnp.bfloat16)

    return pl.pallas_call(
        kernel,
        out_shape=(
            jax.ShapeDtypeStruct((columns, rows), jnp.float32),
            jax.ShapeDtypeStruct((t_count - 1, columns, rows), jnp.bfloat16),
        ),
        in_specs=[in_smem()] + in_vmem(slots + shares),
        out_specs=tuple(in_vmem(2)),
        scratch_shapes=[pltpu.VMEM((columns, slots * rows), jnp.float32)],
        compiler_params=params(),
        cost_estimate=cost(2 * slots * rows * width * columns, 2 * width * columns),
        name="project",
    )(jnp.stack([t, s]).astype(jnp.int32), *attended, *weights)


def activate(pieces, gain_table, weights, pair, t):
    slots = len(pieces)
    depth, rows = pieces[0][0].shape
    lanes = slots * rows
    experts = len(weights)
    units = weights[0].shape[1]

    def kernel(place_ref, *refs):
        piece_refs = refs[: slots * slots]
        table_ref = refs[slots * slots]
        weight_refs = refs[slots * slots + 1 : slots * slots + 1 + experts]
        out_ref, rows_ref, stage_ref, held_ref, arrived = refs[slots * slots + 1 + experts :]
        copies = fetches([ref.at[k] for ref in weight_refs for k in range(2)], held_ref, arrived)
        for copy in copies:
            copy.start()
        for m in range(slots):
            for r in range(slots):
                lane = pl.ds(pl.multiple_of((place_ref[1] ^ r ^ m) * rows, 128), rows)
                index = place_ref[0] ^ r
                block = piece_refs[m * slots + r][...]
                if aligned(depth):
                    rows_ref[pl.ds(pl.multiple_of(index * depth, 16), depth), lane] = block
                else:
                    stage_ref[index, :, lane] = block
        if not aligned(depth):
            for index in range(slots):
                rows_ref[index * depth : (index + 1) * depth, :] = stage_ref[index]
        plain = rows_ref[...].astype(jnp.float32)
        square = jnp.sum(dot(table_ref[...], (plain * plain).astype(jnp.bfloat16)), axis=0, keepdims=True)
        scale = lax.rsqrt(square / D + 1e-05)
        for e in range(experts):
            copies[2 * e].wait()
            gate = dot(held_ref[2 * e], rows_ref[...]) * scale
            copies[2 * e + 1].wait()
            up = dot(held_ref[2 * e + 1], rows_ref[...]) * scale
            out_ref[e] = ((up + 1.0) * gate * jax.nn.sigmoid(1.702 * gate)).astype(jnp.bfloat16)

    flat = [piece for part in pieces for piece in part]
    return pl.pallas_call(
        kernel,
        out_shape=jax.ShapeDtypeStruct((experts, units, lanes), jnp.bfloat16),
        in_specs=[in_smem()] + in_vmem(len(flat) + 1) + [pl.BlockSpec(memory_space=pl.ANY)] * experts,
        out_specs=in_vmem(1)[0],
        scratch_shapes=[
            pltpu.VMEM((D, lanes), jnp.bfloat16),
            pltpu.VMEM((1, 16, 128) if aligned(depth) else (slots, depth, lanes), jnp.bfloat16),
            pltpu.VMEM((2 * experts, units, D), jnp.bfloat16),
            pltpu.SemaphoreType.DMA((2 * experts,)),
        ],
        compiler_params=params(FETCH_BYTES),
        cost_estimate=cost(4 * experts * lanes * D * units, 4 * experts * D * units),
        name="activate",
    )(jnp.stack([pair, t]).astype(jnp.int32), *flat, gain_table, *weights)


def combine(activated, share, weights, t, slots):
    t_count = len(activated)
    experts, units, lanes = activated[0].shape
    width = weights[0].shape[0]
    rows = lanes // slots

    def kernel(t_ref, *refs):
        activated_refs = refs[:t_count]
        share_ref = refs[t_count]
        weight_refs = refs[t_count + 1 : t_count + 1 + experts]
        *out_refs, all_ref, stage_ref, held_ref, arrived = refs[t_count + 1 + experts :]
        copies = fetches(weight_refs, held_ref, arrived)
        for copy in copies:
            copy.start()
        for u in range(t_count):
            index = t_ref[0] ^ u
            if aligned(units):
                all_ref[:, pl.ds(pl.multiple_of(index * units, 16), units), :] = activated_refs[u][...]
            else:
                stage_ref[index] = activated_refs[u][...]
        if not aligned(units):
            for index in range(t_count):
                all_ref[:, index * units : (index + 1) * units, :] = stage_ref[index]
        total = 0.0
        for e in range(experts):
            copies[e].wait()
            result = dot(held_ref[e], all_ref[e]).astype(jnp.bfloat16).astype(jnp.float32)
            total = total + share_ref[e : e + 1, :] * result
        for j in range(slots):
            out_refs[j][...] = total[:, j * rows : (j + 1) * rows].astype(jnp.bfloat16)

    return pl.pallas_call(
        kernel,
        out_shape=tuple(jax.ShapeDtypeStruct((width, rows), jnp.bfloat16) for _ in range(slots)),
        in_specs=[in_smem()] + in_vmem(t_count + 1) + [pl.BlockSpec(memory_space=pl.ANY)] * experts,
        out_specs=tuple(in_vmem(slots)),
        scratch_shapes=[
            pltpu.VMEM((experts, t_count * units, lanes), jnp.bfloat16),
            pltpu.VMEM((1, 1, 16, 128) if aligned(units) else (t_count, experts, units, lanes), jnp.bfloat16),
            pltpu.VMEM((experts, width, t_count * units), jnp.bfloat16),
            pltpu.SemaphoreType.DMA((experts,)),
        ],
        compiler_params=params(FETCH_BYTES),
        cost_estimate=cost(
            2 * experts * lanes * t_count * units * width, 2 * experts * t_count * units * width
        ),
        name="combine",
    )(t.reshape(1), *activated, share, *weights)


def local(
    queries,
    key_rows,
    value_rows,
    sink_logits,
    out_weight,
    residual,
    norm_gain,
    expert_in,
    expert_out,
    routes,
    route_scores,
):
    rows = queries.shape[0]
    z_count, t_count, s_count = lax.axis_size("ep"), lax.axis_size("tp"), lax.axis_size("sub")
    z, t, s = (lax.axis_index(name).astype(jnp.int32) for name in ("ep", "tp", "sub"))
    columns = out_weight.shape[1]
    width = expert_out.shape[2]
    slots = t_count
    group = z_count // slots
    pair = z // group

    paired = jnp.concatenate([key_rows, value_rows], axis=1)
    earlier = shifted(paired, ("ep", "sub"), 1)
    out_weight = out_weight.T
    g_count = lax.axis_size("groups")
    share = s * g_count + lax.axis_index("groups").astype(jnp.int32)
    depth = out_weight.shape[1] // (s_count * g_count)
    near = lax.dynamic_slice_in_dim(out_weight, share * depth, depth, 1)
    residual = picked(residual.T.reshape(slots, group * columns, rows), pair ^ t, 0)
    earlier, near, residual, expert_in, expert_out = lax.optimization_barrier(
        (earlier, near, residual, expert_in, expert_out)
    )

    near = swapped(near, "ep", 1)
    near_weights = [near] + [swapped(near, "groups", g) for g in range(1, g_count)]

    route = [
        (i * t_count + k, (i ^ (group * k)) * t_count + k) for i in range(z_count) for k in range(t_count)
    ]
    residual = lax.ppermute(residual, ("ep", "tp"), route)

    expert_in = expert_in[0].transpose(0, 2, 1)
    expert_out = expert_out[0]
    experts_in = [expert_in] + [swapped(expert_in, "sub", e) for e in range(1, s_count)]
    experts_out = [expert_out.T] + [swapped(expert_out, "sub", e).T for e in range(1, s_count)]

    first = (lax.axis_index(("ep", "sub")) == 0).astype(jnp.int32).reshape(1)
    attended = attention(queries, earlier, key_rows, value_rows, sink_logits, first)

    expert_count = z_count * s_count
    route_float = route_scores.T.astype(jnp.float32)
    mix_share = route_float / jnp.sum(route_float, axis=0, keepdims=True)
    experts = jnp.arange(expert_count, dtype=jnp.int32)
    named = routes.T[:, None, :] == experts[None, :, None]
    table = jnp.sum(jnp.where(named, mix_share[:, None, :], 0.0), axis=0)
    tables = jnp.stack([table] + [swapped(table, "ep", d) for d in range(1, z_count)])
    tables = jnp.take(tables, jnp.stack([z * s_count + (s ^ e) for e in range(s_count)]), axis=1)
    tables = tables.reshape(slots, group, s_count, rows)

    gathered = [attended] + [swapped(attended, "ep", group * j) for j in range(1, slots)]
    near_weights = near_weights + [
        swapped(part, "sub", u) for u in range(1, s_count) for part in near_weights
    ]
    gathered, residual, tables, experts_out = lax.optimization_barrier((gathered, residual, tables, experts_out))
    mine = project(gathered, [out_weight], t, s * 0, t_count)
    other = project(gathered, near_weights, t, share, t_count)
    first_member = z % group == 0

    def ordered(a, b):
        return jnp.concatenate([jnp.where(first_member, a, b), jnp.where(first_member, b, a)], axis=0)

    hidden = ordered(mine[0], other[0]) + residual.astype(jnp.float32)
    for m in range(1, t_count):
        received = swapped(ordered(mine[1][m - 1], other[1][m - 1]), "tp", m)
        hidden = hidden + received.astype(jnp.float32)
    gain_part = picked(norm_gain.reshape(slots, group * columns), pair, 0)
    scaled = (hidden * gain_part[:, None]).astype(jnp.bfloat16)

    own = {0: scaled}
    pieces = [own] + [{} for m in range(1, t_count)]
    distance = z_count // 2
    while distance:
        held = list(own)
        if distance >= group:
            for m in range(1, t_count):
                pieces[m].update({d: swapped(own[d], "tp", m) for d in held if d not in pieces[m]})
        for d in held:
            own[d + distance] = swapped(own[d], "ep", distance)
        distance //= 2
    for m in range(1, t_count):
        pieces[m].update({d: swapped(own[d], "tp", m) for d in range(0, z_count, group) if d not in pieces[m]})
    late = {d: own[d] for d in own if d % group}
    late, pieces[1:] = lax.optimization_barrier((late, pieces[1:]))
    for m in range(1, t_count):
        pieces[m].update({d: swapped(late[d], "tp", m) for d in late})

    inverse_gain = 1.0 / norm_gain
    inverse_square = inverse_gain * inverse_gain
    coarse = inverse_square.astype(jnp.bfloat16)
    fine = (inverse_square - coarse.astype(jnp.float32)).astype(jnp.bfloat16)
    gain_table = jnp.concatenate([coarse[None], fine[None], jnp.zeros((14, D), jnp.bfloat16)], axis=0)

    total = 0.0
    for m in range(t_count):
        for r in range(slots):
            here = (pair == m) & ((pair ^ t) == r)
            total = total + jnp.where(here, pieces[m][group * r].astype(jnp.float32), 0.0)
    total = total * lax.dynamic_slice_in_dim(inverse_gain, t * width, width, 0)[:, None]
    total = lax.optimization_barrier(total)

    after = None
    for p in range(group):
        part = [[pieces[m][group * r + p] for r in range(slots)] for m in range(t_count)]
        if p:
            part, after = lax.optimization_barrier((part, after))
        activated = activate(part, gain_table, experts_in, pair, t)
        after = activated
        activated = [activated] + [swapped(activated, "tp", m) for m in range(1, t_count)]
        share = tables[:, p].transpose(1, 0, 2).reshape(s_count, slots * rows)
        for j, result in enumerate(combine(activated, share, experts_out, t, slots)):
            distance = group * j + p
            result = swapped(result, "ep", distance) if distance else result
            total = total + result.astype(jnp.float32)
    return total.astype(jnp.bfloat16).T


def solution(mesh):
    in_specs = (
        P(("groups", "ep", "sub"), "tp"),
        P(("groups", "ep", "sub"), "tp"),
        P(("groups", "ep", "sub"), "tp"),
        P("tp"),
        P("tp", "ep"),
        P(("groups", "ep", "sub"), None),
        P(),
        P(("ep", "sub"), None, None, "tp"),
        P(("ep", "sub"), None, "tp"),
        P(("groups", "ep", "sub"), None),
        P(("groups", "ep", "sub"), None),
    )
    out_specs = P(("groups", "ep", "sub"), "tp")
    return jax.shard_map(local, mesh=mesh, in_specs=in_specs, out_specs=out_specs, check_vma=False)
```

```python
import functools

import jax
import jax.numpy as jnp
from jax import lax
from jax.experimental import pallas as pl
from jax.experimental.pallas import tpu as pltpu
from jax.sharding import PartitionSpec as P

D = 2880
HD = 64
WIN = 128
TOP = 4
VMEM_BYTES = 16 * 1024 * 1024
FETCH_BYTES = 32 * 1024 * 1024


def shifted(block, axis, distance):
    devices = range(lax.axis_size(axis))
    route = [(i - distance, i) for i in devices if i - distance in devices]
    return lax.ppermute(block, axis, route)


def swapped(block, axis, distance):
    return lax.ppermute(block, axis, [(i, i ^ distance) for i in range(lax.axis_size(axis))])


def picked(blocks, index, axis):
    return lax.dynamic_index_in_dim(blocks, index, axis, keepdims=False)


def in_vmem(count):
    return [pl.BlockSpec(memory_space=pltpu.VMEM)] * count


def in_smem():
    return pl.BlockSpec(memory_space=pltpu.SMEM)


def cost(flops, bytes_accessed):
    return pl.CostEstimate(flops=flops, bytes_accessed=bytes_accessed, transcendentals=0)


def dot(left, right):
    return jnp.dot(left, right, preferred_element_type=jnp.float32)


def aligned(size):
    return size % 16 == 0


def params(limit=VMEM_BYTES):
    return pltpu.CompilerParams(vmem_limit_bytes=limit)


class Fetches:
    def __init__(self, pairs, arrived, flying=3):
        self.copies = [
            pltpu.make_async_copy(source, target, arrived.at[index])
            for index, (source, target) in enumerate(pairs)
        ]
        self.flying = flying
        self.taken = 0
        for copy in self.copies[:flying]:
            copy.start()

    def take(self):
        self.copies[self.taken].wait()
        if self.taken + self.flying < len(self.copies):
            self.copies[self.taken + self.flying].start()
        self.taken += 1


def cuts_of(size, count):
    count = count if size % (16 * count) == 0 else 1
    return [slice(i * (size // count), (i + 1) * (size // count)) for i in range(count)]


def attention_kernel(part, parts, first_ref, sink_ref, q_ref, earlier_ref, k_ref, v_ref, out_ref):
    rows = q_ref.shape[0]
    kv_count = k_ref.shape[1] // HD
    pairs = q_ref.shape[1] // (2 * HD * kv_count)
    key = lax.broadcasted_iota(jnp.int32, (rows, rows), 0)
    query = lax.broadcasted_iota(jnp.int32, (rows, rows), 1)
    before = key > query
    shut = before & (first_ref[0] == 1)
    blank = jnp.zeros((2 * rows, HD), jnp.bfloat16)
    values = jnp.concatenate(
        [
            block.astype(jnp.float32).T.astype(jnp.bfloat16)
            for block in (earlier_ref[:, kv_count * HD :], v_ref[...])
        ],
        axis=1,
    )
    span = kv_count * pairs // parts
    chosen = range(part * span, (part + 1) * span)
    for g in range(kv_count):
        head = slice(g * HD, (g + 1) * HD)
        if not any(index // pairs == g for index in chosen):
            continue
        keys = jnp.concatenate([earlier_ref[:, head], k_ref[:, head]], axis=0) * jnp.bfloat16(HD ** (-0.5))
        keys = jnp.concatenate(
            [jnp.concatenate([keys, blank], axis=1), jnp.concatenate([blank, keys], axis=1)], axis=0
        )
        for index in chosen:
            if index // pairs != g:
                continue
            start = index * 2 * HD
            products = lax.dot_general(
                keys,
                q_ref[:, start : start + 2 * HD],
                (((1,), (1,)), ((), ())),
                preferred_element_type=jnp.float32,
            )
            weights = []
            for side in range(2):
                sink = sink_ref[index * 2 + side]
                product = products[side * 2 * rows : (side + 1) * 2 * rows]
                scores = jnp.where(before, product[:rows], product[rows:])
                scores = jnp.where(shut, -1e30, scores)
                largest = jnp.maximum(jnp.max(scores, axis=0, keepdims=True), sink)
                numerator = jnp.exp(scores - largest)
                denominator = jnp.sum(numerator, axis=0, keepdims=True) + jnp.exp(sink - largest)
                numerator = numerator * (1.0 / denominator)
                weights.append(
                    jnp.concatenate(
                        [
                            jnp.where(before, numerator, 0.0).astype(jnp.bfloat16),
                            jnp.where(before, 0.0, numerator).astype(jnp.bfloat16),
                        ],
                        axis=0,
                    )
                )
            result = dot(values[head], jnp.concatenate(weights, axis=1)).astype(jnp.bfloat16)
            start = start - part * span * 2 * HD
            out_ref[start : start + HD, :] = result[:, :rows]
            out_ref[start + HD : start + 2 * HD, :] = result[:, rows:]


def attention(queries, earlier, key_rows, value_rows, sink_logits, first, part, parts):
    rows, width = queries.shape
    return pl.pallas_call(
        functools.partial(attention_kernel, part, parts),
        out_shape=jax.ShapeDtypeStruct((width // parts, rows), jnp.bfloat16),
        in_specs=[in_smem(), in_smem()] + in_vmem(4),
        out_specs=in_vmem(1)[0],
        compiler_params=params(),
        cost_estimate=cost(8 * rows * rows * width // parts, 6 * rows * width // parts),
        name="attention",
    )(first, sink_logits, queries, earlier, key_rows, value_rows)


def project(attended, weights, t, s, t_count):
    slots, parts = len(attended), len(attended[0])
    part_width, rows = attended[0][0].shape
    width = parts * part_width
    columns = weights[0].shape[0]
    shares = len(weights)
    depth = width // shares

    def kernel(place_ref, *refs):
        attended_refs = refs[: slots * parts]
        weight_refs = refs[slots * parts : slots * parts + shares]
        kept_ref, sent_ref, all_ref, total = refs[slots * parts + shares :]
        t, s = place_ref[0], place_ref[1]
        for j in range(slots):
            for i in range(parts):
                span = slice(i * part_width, (i + 1) * part_width)
                all_ref[span, j * rows : (j + 1) * rows] = attended_refs[j * parts + i][...]
        result = 0.0
        for u in range(shares):
            span = pl.ds(pl.multiple_of((s ^ u) * depth, 128), depth)
            result = result + dot(weight_refs[u][...], all_ref[span, :])
        total[...] = result
        for m in range(t_count):
            block = total[:, pl.ds(pl.multiple_of((t ^ m) * rows, 128), rows)]
            if m == 0:
                kept_ref[...] = block
            else:
                sent_ref[m - 1] = block.astype(jnp.bfloat16)

    flat = [part for block in attended for part in block]
    return pl.pallas_call(
        kernel,
        out_shape=(
            jax.ShapeDtypeStruct((columns, rows), jnp.float32),
            jax.ShapeDtypeStruct((t_count - 1, columns, rows), jnp.bfloat16),
        ),
        in_specs=[in_smem()] + in_vmem(len(flat) + shares),
        out_specs=tuple(in_vmem(2)),
        scratch_shapes=[
            pltpu.VMEM((width, slots * rows), jnp.bfloat16),
            pltpu.VMEM((columns, slots * rows), jnp.float32),
        ],
        compiler_params=params(),
        cost_estimate=cost(2 * slots * rows * width * columns, 2 * width * columns),
        name="project",
    )(jnp.stack([t, s]).astype(jnp.int32), *flat, *weights)


def activate(pieces, gain_table, weights, pair, t):
    slots = len(pieces)
    depth, rows = pieces[0][0].shape
    lanes = slots * rows
    experts = len(weights)
    units = weights[0].shape[1]
    cuts = cuts_of(units, 3)

    def kernel(place_ref, *refs):
        piece_refs = refs[: slots * slots]
        table_ref = refs[slots * slots]
        weight_refs = refs[slots * slots + 1 : slots * slots + 1 + experts]
        out_ref, rows_ref, stage_ref, held_ref, arrived = refs[slots * slots + 1 + experts :]
        fetched = Fetches(
            [
                (weight_refs[e].at[k, cut], held_ref.at[2 * e + k, cut])
                for e in range(experts)
                for cut in cuts
                for k in range(2)
            ],
            arrived,
        )
        for m in range(slots):
            for r in range(slots):
                lane = pl.ds(pl.multiple_of((place_ref[1] ^ r ^ m) * rows, 128), rows)
                index = place_ref[0] ^ r
                block = piece_refs[m * slots + r][...]
                if aligned(depth):
                    rows_ref[pl.ds(pl.multiple_of(index * depth, 16), depth), lane] = block
                else:
                    stage_ref[index, :, lane] = block
        if not aligned(depth):
            for index in range(slots):
                rows_ref[index * depth : (index + 1) * depth, :] = stage_ref[index]
        plain = rows_ref[...].astype(jnp.float32)
        square = jnp.sum(dot(table_ref[...], (plain * plain).astype(jnp.bfloat16)), axis=0, keepdims=True)
        scale = lax.rsqrt(square / D + 1e-05)
        for e in range(experts):
            for cut in cuts:
                fetched.take()
                gate = dot(held_ref[2 * e, cut], rows_ref[...]) * scale
                fetched.take()
                up = dot(held_ref[2 * e + 1, cut], rows_ref[...]) * scale
                out_ref[e, cut] = ((up + 1.0) * gate * jax.nn.sigmoid(1.702 * gate)).astype(jnp.bfloat16)

    flat = [piece for part in pieces for piece in part]
    return pl.pallas_call(
        kernel,
        out_shape=jax.ShapeDtypeStruct((experts, units, lanes), jnp.bfloat16),
        in_specs=[in_smem()] + in_vmem(len(flat) + 1) + [pl.BlockSpec(memory_space=pl.ANY)] * experts,
        out_specs=in_vmem(1)[0],
        scratch_shapes=[
            pltpu.VMEM((D, lanes), jnp.bfloat16),
            pltpu.VMEM((1, 16, 128) if aligned(depth) else (slots, depth, lanes), jnp.bfloat16),
            pltpu.VMEM((2 * experts, units, D), jnp.bfloat16),
            pltpu.SemaphoreType.DMA((2 * experts * len(cuts),)),
        ],
        compiler_params=params(FETCH_BYTES),
        cost_estimate=cost(4 * experts * lanes * D * units, 4 * experts * D * units),
        name="activate",
    )(jnp.stack([pair, t]).astype(jnp.int32), *flat, gain_table, *weights)


def combine(activated, share, weights, t, slots):
    t_count = len(activated)
    experts, units, lanes = activated[0].shape
    width = weights[0].shape[0]
    rows = lanes // slots
    cuts = cuts_of(width, 3)

    def kernel(t_ref, *refs):
        activated_refs = refs[:t_count]
        share_ref = refs[t_count]
        weight_refs = refs[t_count + 1 : t_count + 1 + experts]
        *out_refs, all_ref, stage_ref, held_ref, arrived = refs[t_count + 1 + experts :]
        fetched = Fetches(
            [(weight_refs[e].at[cut], held_ref.at[e, cut]) for cut in cuts for e in range(experts)], arrived
        )
        for u in range(t_count):
            index = t_ref[0] ^ u
            if aligned(units):
                all_ref[:, pl.ds(pl.multiple_of(index * units, 16), units), :] = activated_refs[u][...]
            else:
                stage_ref[index] = activated_refs[u][...]
        if not aligned(units):
            for index in range(t_count):
                all_ref[:, index * units : (index + 1) * units, :] = stage_ref[index]
        for cut in cuts:
            total = 0.0
            for e in range(experts):
                fetched.take()
                result = dot(held_ref[e, cut], all_ref[e]).astype(jnp.bfloat16).astype(jnp.float32)
                total = total + share_ref[e : e + 1, :] * result
            for j in range(slots):
                out_refs[j][cut] = total[:, j * rows : (j + 1) * rows].astype(jnp.bfloat16)

    return pl.pallas_call(
        kernel,
        out_shape=tuple(jax.ShapeDtypeStruct((width, rows), jnp.bfloat16) for _ in range(slots)),
        in_specs=[in_smem()] + in_vmem(t_count + 1) + [pl.BlockSpec(memory_space=pl.ANY)] * experts,
        out_specs=tuple(in_vmem(slots)),
        scratch_shapes=[
            pltpu.VMEM((experts, t_count * units, lanes), jnp.bfloat16),
            pltpu.VMEM((1, 1, 16, 128) if aligned(units) else (t_count, experts, units, lanes), jnp.bfloat16),
            pltpu.VMEM((experts, width, t_count * units), jnp.bfloat16),
            pltpu.SemaphoreType.DMA((experts * len(cuts),)),
        ],
        compiler_params=params(FETCH_BYTES),
        cost_estimate=cost(
            2 * experts * lanes * t_count * units * width, 2 * experts * t_count * units * width
        ),
        name="combine",
    )(t.reshape(1), *activated, share, *weights)


def local(
    queries,
    key_rows,
    value_rows,
    sink_logits,
    out_weight,
    residual,
    norm_gain,
    expert_in,
    expert_out,
    routes,
    route_scores,
):
    rows = queries.shape[0]
    z_count, t_count, s_count = lax.axis_size("ep"), lax.axis_size("tp"), lax.axis_size("sub")
    z, t, s = (lax.axis_index(name).astype(jnp.int32) for name in ("ep", "tp", "sub"))
    columns = out_weight.shape[1]
    width = expert_out.shape[2]
    slots = t_count
    group = z_count // slots
    pair = z // group

    paired = jnp.concatenate([key_rows, value_rows], axis=1)
    earlier = shifted(paired, ("ep", "sub"), 1)
    out_weight = out_weight.T
    depth = out_weight.shape[1] // s_count
    near = lax.dynamic_slice_in_dim(out_weight, s * depth, depth, 1)
    residual = picked(residual.T.reshape(slots, group * columns, rows), pair ^ t, 0)
    earlier, near, residual, expert_in = lax.optimization_barrier((earlier, near, residual, expert_in))

    near = swapped(near, "ep", 1)

    route = [
        (i * t_count + k, (i ^ (group * k)) * t_count + k) for i in range(z_count) for k in range(t_count)
    ]
    residual = lax.ppermute(residual, ("ep", "tp"), route)

    expert_in = expert_in[0].transpose(0, 2, 1)
    experts_in = [expert_in] + [swapped(expert_in, "sub", e) for e in range(1, s_count)]

    first = (lax.axis_index(("ep", "sub")) == 0).astype(jnp.int32).reshape(1)
    gathered = [[] for _ in range(slots)]
    for part in range(2):
        attended = attention(queries, earlier, key_rows, value_rows, sink_logits, first, part, 2)
        for j in range(slots):
            gathered[j].append(swapped(attended, "ep", group * j) if j else attended)
        if not part:
            queries, _ = lax.optimization_barrier((queries, attended))

    arrived = [block[0] for block in gathered]
    arrived, near, expert_out, routes, route_scores = lax.optimization_barrier(
        (arrived, near, expert_out, routes, route_scores)
    )
    gathered = [[arrived[j], gathered[j][1]] for j in range(slots)]
    near_weights = [near] + [swapped(near, "sub", u) for u in range(1, s_count)]
    expert_out = expert_out[0].T
    experts_out = [expert_out] + [swapped(expert_out, "sub", e) for e in range(1, s_count)]

    expert_count = z_count * s_count
    route_float = route_scores.T.astype(jnp.float32)
    mix_share = route_float / jnp.sum(route_float, axis=0, keepdims=True)
    experts = jnp.arange(expert_count, dtype=jnp.int32)
    named = routes.T[:, None, :] == experts[None, :, None]
    table = jnp.sum(jnp.where(named, mix_share[:, None, :], 0.0), axis=0)
    tables = jnp.stack([table] + [swapped(table, "ep", d) for d in range(1, z_count)])
    tables = jnp.take(tables, jnp.stack([z * s_count + (s ^ e) for e in range(s_count)]), axis=1)
    tables = tables.reshape(slots, group, s_count, rows)

    gathered, residual, tables, expert_out = lax.optimization_barrier((gathered, residual, tables, expert_out))
    experts_out[0] = expert_out
    mine = project(gathered, [out_weight], t, s * 0, t_count)
    other = project(gathered, near_weights, t, s, t_count)
    first_member = z % group == 0

    def ordered(a, b):
        return jnp.concatenate([jnp.where(first_member, a, b), jnp.where(first_member, b, a)], axis=0)

    hidden = ordered(mine[0], other[0]) + residual.astype(jnp.float32)
    for m in range(1, t_count):
        received = swapped(ordered(mine[1][m - 1], other[1][m - 1]), "tp", m)
        hidden = hidden + received.astype(jnp.float32)
    gain_part = picked(norm_gain.reshape(slots, group * columns), pair, 0)
    scaled = (hidden * gain_part[:, None]).astype(jnp.bfloat16)

    own = {0: scaled}
    pieces = [own] + [{} for m in range(1, t_count)]
    distance = z_count // 2
    while distance:
        held = list(own)
        if distance >= group:
            for m in range(1, t_count):
                pieces[m].update({d: swapped(own[d], "tp", m) for d in held if d not in pieces[m]})
        for d in held:
            own[d + distance] = swapped(own[d], "ep", distance)
        distance //= 2
    for m in range(1, t_count):
        pieces[m].update({d: swapped(own[d], "tp", m) for d in range(0, z_count, group) if d not in pieces[m]})
    late = {d: own[d] for d in own if d % group}
    late, pieces[1:] = lax.optimization_barrier((late, pieces[1:]))
    for m in range(1, t_count):
        pieces[m].update({d: swapped(late[d], "tp", m) for d in late})

    inverse_gain = 1.0 / norm_gain
    inverse_square = inverse_gain * inverse_gain
    coarse = inverse_square.astype(jnp.bfloat16)
    fine = (inverse_square - coarse.astype(jnp.float32)).astype(jnp.bfloat16)
    gain_table = jnp.concatenate([coarse[None], fine[None], jnp.zeros((14, D), jnp.bfloat16)], axis=0)

    total = 0.0
    for m in range(t_count):
        for r in range(slots):
            here = (pair == m) & ((pair ^ t) == r)
            total = total + jnp.where(here, pieces[m][group * r].astype(jnp.float32), 0.0)
    total = total * lax.dynamic_slice_in_dim(inverse_gain, t * width, width, 0)[:, None]
    total = lax.optimization_barrier(total)

    after = None
    for p in range(group):
        part = [[pieces[m][group * r + p] for r in range(slots)] for m in range(t_count)]
        if p:
            part, after = lax.optimization_barrier((part, after))
        activated = activate(part, gain_table, experts_in, pair, t)
        after = activated
        activated = [activated] + [swapped(activated, "tp", m) for m in range(1, t_count)]
        share = tables[:, p].transpose(1, 0, 2).reshape(s_count, slots * rows)
        for j, result in enumerate(combine(activated, share, experts_out, t, slots)):
            distance = group * j + p
            result = swapped(result, "ep", distance) if distance else result
            total = total + result.astype(jnp.float32)
    return total.astype(jnp.bfloat16).T


def solution(mesh):
    in_specs = (
        P(("groups", "ep", "sub"), "tp"),
        P(("groups", "ep", "sub"), "tp"),
        P(("groups", "ep", "sub"), "tp"),
        P("tp"),
        P("tp", "ep"),
        P(("groups", "ep", "sub"), None),
        P(),
        P(("ep", "sub"), None, None, "tp"),
        P(("ep", "sub"), None, "tp"),
        P(("groups", "ep", "sub"), None),
        P(("groups", "ep", "sub"), None),
    )
    out_specs = P(("groups", "ep", "sub"), "tp")
    return jax.shard_map(local, mesh=mesh, in_specs=in_specs, out_specs=out_specs, check_vma=False)
```

```python
import jax
import jax.numpy as jnp
from jax import lax
from jax.experimental import pallas as pl
from jax.experimental.pallas import tpu as pltpu
from jax.sharding import PartitionSpec as P

D = 2880
HD = 64
WIN = 128
TOP = 4
VMEM_BYTES = 16 * 1024 * 1024
FETCH_BYTES = 32 * 1024 * 1024


def shifted(block, axis, distance):
    devices = range(lax.axis_size(axis))
    route = [(i - distance, i) for i in devices if i - distance in devices]
    return lax.ppermute(block, axis, route)


def swapped(block, axis, distance):
    return lax.ppermute(block, axis, [(i, i ^ distance) for i in range(lax.axis_size(axis))])


def picked(blocks, index, axis):
    return lax.dynamic_index_in_dim(blocks, index, axis, keepdims=False)


def in_vmem(count):
    return [pl.BlockSpec(memory_space=pltpu.VMEM)] * count


def in_smem():
    return pl.BlockSpec(memory_space=pltpu.SMEM)


def cost(flops, bytes_accessed):
    return pl.CostEstimate(flops=flops, bytes_accessed=bytes_accessed, transcendentals=0)


def dot(left, right):
    return jnp.dot(left, right, preferred_element_type=jnp.float32)


def aligned(size):
    return size % 16 == 0


def params(limit=VMEM_BYTES):
    return pltpu.CompilerParams(vmem_limit_bytes=limit)


def attention_kernel(first_ref, sink_ref, q_ref, earlier_ref, k_ref, v_ref, routes_ref, *refs):
    residual_refs, out_refs = refs[: len(refs) // 2], refs[len(refs) // 2 :]
    width, depth = q_ref.shape[1], residual_refs[0].shape[0]
    for residual_ref, out_ref in zip(residual_refs, out_refs):
        out_ref[width : width + depth, :] = residual_ref[...]
        out_ref[width + depth :, :] = routes_ref[...]
    rows = q_ref.shape[0]
    kv_count = k_ref.shape[1] // HD
    pairs = q_ref.shape[1] // (2 * HD * kv_count)
    key = lax.broadcasted_iota(jnp.int32, (rows, rows), 0)
    query = lax.broadcasted_iota(jnp.int32, (rows, rows), 1)
    before = key > query
    shut = before & (first_ref[0] == 1)
    blank = jnp.zeros((2 * rows, HD), jnp.bfloat16)
    values = jnp.concatenate(
        [
            block.astype(jnp.float32).T.astype(jnp.bfloat16)
            for block in (earlier_ref[:, kv_count * HD :], v_ref[...])
        ],
        axis=1,
    )
    for g in range(kv_count):
        head = slice(g * HD, (g + 1) * HD)
        keys = jnp.concatenate([earlier_ref[:, head], k_ref[:, head]], axis=0) * jnp.bfloat16(HD ** (-0.5))
        keys = jnp.concatenate(
            [jnp.concatenate([keys, blank], axis=1), jnp.concatenate([blank, keys], axis=1)], axis=0
        )
        for i in range(pairs):
            start = (g * pairs + i) * 2 * HD
            products = lax.dot_general(
                keys,
                q_ref[:, start : start + 2 * HD],
                (((1,), (1,)), ((), ())),
                preferred_element_type=jnp.float32,
            )
            weights = []
            for side in range(2):
                sink = sink_ref[(g * pairs + i) * 2 + side]
                part = products[side * 2 * rows : (side + 1) * 2 * rows]
                scores = jnp.where(before, part[:rows], part[rows:])
                scores = jnp.where(shut, -1e30, scores)
                largest = jnp.maximum(jnp.max(scores, axis=0, keepdims=True), sink)
                numerator = jnp.exp(scores - largest)
                denominator = jnp.sum(numerator, axis=0, keepdims=True) + jnp.exp(sink - largest)
                numerator = numerator * (1.0 / denominator)
                weights.append(
                    jnp.concatenate(
                        [
                            jnp.where(before, numerator, 0.0).astype(jnp.bfloat16),
                            jnp.where(before, 0.0, numerator).astype(jnp.bfloat16),
                        ],
                        axis=0,
                    )
                )
            result = dot(values[head], jnp.concatenate(weights, axis=1)).astype(jnp.bfloat16)
            for out_ref in out_refs:
                out_ref[start : start + HD, :] = result[:, :rows]
                out_ref[start + HD : start + 2 * HD, :] = result[:, rows:]


def attention(queries, earlier, key_rows, value_rows, sink_logits, first, routes, residuals):
    rows, width = queries.shape
    height = width + residuals[0].shape[0] + routes.shape[0]
    return pl.pallas_call(
        attention_kernel,
        out_shape=tuple(jax.ShapeDtypeStruct((height, rows), jnp.bfloat16) for _ in residuals),
        in_specs=[in_smem(), in_smem()] + in_vmem(5 + len(residuals)),
        out_specs=tuple(in_vmem(len(residuals))),
        compiler_params=params(),
        cost_estimate=cost(8 * rows * rows * width, 6 * rows * width),
        name="attention",
    )(first, sink_logits, queries, earlier, key_rows, value_rows, routes, *residuals)


def flip(arrays):
    def kernel(*refs):
        for i in range(len(arrays)):
            refs[len(arrays) + i][...] = refs[i][...].T

    return pl.pallas_call(
        kernel,
        out_shape=tuple(jax.ShapeDtypeStruct(a.shape[::-1], a.dtype) for a in arrays),
        in_specs=in_vmem(len(arrays)),
        out_specs=tuple(in_vmem(len(arrays))),
        compiler_params=params(FETCH_BYTES),
        cost_estimate=cost(0, 4 * sum(a.size for a in arrays)),
        name="flip",
    )(*arrays)


def project(attended, weights, t, s, t_count):
    slots = len(attended)
    rows = attended[0].shape[1]
    columns, depth = weights[0].shape
    shares = len(weights)
    width = shares * depth

    def kernel(place_ref, *refs):
        attended_refs = refs[:slots]
        weight_refs = refs[slots : slots + shares]
        kept_ref, sent_ref, total = refs[slots + shares :]
        t, s = place_ref[0], place_ref[1]
        result = 0.0
        for u in range(shares):
            span = pl.ds(pl.multiple_of((s ^ u) * depth, 128), depth)
            block = jnp.concatenate([ref[span, :] for ref in attended_refs], axis=1)
            result = result + dot(weight_refs[u][...], block)
        total[...] = result
        for m in range(t_count):
            block = total[:, pl.ds(pl.multiple_of((t ^ m) * rows, 128), rows)]
            if m == 0:
                kept_ref[...] = block
            else:
                sent_ref[m - 1] = block.astype(jnp.bfloat16)

    return pl.pallas_call(
        kernel,
        out_shape=(
            jax.ShapeDtypeStruct((columns, rows), jnp.float32),
            jax.ShapeDtypeStruct((t_count - 1, columns, rows), jnp.bfloat16),
        ),
        in_specs=[in_smem()] + in_vmem(slots + shares),
        out_specs=tuple(in_vmem(2)),
        scratch_shapes=[pltpu.VMEM((columns, slots * rows), jnp.float32)],
        compiler_params=params(),
        cost_estimate=cost(2 * slots * rows * width * columns, 2 * width * columns),
        name="project",
    )(jnp.stack([t, s]).astype(jnp.int32), *attended, *weights)


def activate(pieces, gain_table, weights, pair, t, chosen):
    slots = len(pieces)
    height, rows = pieces[0][0].shape
    depth = D // slots
    lanes = slots * rows
    experts = len(weights)
    units = weights[0].shape[0] // 2

    def kernel(place_ref, *refs):
        piece_refs = refs[: slots * slots]
        table_ref = refs[slots * slots]
        weight_refs = refs[slots * slots + 1 : slots * slots + 1 + experts]
        out_ref, share_ref, rows_ref, stage_ref, routes_ref, held_ref, arrived = refs[
            slots * slots + 1 + experts :
        ]
        copies = [
            pltpu.make_async_copy(weight_refs[e], held_ref.at[e - 1], arrived.at[e - 1])
            for e in range(1, experts)
        ]
        for copy in copies:
            copy.start()
        for m in range(slots):
            for r in range(slots):
                lane = pl.ds(pl.multiple_of((place_ref[1] ^ r ^ m) * rows, 128), rows)
                index = place_ref[0] ^ r
                piece_ref = piece_refs[m * slots + r]
                block = piece_ref[:depth, :]
                if aligned(depth):
                    rows_ref[pl.ds(pl.multiple_of(index * depth, 16), depth), lane] = block
                else:
                    stage_ref[index, :, lane] = block
                if not r:
                    routes_ref[:, lane] = piece_ref[depth:, :]
        if not aligned(depth):
            for index in range(slots):
                rows_ref[index * depth : (index + 1) * depth, :] = stage_ref[index]
        routes = routes_ref[...].astype(jnp.float32)
        scores = routes[TOP : 2 * TOP] * 256.0 + routes[2 * TOP : 3 * TOP]
        scores = scores / jnp.sum(scores, axis=0, keepdims=True)
        for e in range(experts):
            mine = routes[:TOP] == place_ref[2 + e].astype(jnp.float32)
            share_ref[e : e + 1, :] = jnp.sum(jnp.where(mine, scores, 0.0), axis=0, keepdims=True)
        plain = rows_ref[...].astype(jnp.float32)
        square = jnp.sum(dot(table_ref[...], (plain * plain).astype(jnp.bfloat16)), axis=0, keepdims=True)
        scale = lax.rsqrt(square / D + 1e-05)
        for e in range(experts):
            if e:
                copies[e - 1].wait()
            both = dot(held_ref[e - 1] if e else weight_refs[0][...], rows_ref[...]) * scale
            gate, up = both[:units], both[units:]
            out_ref[e] = ((up + 1.0) * gate * jax.nn.sigmoid(1.702 * gate)).astype(jnp.bfloat16)

    flat = [piece for part in pieces for piece in part]
    return pl.pallas_call(
        kernel,
        out_shape=(
            jax.ShapeDtypeStruct((experts, units, lanes), jnp.bfloat16),
            jax.ShapeDtypeStruct((experts, lanes), jnp.float32),
        ),
        in_specs=[in_smem()]
        + in_vmem(len(flat) + 2)
        + [pl.BlockSpec(memory_space=pl.ANY)] * (experts - 1),
        out_specs=tuple(in_vmem(2)),
        scratch_shapes=[
            pltpu.VMEM((D, lanes), jnp.bfloat16),
            pltpu.VMEM((1, 16, 128) if aligned(depth) else (slots, depth, lanes), jnp.bfloat16),
            pltpu.VMEM((height - depth, lanes), jnp.bfloat16),
            pltpu.VMEM((max(1, experts - 1), 2 * units, D), jnp.bfloat16),
            pltpu.SemaphoreType.DMA((max(1, experts - 1),)),
        ],
        compiler_params=params(FETCH_BYTES),
        cost_estimate=cost(4 * experts * lanes * D * units, 4 * experts * D * units),
        name="activate",
    )(jnp.stack([pair, t] + chosen).astype(jnp.int32), *flat, gain_table, *weights)


def combine(activated, share, weights, t, slots):
    t_count = len(activated)
    experts, units, lanes = activated[0].shape
    width = weights[0].shape[0]
    rows = lanes // slots

    def kernel(t_ref, *refs):
        activated_refs = refs[:t_count]
        share_ref = refs[t_count]
        weight_refs = refs[t_count + 1 : t_count + 1 + experts]
        *out_refs, all_ref, stage_ref, held_ref, arrived = refs[t_count + 1 + experts :]
        copies = [
            pltpu.make_async_copy(weight_refs[e], held_ref.at[e - 1], arrived.at[e - 1])
            for e in range(1, experts)
        ]
        for copy in copies:
            copy.start()
        for u in range(t_count):
            index = t_ref[0] ^ u
            if aligned(units):
                all_ref[:, pl.ds(pl.multiple_of(index * units, 16), units), :] = activated_refs[u][...]
            else:
                stage_ref[index] = activated_refs[u][...]
        if not aligned(units):
            for index in range(t_count):
                all_ref[:, index * units : (index + 1) * units, :] = stage_ref[index]
        total = 0.0
        for e in range(experts):
            if e:
                copies[e - 1].wait()
            result = dot(held_ref[e - 1] if e else weight_refs[0][...], all_ref[e])
            result = result.astype(jnp.bfloat16).astype(jnp.float32)
            total = total + share_ref[e : e + 1, :] * result
        for j in range(slots):
            out_refs[j][...] = total[:, j * rows : (j + 1) * rows].astype(jnp.bfloat16)

    return pl.pallas_call(
        kernel,
        out_shape=tuple(jax.ShapeDtypeStruct((width, rows), jnp.bfloat16) for _ in range(slots)),
        in_specs=[in_smem()]
        + in_vmem(t_count + 2)
        + [pl.BlockSpec(memory_space=pl.ANY)] * (experts - 1),
        out_specs=tuple(in_vmem(slots)),
        scratch_shapes=[
            pltpu.VMEM((experts, t_count * units, lanes), jnp.bfloat16),
            pltpu.VMEM((1, 1, 16, 128) if aligned(units) else (t_count, experts, units, lanes), jnp.bfloat16),
            pltpu.VMEM((max(1, experts - 1), width, t_count * units), jnp.bfloat16),
            pltpu.SemaphoreType.DMA((max(1, experts - 1),)),
        ],
        compiler_params=params(FETCH_BYTES),
        cost_estimate=cost(
            2 * experts * lanes * t_count * units * width, 2 * experts * t_count * units * width
        ),
        name="combine",
    )(t.reshape(1), *activated, share, *weights)


def local(
    queries,
    key_rows,
    value_rows,
    sink_logits,
    out_weight,
    residual,
    norm_gain,
    expert_in,
    expert_out,
    routes,
    route_scores,
):
    rows = queries.shape[0]
    z_count, t_count, s_count = lax.axis_size("ep"), lax.axis_size("tp"), lax.axis_size("sub")
    z, t, s = (lax.axis_index(name).astype(jnp.int32) for name in ("ep", "tp", "sub"))
    columns = out_weight.shape[1]
    width = expert_out.shape[2]
    slots = t_count
    group = z_count // slots
    pair = z // group

    paired = jnp.concatenate([key_rows, value_rows], axis=1)
    earlier = shifted(paired, ("ep", "sub"), 1)
    out_weight = out_weight.T
    depth = out_weight.shape[1] // s_count
    near = lax.dynamic_slice_in_dim(out_weight, s * depth, depth, 1)
    residual = residual.T.reshape(slots, group * columns, rows)
    residuals = [picked(residual, pair ^ j, 0) for j in range(slots)]
    route_rows = jnp.concatenate(
        [routes.T, route_scores.T // 256, route_scores.T % 256, jnp.zeros((16 - 3 * TOP, rows), jnp.int32)], axis=0
    ).astype(jnp.bfloat16)
    earlier, near, residuals, route_rows, expert_in, expert_out = lax.optimization_barrier(
        (earlier, near, residuals, route_rows, expert_in, expert_out)
    )

    near = swapped(near, "ep", 1)

    expert_in = expert_in[0].transpose(0, 2, 1).reshape(-1, D)
    expert_out = expert_out[0]
    experts_in = [expert_in] + [swapped(expert_in, "sub", e) for e in range(1, s_count)]
    experts_out = [expert_out] + [swapped(expert_out, "sub", e) for e in range(1, s_count)]
    chosen = [z * s_count + (s ^ e) for e in range(s_count)]

    first = (lax.axis_index(("ep", "sub")) == 0).astype(jnp.int32).reshape(1)
    sent = attention(
        queries, earlier, key_rows, value_rows, sink_logits, first, route_rows, residuals[1:]
    )
    gathered = [sent[0]] + [swapped(sent[j - 1], "ep", group * j) for j in range(1, slots)]
    experts_out, _ = lax.optimization_barrier((experts_out, sent))
    experts_out = flip(experts_out)

    gathered, near, experts_out = lax.optimization_barrier((gathered, near, experts_out))
    near_weights = [near] + [swapped(near, "sub", u) for u in range(1, s_count)]
    mine = project(gathered, [out_weight], t, s * 0, t_count)
    other = project(gathered, near_weights, t, s, t_count)
    first_member = z % group == 0

    def ordered(a, b):
        return jnp.concatenate([jnp.where(first_member, a, b), jnp.where(first_member, b, a)], axis=0)

    width_in, below = queries.shape[1], group * columns
    residual_part, kept_routes = residuals[0], route_rows
    for j in range(1, slots):
        residual_part = jnp.where(t == j, gathered[j][width_in : width_in + below], residual_part)
        kept_routes = jnp.where(t == j, gathered[j][width_in + below :], kept_routes)
    hidden = ordered(mine[0], other[0]) + residual_part.astype(jnp.float32)
    for m in range(1, t_count):
        received = swapped(ordered(mine[1][m - 1], other[1][m - 1]), "tp", m)
        hidden = hidden + received.astype(jnp.float32)
    gain_part = picked(norm_gain.reshape(slots, group * columns), pair, 0)
    scaled = jnp.concatenate([(hidden * gain_part[:, None]).astype(jnp.bfloat16), kept_routes], axis=0)

    own = {0: scaled}
    pieces = [own] + [{} for m in range(1, t_count)]
    distance = z_count // 2
    while distance:
        held = list(own)
        if distance >= group:
            for m in range(1, t_count):
                pieces[m].update({d: swapped(own[d], "tp", m) for d in held if d not in pieces[m]})
        for d in held:
            own[d + distance] = swapped(own[d], "ep", distance)
        distance //= 2
    for m in range(1, t_count):
        pieces[m].update({d: swapped(own[d], "tp", m) for d in range(0, z_count, group) if d not in pieces[m]})
    late = {d: own[d] for d in own if d % group}
    late, pieces[1:] = lax.optimization_barrier((late, pieces[1:]))
    for m in range(1, t_count):
        pieces[m].update({d: swapped(late[d], "tp", m) for d in late})

    inverse_gain = 1.0 / norm_gain
    inverse_square = inverse_gain * inverse_gain
    coarse = inverse_square.astype(jnp.bfloat16)
    fine = (inverse_square - coarse.astype(jnp.float32)).astype(jnp.bfloat16)
    gain_table = jnp.concatenate([coarse[None], fine[None], jnp.zeros((14, D), jnp.bfloat16)], axis=0)

    total = 0.0
    for m in range(t_count):
        for r in range(slots):
            here = (pair == m) & ((pair ^ t) == r)
            total = total + jnp.where(here, pieces[m][group * r][:width].astype(jnp.float32), 0.0)
    total = total * lax.dynamic_slice_in_dim(inverse_gain, t * width, width, 0)[:, None]
    total = lax.optimization_barrier(total)

    after = None
    for p in range(group):
        part = [[pieces[m][group * r + p] for r in range(slots)] for m in range(t_count)]
        if p:
            part, after = lax.optimization_barrier((part, after))
        activated, share = activate(part, gain_table, experts_in, pair, t, chosen)
        after = activated
        activated = [activated] + [swapped(activated, "tp", m) for m in range(1, t_count)]
        for j, result in enumerate(combine(activated, share, experts_out, t, slots)):
            distance = group * j + p
            result = swapped(result, "ep", distance) if distance else result
            total = total + result.astype(jnp.float32)
    return total.astype(jnp.bfloat16).T


def solution(mesh):
    in_specs = (
        P(("groups", "ep", "sub"), "tp"),
        P(("groups", "ep", "sub"), "tp"),
        P(("groups", "ep", "sub"), "tp"),
        P("tp"),
        P("tp", "ep"),
        P(("groups", "ep", "sub"), None),
        P(),
        P(("ep", "sub"), None, None, "tp"),
        P(("ep", "sub"), None, "tp"),
        P(("groups", "ep", "sub"), None),
        P(("groups", "ep", "sub"), None),
    )
    out_specs = P(("groups", "ep", "sub"), "tp")
    return jax.shard_map(local, mesh=mesh, in_specs=in_specs, out_specs=out_specs, check_vma=False)
```

```python
import jax
import jax.numpy as jnp
from jax import lax
from jax.experimental import pallas as pl
from jax.experimental.pallas import tpu as pltpu
from jax.sharding import PartitionSpec as P

D = 2880
HD = 64
WIN = 128
TOP = 4
VMEM_BYTES = 16 * 1024 * 1024


def shifted(block, axis, distance):
    devices = range(lax.axis_size(axis))
    route = [(i - distance, i) for i in devices if i - distance in devices]
    return lax.ppermute(block, axis, route)


def swapped(block, axis, distance):
    return lax.ppermute(block, axis, [(i, i ^ distance) for i in range(lax.axis_size(axis))])


def picked(blocks, index, axis):
    return lax.dynamic_index_in_dim(blocks, index, axis, keepdims=False)


def in_vmem(count):
    return [pl.BlockSpec(memory_space=pltpu.VMEM)] * count


def in_smem():
    return pl.BlockSpec(memory_space=pltpu.SMEM)


def cost(flops, bytes_accessed):
    return pl.CostEstimate(flops=flops, bytes_accessed=bytes_accessed, transcendentals=0)


def dot(left, right):
    return jnp.dot(left, right, preferred_element_type=jnp.float32)


def aligned(size):
    return size % 16 == 0


def params():
    return pltpu.CompilerParams(vmem_limit_bytes=VMEM_BYTES)


def attention_kernel(
    place_ref, sink_ref, q_ref, earlier_ref, k_ref, v_ref, residual_ref, routes_ref, scores_ref, *out_refs
):
    width, depth = q_ref.shape[1], residual_ref.shape[1]
    numbers = [routes_ref[...], scores_ref[...] // 256, scores_ref[...] % 256]
    numbers.append(jnp.zeros((out_refs[0].shape[0] - width - depth - 3 * TOP, q_ref.shape[0]), jnp.int32))
    numbers = jnp.concatenate(numbers, axis=0).astype(jnp.float32).astype(jnp.bfloat16)
    for j, out_ref in enumerate(out_refs):
        out_ref[width : width + depth, :] = residual_ref[place_ref[1] ^ (j + 1)]
        out_ref[width + depth :, :] = numbers
    rows = q_ref.shape[0]
    kv_count = k_ref.shape[1] // HD
    pairs = q_ref.shape[1] // (2 * HD * kv_count)
    key = lax.broadcasted_iota(jnp.int32, (rows, rows), 0)
    query = lax.broadcasted_iota(jnp.int32, (rows, rows), 1)
    before = key > query
    shut = before & (place_ref[0] == 1)
    blank = jnp.zeros((2 * rows, HD), jnp.bfloat16)
    values = jnp.concatenate(
        [
            block.astype(jnp.float32).T.astype(jnp.bfloat16)
            for block in (earlier_ref[:, kv_count * HD :], v_ref[...])
        ],
        axis=1,
    )
    for g in range(kv_count):
        head = slice(g * HD, (g + 1) * HD)
        keys = jnp.concatenate([earlier_ref[:, head], k_ref[:, head]], axis=0) * jnp.bfloat16(HD ** (-0.5))
        keys = jnp.concatenate(
            [jnp.concatenate([keys, blank], axis=1), jnp.concatenate([blank, keys], axis=1)], axis=0
        )
        for i in range(pairs):
            start = (g * pairs + i) * 2 * HD
            products = lax.dot_general(
                keys,
                q_ref[:, start : start + 2 * HD],
                (((1,), (1,)), ((), ())),
                preferred_element_type=jnp.float32,
            )
            weights = []
            for side in range(2):
                sink = sink_ref[(g * pairs + i) * 2 + side]
                part = products[side * 2 * rows : (side + 1) * 2 * rows]
                scores = jnp.where(before, part[:rows], part[rows:])
                scores = jnp.where(shut, -1e30, scores)
                largest = jnp.maximum(jnp.max(scores, axis=0, keepdims=True), sink)
                numerator = jnp.exp(scores - largest)
                denominator = jnp.sum(numerator, axis=0, keepdims=True) + jnp.exp(sink - largest)
                numerator = numerator * (1.0 / denominator)
                weights.append(
                    jnp.concatenate(
                        [
                            jnp.where(before, numerator, 0.0).astype(jnp.bfloat16),
                            jnp.where(before, 0.0, numerator).astype(jnp.bfloat16),
                        ],
                        axis=0,
                    )
                )
            result = dot(values[head], jnp.concatenate(weights, axis=1)).astype(jnp.bfloat16)
            for out_ref in out_refs:
                out_ref[start : start + HD, :] = result[:, :rows]
                out_ref[start + HD : start + 2 * HD, :] = result[:, rows:]


def attention(queries, earlier, key_rows, value_rows, sink_logits, place, residual, routes, scores):
    rows, width = queries.shape
    slots, depth, _ = residual.shape
    return pl.pallas_call(
        attention_kernel,
        out_shape=tuple(
            jax.ShapeDtypeStruct((width + depth + 16, rows), jnp.bfloat16) for _ in range(slots - 1)
        ),
        in_specs=[in_smem(), in_smem()] + in_vmem(7),
        out_specs=tuple(in_vmem(slots - 1)),
        compiler_params=params(),
        cost_estimate=cost(8 * rows * rows * width, 6 * rows * width),
        name="attention",
    )(place, sink_logits, queries, earlier, key_rows, value_rows, residual, routes, scores)


def flip(arrays):
    def kernel(*refs):
        for i in range(len(arrays)):
            refs[len(arrays) + i][...] = refs[i][...].T

    return pl.pallas_call(
        kernel,
        out_shape=tuple(jax.ShapeDtypeStruct(a.shape[::-1], a.dtype) for a in arrays),
        in_specs=in_vmem(len(arrays)),
        out_specs=tuple(in_vmem(len(arrays))),
        compiler_params=params(),
        cost_estimate=cost(0, 4 * sum(a.size for a in arrays)),
        name="flip",
    )(*arrays)


def project(attended, weights, t, s, t_count):
    slots = len(attended)
    rows = attended[0].shape[1]
    columns, depth = weights[0].shape
    shares = len(weights)
    width = shares * depth

    def kernel(place_ref, *refs):
        attended_refs = refs[:slots]
        weight_refs = refs[slots : slots + shares]
        kept_ref, sent_ref, total = refs[slots + shares :]
        t, s = place_ref[0], place_ref[1]
        result = 0.0
        for u in range(shares):
            span = pl.ds(pl.multiple_of((s ^ u) * depth, 128), depth)
            block = jnp.concatenate([ref[span, :] for ref in attended_refs], axis=1)
            result = result + dot(weight_refs[u][...], block)
        total[...] = result
        for m in range(t_count):
            block = total[:, pl.ds(pl.multiple_of((t ^ m) * rows, 128), rows)]
            if m == 0:
                kept_ref[...] = block
            else:
                sent_ref[m - 1] = block.astype(jnp.bfloat16)

    return pl.pallas_call(
        kernel,
        out_shape=(
            jax.ShapeDtypeStruct((columns, rows), jnp.float32),
            jax.ShapeDtypeStruct((t_count - 1, columns, rows), jnp.bfloat16),
        ),
        in_specs=[in_smem()] + in_vmem(slots + shares),
        out_specs=tuple(in_vmem(2)),
        scratch_shapes=[pltpu.VMEM((columns, slots * rows), jnp.float32)],
        compiler_params=params(),
        cost_estimate=cost(2 * slots * rows * width * columns, 2 * width * columns),
        name="project",
    )(jnp.stack([t, s]).astype(jnp.int32), *attended, *weights)


def activate(pieces, gain_table, weights, pair, t, chosen):
    slots = len(pieces)
    height, rows = pieces[0][0].shape
    depth = D // slots
    lanes = slots * rows
    experts = len(weights)
    units = weights[0].shape[1]

    def kernel(place_ref, *refs):
        piece_refs = refs[: slots * slots]
        table_ref = refs[slots * slots]
        weight_refs = refs[slots * slots + 1 : slots * slots + 1 + experts]
        out_ref, share_ref, rows_ref, stage_ref, routes_ref = refs[slots * slots + 1 + experts :]
        for m in range(slots):
            for r in range(slots):
                lane = pl.ds(pl.multiple_of((place_ref[1] ^ r ^ m) * rows, 128), rows)
                index = place_ref[0] ^ r
                piece_ref = piece_refs[m * slots + r]
                block = piece_ref[:depth, :]
                if aligned(depth):
                    rows_ref[pl.ds(pl.multiple_of(index * depth, 16), depth), lane] = block
                else:
                    stage_ref[index, :, lane] = block
                if not r:
                    routes_ref[:, lane] = piece_ref[depth:, :]
        if not aligned(depth):
            for index in range(slots):
                rows_ref[index * depth : (index + 1) * depth, :] = stage_ref[index]
        routes = routes_ref[...].astype(jnp.float32)
        scores = routes[TOP : 2 * TOP] * 256.0 + routes[2 * TOP : 3 * TOP]
        scores = scores / jnp.sum(scores, axis=0, keepdims=True)
        for e in range(experts):
            mine = routes[:TOP] == place_ref[2 + e].astype(jnp.float32)
            share_ref[e : e + 1, :] = jnp.sum(jnp.where(mine, scores, 0.0), axis=0, keepdims=True)
        plain = rows_ref[...].astype(jnp.float32)
        square = jnp.sum(dot(table_ref[...], (plain * plain).astype(jnp.bfloat16)), axis=0, keepdims=True)
        scale = lax.rsqrt(square / D + 1e-05)
        for e in range(experts):
            gate = dot(weight_refs[e][0], rows_ref[...]) * scale
            up = dot(weight_refs[e][1], rows_ref[...]) * scale
            out_ref[e] = ((up + 1.0) * gate * jax.nn.sigmoid(1.702 * gate)).astype(jnp.bfloat16)

    flat = [piece for part in pieces for piece in part]
    return pl.pallas_call(
        kernel,
        out_shape=(
            jax.ShapeDtypeStruct((experts, units, lanes), jnp.bfloat16),
            jax.ShapeDtypeStruct((experts, lanes), jnp.float32),
        ),
        in_specs=[in_smem()] + in_vmem(len(flat) + 1 + experts),
        out_specs=tuple(in_vmem(2)),
        scratch_shapes=[
            pltpu.VMEM((D, lanes), jnp.bfloat16),
            pltpu.VMEM((1, 16, 128) if aligned(depth) else (slots, depth, lanes), jnp.bfloat16),
            pltpu.VMEM((height - depth, lanes), jnp.bfloat16),
        ],
        compiler_params=params(),
        cost_estimate=cost(4 * experts * lanes * D * units, 4 * experts * D * units),
        name="activate",
    )(jnp.stack([pair, t] + chosen).astype(jnp.int32), *flat, gain_table, *weights)


def combine(activated, share, weights, t, slots):
    t_count = len(activated)
    experts, units, lanes = activated[0].shape
    width = weights[0].shape[0]
    rows = lanes // slots

    def kernel(t_ref, *refs):
        activated_refs = refs[:t_count]
        share_ref = refs[t_count]
        weight_refs = refs[t_count + 1 : t_count + 1 + experts]
        *out_refs, all_ref, stage_ref = refs[t_count + 1 + experts :]
        for u in range(t_count):
            index = t_ref[0] ^ u
            if aligned(units):
                all_ref[:, pl.ds(pl.multiple_of(index * units, 16), units), :] = activated_refs[u][...]
            else:
                stage_ref[index] = activated_refs[u][...]
        if not aligned(units):
            for index in range(t_count):
                all_ref[:, index * units : (index + 1) * units, :] = stage_ref[index]
        total = 0.0
        for e in range(experts):
            result = dot(weight_refs[e][...], all_ref[e]).astype(jnp.bfloat16).astype(jnp.float32)
            total = total + share_ref[e : e + 1, :] * result
        for j in range(slots):
            out_refs[j][...] = total[:, j * rows : (j + 1) * rows].astype(jnp.bfloat16)

    return pl.pallas_call(
        kernel,
        out_shape=tuple(jax.ShapeDtypeStruct((width, rows), jnp.bfloat16) for _ in range(slots)),
        in_specs=[in_smem()] + in_vmem(t_count + 1 + experts),
        out_specs=tuple(in_vmem(slots)),
        scratch_shapes=[
            pltpu.VMEM((experts, t_count * units, lanes), jnp.bfloat16),
            pltpu.VMEM((1, 1, 16, 128) if aligned(units) else (t_count, experts, units, lanes), jnp.bfloat16),
        ],
        compiler_params=params(),
        cost_estimate=cost(
            2 * experts * lanes * t_count * units * width, 2 * experts * t_count * units * width
        ),
        name="combine",
    )(t.reshape(1), *activated, share, *weights)


def local(
    queries,
    key_rows,
    value_rows,
    sink_logits,
    out_weight,
    residual,
    norm_gain,
    expert_in,
    expert_out,
    routes,
    route_scores,
):
    rows = queries.shape[0]
    z_count, t_count, s_count = lax.axis_size("ep"), lax.axis_size("tp"), lax.axis_size("sub")
    z, t, s = (lax.axis_index(name).astype(jnp.int32) for name in ("ep", "tp", "sub"))
    columns = out_weight.shape[1]
    width = expert_out.shape[2]
    slots = t_count
    group = z_count // slots
    pair = z // group

    paired = jnp.concatenate([key_rows, value_rows], axis=1)
    earlier = shifted(paired, ("ep", "sub"), 1)
    out_weight = out_weight.T
    g_count = lax.axis_size("groups")
    share = s * g_count + lax.axis_index("groups").astype(jnp.int32)
    depth = out_weight.shape[1] // (s_count * g_count)
    near = lax.dynamic_slice_in_dim(out_weight, share * depth, depth, 1)
    residual = residual.T.reshape(slots, group * columns, rows)
    earlier, near, expert_in, expert_out = lax.optimization_barrier((earlier, near, expert_in, expert_out))

    near = swapped(near, "ep", 1)

    expert_in = expert_in[0].transpose(0, 2, 1)
    expert_out = expert_out[0]
    experts_in = [expert_in] + [swapped(expert_in, "sub", e) for e in range(1, s_count)]
    experts_out = [expert_out] + [swapped(expert_out, "sub", e) for e in range(1, s_count)]
    chosen = [z * s_count + (s ^ e) for e in range(s_count)]

    first = (lax.axis_index(("ep", "sub")) == 0).astype(jnp.int32)
    place = jnp.stack([first, pair])
    sent = attention(
        queries, earlier, key_rows, value_rows, sink_logits, place, residual, routes.T, route_scores.T
    )
    gathered = [sent[0]] + [swapped(sent[j - 1], "ep", group * j) for j in range(1, slots)]
    experts_out, _ = lax.optimization_barrier((experts_out, sent))
    experts_out = flip(experts_out)

    near, experts_out = lax.optimization_barrier((near, experts_out))
    near_weights = [near] + [swapped(near, "groups", g) for g in range(1, g_count)]
    near_weights = near_weights + [
        swapped(part, "sub", u) for u in range(1, s_count) for part in near_weights
    ]
    mine = project(gathered, [out_weight], t, s * 0, t_count)
    other = project(gathered, near_weights, t, share, t_count)
    first_member = z % group == 0

    def ordered(a, b):
        return jnp.concatenate([jnp.where(first_member, a, b), jnp.where(first_member, b, a)], axis=0)

    width_in, below = queries.shape[1], group * columns
    residual_part, kept_routes = picked(residual, pair, 0), gathered[0][width_in + below :]
    for j in range(1, slots):
        residual_part = jnp.where(t == j, gathered[j][width_in : width_in + below], residual_part)
        kept_routes = jnp.where(t == j, gathered[j][width_in + below :], kept_routes)
    hidden = ordered(mine[0], other[0]) + residual_part.astype(jnp.float32)
    for m in range(1, t_count):
        received = swapped(ordered(mine[1][m - 1], other[1][m - 1]), "tp", m)
        hidden = hidden + received.astype(jnp.float32)
    gain_part = picked(norm_gain.reshape(slots, group * columns), pair, 0)
    scaled = jnp.concatenate([(hidden * gain_part[:, None]).astype(jnp.bfloat16), kept_routes], axis=0)

    own = {0: scaled}
    distance = z_count // 2
    while distance >= group:
        own.update({d + distance: swapped(own[d], "ep", distance) for d in list(own)})
        distance //= 2
    pieces = [own] + [{d: swapped(own[d], "tp", m) for d in own} for m in range(1, t_count)]
    while distance:
        for part in pieces:
            part[distance] = swapped(part[0], "ep", distance)
        own.update({d + distance: swapped(own[d], "ep", distance) for d in list(own) if d + distance not in own})
        distance //= 2
    late = {d: own[d] for d in own if d not in pieces[-1]}
    late, pieces[1:] = lax.optimization_barrier((late, pieces[1:]))
    for m in range(1, t_count):
        pieces[m].update({d: swapped(late[d], "tp", m) for d in late})

    inverse_gain = 1.0 / norm_gain
    inverse_square = inverse_gain * inverse_gain
    coarse = inverse_square.astype(jnp.bfloat16)
    fine = (inverse_square - coarse.astype(jnp.float32)).astype(jnp.bfloat16)
    gain_table = jnp.concatenate([coarse[None], fine[None], jnp.zeros((14, D), jnp.bfloat16)], axis=0)

    total = 0.0
    for m in range(t_count):
        for r in range(slots):
            here = (pair == m) & ((pair ^ t) == r)
            total = total + jnp.where(here, pieces[m][group * r][:width].astype(jnp.float32), 0.0)
    total = total * lax.dynamic_slice_in_dim(inverse_gain, t * width, width, 0)[:, None]
    total = lax.optimization_barrier(total)

    after = None
    for p in range(group):
        part = [[pieces[m][group * r + p] for r in range(slots)] for m in range(t_count)]
        if p:
            part, after = lax.optimization_barrier((part, after))
        activated, share = activate(part, gain_table, experts_in, pair, t, chosen)
        after = activated
        activated = [activated] + [swapped(activated, "tp", m) for m in range(1, t_count)]
        for j, result in enumerate(combine(activated, share, experts_out, t, slots)):
            distance = group * j + p
            result = swapped(result, "ep", distance) if distance else result
            total = total + result.astype(jnp.float32)
    return total.astype(jnp.bfloat16).T


def solution(mesh):
    in_specs = (
        P(("groups", "ep", "sub"), "tp"),
        P(("groups", "ep", "sub"), "tp"),
        P(("groups", "ep", "sub"), "tp"),
        P("tp"),
        P("tp", "ep"),
        P(("groups", "ep", "sub"), None),
        P(),
        P(("ep", "sub"), None, None, "tp"),
        P(("ep", "sub"), None, "tp"),
        P(("groups", "ep", "sub"), None),
        P(("groups", "ep", "sub"), None),
    )
    out_specs = P(("groups", "ep", "sub"), "tp")
    return jax.shard_map(local, mesh=mesh, in_specs=in_specs, out_specs=out_specs, check_vma=False)
```

```python
import jax
import jax.numpy as jnp
from jax import lax
from jax.experimental import pallas as pl
from jax.experimental.pallas import tpu as pltpu
from jax.sharding import PartitionSpec as P

D = 2880
HD = 64
WIN = 128
TOP = 4
VMEM_BYTES = 16 * 1024 * 1024


def shifted(block, axis, distance):
    devices = range(lax.axis_size(axis))
    route = [(i - distance, i) for i in devices if i - distance in devices]
    return lax.ppermute(block, axis, route)


def swapped(block, axis, distance):
    return lax.ppermute(block, axis, [(i, i ^ distance) for i in range(lax.axis_size(axis))])


def picked(blocks, index, axis):
    return lax.dynamic_index_in_dim(blocks, index, axis, keepdims=False)


def in_vmem(count):
    return [pl.BlockSpec(memory_space=pltpu.VMEM)] * count


def in_smem():
    return pl.BlockSpec(memory_space=pltpu.SMEM)


def cost(flops, bytes_accessed):
    return pl.CostEstimate(flops=flops, bytes_accessed=bytes_accessed, transcendentals=0)


def dot(left, right):
    return jnp.dot(left, right, preferred_element_type=jnp.float32)


def aligned(size):
    return size % 16 == 0


def fetches(source, target, arrived, cuts):
    return [
        pltpu.make_async_copy(source.at[cut], target.at[cut], arrived.at[index]) for index, cut in enumerate(cuts)
    ]


def cuts_of(lead, size, count):
    count = count if size % (16 * count) == 0 else 1
    step = size // count
    return [(*at, pl.ds(i * step, step)) for at in lead for i in range(count)]


def params():
    return pltpu.CompilerParams(vmem_limit_bytes=VMEM_BYTES)


def attention_kernel(place_ref, sink_ref, q_ref, earlier_ref, k_ref, v_ref, routes_ref, scores_ref, out_ref):
    width = q_ref.shape[1]
    numbers = [routes_ref[...], scores_ref[...] // 256, scores_ref[...] % 256]
    numbers.append(jnp.zeros((out_ref.shape[0] - width - 3 * TOP, q_ref.shape[0]), jnp.int32))
    out_ref[width:, :] = jnp.concatenate(numbers, axis=0).astype(jnp.float32).astype(jnp.bfloat16)
    rows = q_ref.shape[0]
    kv_count = k_ref.shape[1] // HD
    pairs = q_ref.shape[1] // (2 * HD * kv_count)
    key = lax.broadcasted_iota(jnp.int32, (rows, rows), 0)
    query = lax.broadcasted_iota(jnp.int32, (rows, rows), 1)
    before = key > query
    shut = before & (place_ref[0] == 1)
    blank = jnp.zeros((2 * rows, HD), jnp.bfloat16)
    values = jnp.concatenate(
        [
            block.astype(jnp.float32).T.astype(jnp.bfloat16)
            for block in (earlier_ref[:, kv_count * HD :], v_ref[...])
        ],
        axis=1,
    )
    for g in range(kv_count):
        head = slice(g * HD, (g + 1) * HD)
        keys = jnp.concatenate([earlier_ref[:, head], k_ref[:, head]], axis=0) * jnp.bfloat16(HD ** (-0.5))
        keys = jnp.concatenate(
            [jnp.concatenate([keys, blank], axis=1), jnp.concatenate([blank, keys], axis=1)], axis=0
        )
        for i in range(pairs):
            start = (g * pairs + i) * 2 * HD
            products = lax.dot_general(
                keys,
                q_ref[:, start : start + 2 * HD],
                (((1,), (1,)), ((), ())),
                preferred_element_type=jnp.float32,
            )
            weights = []
            for side in range(2):
                sink = sink_ref[(g * pairs + i) * 2 + side]
                part = products[side * 2 * rows : (side + 1) * 2 * rows]
                scores = jnp.where(before, part[:rows], part[rows:])
                scores = jnp.where(shut, -1e30, scores)
                largest = jnp.maximum(jnp.max(scores, axis=0, keepdims=True), sink)
                numerator = jnp.exp(scores - largest)
                denominator = jnp.sum(numerator, axis=0, keepdims=True) + jnp.exp(sink - largest)
                numerator = numerator * (1.0 / denominator)
                weights.append(
                    jnp.concatenate(
                        [
                            jnp.where(before, numerator, 0.0).astype(jnp.bfloat16),
                            jnp.where(before, 0.0, numerator).astype(jnp.bfloat16),
                        ],
                        axis=0,
                    )
                )
            result = dot(values[head], jnp.concatenate(weights, axis=1)).astype(jnp.bfloat16)
            out_ref[start : start + HD, :] = result[:, :rows]
            out_ref[start + HD : start + 2 * HD, :] = result[:, rows:]


def attention(queries, earlier, key_rows, value_rows, sink_logits, first, routes, scores):
    rows, width = queries.shape
    return pl.pallas_call(
        attention_kernel,
        out_shape=jax.ShapeDtypeStruct((width + 16, rows), jnp.bfloat16),
        in_specs=[in_smem(), in_smem()] + in_vmem(6),
        out_specs=in_vmem(1)[0],
        compiler_params=params(),
        cost_estimate=cost(8 * rows * rows * width, 6 * rows * width),
        name="attention",
    )(first, sink_logits, queries, earlier, key_rows, value_rows, routes, scores)


def flip(arrays):
    def kernel(*refs):
        for i in range(len(arrays)):
            refs[len(arrays) + i][...] = refs[i][...].T

    return pl.pallas_call(
        kernel,
        out_shape=tuple(jax.ShapeDtypeStruct(a.shape[::-1], a.dtype) for a in arrays),
        in_specs=in_vmem(len(arrays)),
        out_specs=tuple(in_vmem(len(arrays))),
        compiler_params=params(),
        cost_estimate=cost(0, 4 * sum(a.size for a in arrays)),
        name="flip",
    )(*arrays)


def project(attended, weights, t, s, t_count):
    slots = len(attended)
    rows = attended[0].shape[1]
    columns, depth = weights[0].shape
    shares = len(weights)
    width = shares * depth

    def kernel(place_ref, *refs):
        attended_refs = refs[:slots]
        weight_refs = refs[slots : slots + shares]
        kept_ref, sent_ref, total = refs[slots + shares :]
        t, s = place_ref[0], place_ref[1]
        result = 0.0
        for u in range(shares):
            span = pl.ds(pl.multiple_of((s ^ u) * depth, 128), depth)
            block = jnp.concatenate([ref[span, :] for ref in attended_refs], axis=1)
            result = result + dot(weight_refs[u][...], block)
        total[...] = result
        for m in range(t_count):
            block = total[:, pl.ds(pl.multiple_of((t ^ m) * rows, 128), rows)]
            if m == 0:
                kept_ref[...] = block
            else:
                sent_ref[m - 1] = block.astype(jnp.bfloat16)

    return pl.pallas_call(
        kernel,
        out_shape=(
            jax.ShapeDtypeStruct((columns, rows), jnp.float32),
            jax.ShapeDtypeStruct((t_count - 1, columns, rows), jnp.bfloat16),
        ),
        in_specs=[in_smem()] + in_vmem(slots + shares),
        out_specs=tuple(in_vmem(2)),
        scratch_shapes=[pltpu.VMEM((columns, slots * rows), jnp.float32)],
        compiler_params=params(),
        cost_estimate=cost(2 * slots * rows * width * columns, 2 * width * columns),
        name="project",
    )(jnp.stack([t, s]).astype(jnp.int32), *attended, *weights)


def activate(pieces, gain_table, weights, pair, t, chosen):
    slots = len(pieces)
    height, rows = pieces[0][0].shape
    depth = D // slots
    lanes = slots * rows
    experts = len(weights)
    units = weights[0].shape[1]
    cuts = cuts_of([(0,), (1,)], units, 3)

    def kernel(place_ref, *refs):
        piece_refs = refs[: slots * slots]
        table_ref = refs[slots * slots]
        weight_refs = refs[slots * slots + 1 : slots * slots + 1 + experts]
        out_ref, share_ref, rows_ref, stage_ref, routes_ref, held_ref, arrived = refs[
            slots * slots + 1 + experts :
        ]
        copies = [
            fetches(weight_refs[e], held_ref.at[e - 1], arrived.at[e - 1], cuts) for e in range(1, experts)
        ]
        for copy in sum(copies, []):
            copy.start()
        for m in range(slots):
            for r in range(slots):
                lane = pl.ds(pl.multiple_of((place_ref[1] ^ r ^ m) * rows, 128), rows)
                index = place_ref[0] ^ r
                piece_ref = piece_refs[m * slots + r]
                block = piece_ref[:depth, :]
                if aligned(depth):
                    rows_ref[pl.ds(pl.multiple_of(index * depth, 16), depth), lane] = block
                else:
                    stage_ref[index, :, lane] = block
                if not r:
                    routes_ref[:, lane] = piece_ref[depth:, :]
        if not aligned(depth):
            for index in range(slots):
                rows_ref[index * depth : (index + 1) * depth, :] = stage_ref[index]
        routes = routes_ref[...].astype(jnp.float32)
        scores = routes[TOP : 2 * TOP] * 256.0 + routes[2 * TOP : 3 * TOP]
        scores = scores / jnp.sum(scores, axis=0, keepdims=True)
        for e in range(experts):
            mine = routes[:TOP] == place_ref[2 + e].astype(jnp.float32)
            share_ref[e : e + 1, :] = jnp.sum(jnp.where(mine, scores, 0.0), axis=0, keepdims=True)
        plain = rows_ref[...].astype(jnp.float32)
        square = jnp.sum(dot(table_ref[...], (plain * plain).astype(jnp.bfloat16)), axis=0, keepdims=True)
        scale = lax.rsqrt(square / D + 1e-05)
        for e in range(experts):
            if e:
                for copy in copies[e - 1]:
                    copy.wait()
            weight_ref = held_ref.at[e - 1] if e else weight_refs[0]
            gate = dot(weight_ref[0], rows_ref[...]) * scale
            up = dot(weight_ref[1], rows_ref[...]) * scale
            out_ref[e] = ((up + 1.0) * gate * jax.nn.sigmoid(1.702 * gate)).astype(jnp.bfloat16)

    flat = [piece for part in pieces for piece in part]
    return pl.pallas_call(
        kernel,
        out_shape=(
            jax.ShapeDtypeStruct((experts, units, lanes), jnp.bfloat16),
            jax.ShapeDtypeStruct((experts, lanes), jnp.float32),
        ),
        in_specs=[in_smem()]
        + in_vmem(len(flat) + 2)
        + [pl.BlockSpec(memory_space=pl.ANY)] * (experts - 1),
        out_specs=tuple(in_vmem(2)),
        scratch_shapes=[
            pltpu.VMEM((D, lanes), jnp.bfloat16),
            pltpu.VMEM((1, 16, 128) if aligned(depth) else (slots, depth, lanes), jnp.bfloat16),
            pltpu.VMEM((height - depth, lanes), jnp.bfloat16),
            pltpu.VMEM((max(1, experts - 1), 2, units, D), jnp.bfloat16),
            pltpu.SemaphoreType.DMA((max(1, experts - 1), len(cuts))),
        ],
        compiler_params=params(),
        cost_estimate=cost(4 * experts * lanes * D * units, 4 * experts * D * units),
        name="activate",
    )(jnp.stack([pair, t] + chosen).astype(jnp.int32), *flat, gain_table, *weights)


def combine(activated, share, weights, t, slots):
    t_count = len(activated)
    experts, units, lanes = activated[0].shape
    width = weights[0].shape[0]
    rows = lanes // slots
    cuts = cuts_of([()], width, 3)

    def kernel(t_ref, *refs):
        activated_refs = refs[:t_count]
        share_ref = refs[t_count]
        weight_refs = refs[t_count + 1 : t_count + 1 + experts]
        *out_refs, all_ref, stage_ref, held_ref, arrived = refs[t_count + 1 + experts :]
        copies = [
            fetches(weight_refs[e], held_ref.at[e - 1], arrived.at[e - 1], cuts) for e in range(1, experts)
        ]
        for copy in sum(copies, []):
            copy.start()
        for u in range(t_count):
            index = t_ref[0] ^ u
            if aligned(units):
                all_ref[:, pl.ds(pl.multiple_of(index * units, 16), units), :] = activated_refs[u][...]
            else:
                stage_ref[index] = activated_refs[u][...]
        if not aligned(units):
            for index in range(t_count):
                all_ref[:, index * units : (index + 1) * units, :] = stage_ref[index]
        total = 0.0
        for e in range(experts):
            if e:
                for copy in copies[e - 1]:
                    copy.wait()
            weight_ref = held_ref.at[e - 1] if e else weight_refs[0]
            result = dot(weight_ref[...], all_ref[e]).astype(jnp.bfloat16).astype(jnp.float32)
            total = total + share_ref[e : e + 1, :] * result
        for j in range(slots):
            out_refs[j][...] = total[:, j * rows : (j + 1) * rows].astype(jnp.bfloat16)

    return pl.pallas_call(
        kernel,
        out_shape=tuple(jax.ShapeDtypeStruct((width, rows), jnp.bfloat16) for _ in range(slots)),
        in_specs=[in_smem()]
        + in_vmem(t_count + 2)
        + [pl.BlockSpec(memory_space=pl.ANY)] * (experts - 1),
        out_specs=tuple(in_vmem(slots)),
        scratch_shapes=[
            pltpu.VMEM((experts, t_count * units, lanes), jnp.bfloat16),
            pltpu.VMEM((1, 1, 16, 128) if aligned(units) else (t_count, experts, units, lanes), jnp.bfloat16),
            pltpu.VMEM((max(1, experts - 1), width, t_count * units), jnp.bfloat16),
            pltpu.SemaphoreType.DMA((max(1, experts - 1), len(cuts))),
        ],
        compiler_params=params(),
        cost_estimate=cost(
            2 * experts * lanes * t_count * units * width, 2 * experts * t_count * units * width
        ),
        name="combine",
    )(t.reshape(1), *activated, share, *weights)


def local(
    queries,
    key_rows,
    value_rows,
    sink_logits,
    out_weight,
    residual,
    norm_gain,
    expert_in,
    expert_out,
    routes,
    route_scores,
):
    rows = queries.shape[0]
    z_count, t_count, s_count = lax.axis_size("ep"), lax.axis_size("tp"), lax.axis_size("sub")
    z, t, s = (lax.axis_index(name).astype(jnp.int32) for name in ("ep", "tp", "sub"))
    columns = out_weight.shape[1]
    width = expert_out.shape[2]
    slots = t_count
    group = z_count // slots
    pair = z // group

    paired = jnp.concatenate([key_rows, value_rows], axis=1)
    earlier = shifted(paired, ("ep", "sub"), 1)
    out_weight = out_weight.T
    depth = out_weight.shape[1] // s_count
    near = lax.dynamic_slice_in_dim(out_weight, s * depth, depth, 1)
    residual = picked(residual.T.reshape(slots, group * columns, rows), pair ^ t, 0)
    earlier, near, residual, expert_in, expert_out = lax.optimization_barrier(
        (earlier, near, residual, expert_in, expert_out)
    )

    near = swapped(near, "ep", 1)

    route = [
        (i * t_count + k, (i ^ (group * k)) * t_count + k) for i in range(z_count) for k in range(t_count)
    ]
    residual = lax.ppermute(residual, ("ep", "tp"), route)

    expert_in = expert_in[0].transpose(0, 2, 1)
    expert_out = expert_out[0]
    experts_in = [expert_in] + [swapped(expert_in, "sub", e) for e in range(1, s_count)]
    experts_out = [expert_out] + [swapped(expert_out, "sub", e) for e in range(1, s_count)]
    chosen = [z * s_count + (s ^ e) for e in range(s_count)]

    first = (lax.axis_index(("ep", "sub")) == 0).astype(jnp.int32).reshape(1)
    attended = attention(
        queries, earlier, key_rows, value_rows, sink_logits, first, routes.T, route_scores.T
    )
    gathered = [attended] + [swapped(attended, "ep", group * j) for j in range(1, slots)]
    experts_out, _ = lax.optimization_barrier((experts_out, attended))
    experts_out = flip(experts_out)

    gathered, near, residual, experts_out = lax.optimization_barrier((gathered, near, residual, experts_out))
    near_weights = [near] + [swapped(near, "sub", u) for u in range(1, s_count)]
    mine = project(gathered, [out_weight], t, s * 0, t_count)
    other = project(gathered, near_weights, t, s, t_count)
    first_member = z % group == 0

    def ordered(a, b):
        return jnp.concatenate([jnp.where(first_member, a, b), jnp.where(first_member, b, a)], axis=0)

    kept_routes = gathered[0][queries.shape[1] :]
    for j in range(1, slots):
        kept_routes = jnp.where(t == j, gathered[j][queries.shape[1] :], kept_routes)
    hidden = ordered(mine[0], other[0]) + residual.astype(jnp.float32)
    for m in range(1, t_count):
        received = swapped(ordered(mine[1][m - 1], other[1][m - 1]), "tp", m)
        hidden = hidden + received.astype(jnp.float32)
    gain_part = picked(norm_gain.reshape(slots, group * columns), pair, 0)
    scaled = jnp.concatenate([(hidden * gain_part[:, None]).astype(jnp.bfloat16), kept_routes], axis=0)

    own = {0: scaled}
    pieces = [own] + [{} for m in range(1, t_count)]
    distance = z_count // 2
    while distance:
        held = list(own)
        if distance >= group:
            for m in range(1, t_count):
                pieces[m].update({d: swapped(own[d], "tp", m) for d in held if d not in pieces[m]})
        for d in held:
            own[d + distance] = swapped(own[d], "ep", distance)
        distance //= 2
    for m in range(1, t_count):
        pieces[m].update({d: swapped(own[d], "tp", m) for d in range(0, z_count, group) if d not in pieces[m]})
    late = {d: own[d] for d in own if d % group}
    late, pieces[1:] = lax.optimization_barrier((late, pieces[1:]))
    for m in range(1, t_count):
        pieces[m].update({d: swapped(late[d], "tp", m) for d in late})

    inverse_gain = 1.0 / norm_gain
    inverse_square = inverse_gain * inverse_gain
    coarse = inverse_square.astype(jnp.bfloat16)
    fine = (inverse_square - coarse.astype(jnp.float32)).astype(jnp.bfloat16)
    gain_table = jnp.concatenate([coarse[None], fine[None], jnp.zeros((14, D), jnp.bfloat16)], axis=0)

    total = 0.0
    for m in range(t_count):
        for r in range(slots):
            here = (pair == m) & ((pair ^ t) == r)
            total = total + jnp.where(here, pieces[m][group * r][:width].astype(jnp.float32), 0.0)
    total = total * lax.dynamic_slice_in_dim(inverse_gain, t * width, width, 0)[:, None]
    total = lax.optimization_barrier(total)

    after = None
    for p in range(group):
        part = [[pieces[m][group * r + p] for r in range(slots)] for m in range(t_count)]
        if p:
            part, after = lax.optimization_barrier((part, after))
        activated, share = activate(part, gain_table, experts_in, pair, t, chosen)
        after = activated
        activated = [activated] + [swapped(activated, "tp", m) for m in range(1, t_count)]
        for j, result in enumerate(combine(activated, share, experts_out, t, slots)):
            distance = group * j + p
            result = swapped(result, "ep", distance) if distance else result
            total = total + result.astype(jnp.float32)
    return total.astype(jnp.bfloat16).T


def solution(mesh):
    in_specs = (
        P(("groups", "ep", "sub"), "tp"),
        P(("groups", "ep", "sub"), "tp"),
        P(("groups", "ep", "sub"), "tp"),
        P("tp"),
        P("tp", "ep"),
        P(("groups", "ep", "sub"), None),
        P(),
        P(("ep", "sub"), None, None, "tp"),
        P(("ep", "sub"), None, "tp"),
        P(("groups", "ep", "sub"), None),
        P(("groups", "ep", "sub"), None),
    )
    out_specs = P(("groups", "ep", "sub"), "tp")
    return jax.shard_map(local, mesh=mesh, in_specs=in_specs, out_specs=out_specs, check_vma=False)
```

```python
import jax
import jax.numpy as jnp
from jax import lax
from jax.experimental import pallas as pl
from jax.experimental.pallas import tpu as pltpu
from jax.sharding import PartitionSpec as P

D = 2880
HD = 64
WIN = 128
TOP = 4
VMEM_BYTES = 16 * 1024 * 1024


def shifted(block, axis, distance):
    devices = range(lax.axis_size(axis))
    route = [(i - distance, i) for i in devices if i - distance in devices]
    return lax.ppermute(block, axis, route)


def swapped(block, axis, distance):
    return lax.ppermute(block, axis, [(i, i ^ distance) for i in range(lax.axis_size(axis))])


def picked(blocks, index, axis):
    return lax.dynamic_index_in_dim(blocks, index, axis, keepdims=False)


def in_vmem(count):
    return [pl.BlockSpec(memory_space=pltpu.VMEM)] * count


def in_smem():
    return pl.BlockSpec(memory_space=pltpu.SMEM)


def cost(flops, bytes_accessed):
    return pl.CostEstimate(flops=flops, bytes_accessed=bytes_accessed, transcendentals=0)


def dot(left, right):
    return jnp.dot(left, right, preferred_element_type=jnp.float32)


def aligned(size):
    return size % 16 == 0


def fetches(source, target, arrived, cuts):
    return [
        pltpu.make_async_copy(source.at[cut], target.at[cut], arrived.at[index]) for index, cut in enumerate(cuts)
    ]


def cuts_of(lead, size, count):
    count = count if size % (16 * count) == 0 else 1
    step = size // count
    return [(*at, pl.ds(i * step, step)) for at in lead for i in range(count)]


def params():
    return pltpu.CompilerParams(vmem_limit_bytes=VMEM_BYTES)


def attention_kernel(sink_ref, q_ref, earlier_ref, own_ref, out_ref):
    rows = q_ref.shape[0]
    kv_count = own_ref.shape[1] // (2 * HD)
    pairs = q_ref.shape[1] // (2 * HD * kv_count)
    key = lax.broadcasted_iota(jnp.int32, (rows, rows), 0)
    query = lax.broadcasted_iota(jnp.int32, (rows, rows), 1)
    before = key > query
    shut = before & (sink_ref[0] == 1.0)
    blank = jnp.zeros((2 * rows, HD), jnp.bfloat16)
    values = jnp.concatenate(
        [
            block.astype(jnp.float32).T.astype(jnp.bfloat16)
            for block in (earlier_ref[:, kv_count * HD :], own_ref[:, kv_count * HD :])
        ],
        axis=1,
    )
    for g in range(kv_count):
        head = slice(g * HD, (g + 1) * HD)
        keys = jnp.concatenate([earlier_ref[:, head], own_ref[:, head]], axis=0) * jnp.bfloat16(HD ** (-0.5))
        keys = jnp.concatenate(
            [jnp.concatenate([keys, blank], axis=1), jnp.concatenate([blank, keys], axis=1)], axis=0
        )
        for i in range(pairs):
            start = (g * pairs + i) * 2 * HD
            products = lax.dot_general(
                keys,
                q_ref[:, start : start + 2 * HD],
                (((1,), (1,)), ((), ())),
                preferred_element_type=jnp.float32,
            )
            weights = []
            for side in range(2):
                sink = sink_ref[1 + (g * pairs + i) * 2 + side]
                part = products[side * 2 * rows : (side + 1) * 2 * rows]
                scores = jnp.where(before, part[:rows], part[rows:])
                scores = jnp.where(shut, -1e30, scores)
                largest = jnp.maximum(jnp.max(scores, axis=0, keepdims=True), sink)
                numerator = jnp.exp(scores - largest)
                denominator = jnp.sum(numerator, axis=0, keepdims=True) + jnp.exp(sink - largest)
                numerator = numerator * (1.0 / denominator)
                weights.append(
                    jnp.concatenate(
                        [
                            jnp.where(before, numerator, 0.0).astype(jnp.bfloat16),
                            jnp.where(before, 0.0, numerator).astype(jnp.bfloat16),
                        ],
                        axis=0,
                    )
                )
            result = dot(values[head], jnp.concatenate(weights, axis=1)).astype(jnp.bfloat16)
            out_ref[start : start + HD, :] = result[:, :rows]
            out_ref[start + HD : start + 2 * HD, :] = result[:, rows:]


def attention(queries, earlier, paired, sinks):
    rows, width = queries.shape
    return pl.pallas_call(
        attention_kernel,
        out_shape=jax.ShapeDtypeStruct((width, rows), jnp.bfloat16),
        in_specs=[in_smem()] + in_vmem(3),
        out_specs=in_vmem(1)[0],
        compiler_params=params(),
        cost_estimate=cost(8 * rows * rows * width, 6 * rows * width),
        name="attention",
    )(sinks, queries, earlier, paired)


def flip(arrays, ahead):
    count = len(arrays)

    def kernel(*refs):
        for i in range(count):
            refs[count + len(ahead) + i][...] = refs[i][...].T

    return pl.pallas_call(
        kernel,
        out_shape=tuple(jax.ShapeDtypeStruct(a.shape[::-1], a.dtype) for a in arrays),
        in_specs=in_vmem(count + len(ahead)),
        out_specs=tuple(in_vmem(count)),
        compiler_params=params(),
        cost_estimate=cost(0, 4 * sum(a.size for a in arrays)),
        name="flip",
    )(*arrays, *ahead)


def project(attended, weights, t, s, t_count):
    slots = len(attended)
    rows = attended[0].shape[1]
    columns, depth = weights[0].shape
    shares = len(weights)
    width = shares * depth

    def kernel(place_ref, *refs):
        attended_refs = refs[:slots]
        weight_refs = refs[slots : slots + shares]
        kept_ref, sent_ref, total = refs[slots + shares :]
        t, s = place_ref[0], place_ref[1]
        result = 0.0
        for u in range(shares):
            span = pl.ds(pl.multiple_of((s ^ u) * depth, 128), depth)
            block = jnp.concatenate([ref[span, :] for ref in attended_refs], axis=1)
            result = result + dot(weight_refs[u][...], block)
        total[...] = result
        for m in range(t_count):
            block = total[:, pl.ds(pl.multiple_of((t ^ m) * rows, 128), rows)]
            if m == 0:
                kept_ref[...] = block
            else:
                sent_ref[m - 1] = block.astype(jnp.bfloat16)

    return pl.pallas_call(
        kernel,
        out_shape=(
            jax.ShapeDtypeStruct((columns, rows), jnp.float32),
            jax.ShapeDtypeStruct((t_count - 1, columns, rows), jnp.bfloat16),
        ),
        in_specs=[in_smem()] + in_vmem(slots + shares),
        out_specs=tuple(in_vmem(2)),
        scratch_shapes=[pltpu.VMEM((columns, slots * rows), jnp.float32)],
        compiler_params=params(),
        cost_estimate=cost(2 * slots * rows * width * columns, 2 * width * columns),
        name="project",
    )(jnp.stack([t, s]).astype(jnp.int32), *attended, *weights)


def activate(pieces, gain_table, weights, pair, t, chosen):
    slots = len(pieces)
    height, rows = pieces[0][0].shape
    depth = D // slots
    lanes = slots * rows
    experts = len(weights)
    units = weights[0].shape[1]
    cuts = cuts_of([(0,), (1,)], units, 3)

    def kernel(place_ref, *refs):
        piece_refs = refs[: slots * slots]
        table_ref = refs[slots * slots]
        weight_refs = refs[slots * slots + 1 : slots * slots + 1 + experts]
        out_ref, share_ref, rows_ref, stage_ref, routes_ref, held_ref, arrived = refs[
            slots * slots + 1 + experts :
        ]
        copies = [
            fetches(weight_refs[e], held_ref.at[e - 1], arrived.at[e - 1], cuts) for e in range(1, experts)
        ]
        for copy in sum(copies, []):
            copy.start()
        for m in range(slots):
            for r in range(slots):
                lane = pl.ds(pl.multiple_of((place_ref[1] ^ r ^ m) * rows, 128), rows)
                index = place_ref[0] ^ r
                piece_ref = piece_refs[m * slots + r]
                block = piece_ref[:depth, :]
                if aligned(depth):
                    rows_ref[pl.ds(pl.multiple_of(index * depth, 16), depth), lane] = block
                else:
                    stage_ref[index, :, lane] = block
                if not r:
                    routes_ref[:, lane] = piece_ref[depth:, :]
        if not aligned(depth):
            for index in range(slots):
                rows_ref[index * depth : (index + 1) * depth, :] = stage_ref[index]
        routes = routes_ref[...].astype(jnp.float32)
        scores = routes[TOP : 2 * TOP] * 256.0 + routes[2 * TOP : 3 * TOP]
        scores = scores / jnp.sum(scores, axis=0, keepdims=True)
        for e in range(experts):
            mine = routes[:TOP] == place_ref[2 + e].astype(jnp.float32)
            share_ref[e : e + 1, :] = jnp.sum(jnp.where(mine, scores, 0.0), axis=0, keepdims=True)
        plain = rows_ref[...].astype(jnp.float32)
        square = jnp.sum(dot(table_ref[...], (plain * plain).astype(jnp.bfloat16)), axis=0, keepdims=True)
        scale = lax.rsqrt(square / D + 1e-05)
        for e in range(experts):
            if e:
                for copy in copies[e - 1]:
                    copy.wait()
            weight_ref = held_ref.at[e - 1] if e else weight_refs[0]
            gate = dot(weight_ref[0], rows_ref[...]) * scale
            up = dot(weight_ref[1], rows_ref[...]) * scale
            out_ref[e] = ((up + 1.0) * gate * jax.nn.sigmoid(1.702 * gate)).astype(jnp.bfloat16)

    flat = [piece for part in pieces for piece in part]
    return pl.pallas_call(
        kernel,
        out_shape=(
            jax.ShapeDtypeStruct((experts, units, lanes), jnp.bfloat16),
            jax.ShapeDtypeStruct((experts, lanes), jnp.float32),
        ),
        in_specs=[in_smem()]
        + in_vmem(len(flat) + 2)
        + [pl.BlockSpec(memory_space=pl.ANY)] * (experts - 1),
        out_specs=tuple(in_vmem(2)),
        scratch_shapes=[
            pltpu.VMEM((D, lanes), jnp.bfloat16),
            pltpu.VMEM((1, 16, 128) if aligned(depth) else (slots, depth, lanes), jnp.bfloat16),
            pltpu.VMEM((height - depth, lanes), jnp.bfloat16),
            pltpu.VMEM((max(1, experts - 1), 2, units, D), jnp.bfloat16),
            pltpu.SemaphoreType.DMA((max(1, experts - 1), len(cuts))),
        ],
        compiler_params=params(),
        cost_estimate=cost(4 * experts * lanes * D * units, 4 * experts * D * units),
        name="activate",
    )(jnp.stack([pair, t] + chosen).astype(jnp.int32), *flat, gain_table, *weights)


def combine(activated, share, weights, t, slots):
    t_count = len(activated)
    experts, units, lanes = activated[0].shape
    width = weights[0].shape[0]
    rows = lanes // slots

    def kernel(t_ref, *refs):
        activated_refs = refs[:t_count]
        share_ref = refs[t_count]
        weight_refs = refs[t_count + 1 : t_count + 1 + experts]
        *out_refs, all_ref, stage_ref = refs[t_count + 1 + experts :]
        for u in range(t_count):
            index = t_ref[0] ^ u
            if aligned(units):
                all_ref[:, pl.ds(pl.multiple_of(index * units, 16), units), :] = activated_refs[u][...]
            else:
                stage_ref[index] = activated_refs[u][...]
        if not aligned(units):
            for index in range(t_count):
                all_ref[:, index * units : (index + 1) * units, :] = stage_ref[index]
        total = 0.0
        for e in range(experts):
            result = dot(weight_refs[e][...], all_ref[e]).astype(jnp.bfloat16).astype(jnp.float32)
            total = total + share_ref[e : e + 1, :] * result
        for j in range(slots):
            out_refs[j][...] = total[:, j * rows : (j + 1) * rows].astype(jnp.bfloat16)

    return pl.pallas_call(
        kernel,
        out_shape=tuple(jax.ShapeDtypeStruct((width, rows), jnp.bfloat16) for _ in range(slots)),
        in_specs=[in_smem()] + in_vmem(t_count + 1 + experts),
        out_specs=tuple(in_vmem(slots)),
        scratch_shapes=[
            pltpu.VMEM((experts, t_count * units, lanes), jnp.bfloat16),
            pltpu.VMEM((1, 1, 16, 128) if aligned(units) else (t_count, experts, units, lanes), jnp.bfloat16),
        ],
        compiler_params=params(),
        cost_estimate=cost(
            2 * experts * lanes * t_count * units * width, 2 * experts * t_count * units * width
        ),
        name="combine",
    )(t.reshape(1), *activated, share, *weights)


def local(
    queries,
    key_rows,
    value_rows,
    sink_logits,
    out_weight,
    residual,
    norm_gain,
    expert_in,
    expert_out,
    routes,
    route_scores,
):
    rows = queries.shape[0]
    z_count, t_count, s_count = lax.axis_size("ep"), lax.axis_size("tp"), lax.axis_size("sub")
    z, t, s = (lax.axis_index(name).astype(jnp.int32) for name in ("ep", "tp", "sub"))
    columns = out_weight.shape[1]
    width = expert_out.shape[2]
    slots = t_count
    group = z_count // slots
    pair = z // group

    paired = jnp.concatenate([key_rows, value_rows], axis=1)
    earlier = shifted(paired, ("ep", "sub"), 1)
    out_weight = out_weight.T
    depth = out_weight.shape[1] // s_count
    near = lax.dynamic_slice_in_dim(out_weight, s * depth, depth, 1)
    scores = route_scores.T
    numbers = [routes.T, scores // 256, scores % 256, jnp.zeros((16 - 3 * TOP, rows), jnp.int32)]
    residual = picked(residual.T.reshape(slots, group * columns, rows), pair ^ t, 0)
    residual = jnp.concatenate([residual, jnp.concatenate(numbers, axis=0).astype(jnp.bfloat16)], axis=0)
    first = lax.axis_index(("ep", "sub")) == 0
    sinks = jnp.concatenate([first.astype(jnp.float32).reshape(1), sink_logits])
    earlier, near, residual, expert_in, expert_out = lax.optimization_barrier(
        (earlier, near, residual, expert_in, expert_out)
    )

    near = swapped(near, "ep", 1)

    route = [
        (i * t_count + k, (i ^ (group * k)) * t_count + k) for i in range(z_count) for k in range(t_count)
    ]
    residual = lax.ppermute(residual, ("ep", "tp"), route)

    expert_in = expert_in[0].transpose(0, 2, 1)
    expert_out = expert_out[0]
    experts_in = [expert_in] + [swapped(expert_in, "sub", e) for e in range(1, s_count)]
    experts_out = [expert_out] + [swapped(expert_out, "sub", e) for e in range(1, s_count)]
    chosen = [z * s_count + (s ^ e) for e in range(s_count)]

    attended = attention(queries, earlier, paired, sinks)
    attended, residual = lax.optimization_barrier((attended, residual))
    gathered = [attended] + [swapped(attended, "ep", group * j) for j in range(1, slots)]
    experts_out, _ = lax.optimization_barrier((experts_out, attended))
    experts_out = flip(experts_out, [out_weight, expert_in])

    gathered, near, experts_out = lax.optimization_barrier((gathered, near, experts_out))
    near_weights = [near] + [swapped(near, "sub", u) for u in range(1, s_count)]
    mine = project(gathered, [out_weight], t, s * 0, t_count)
    other = project(gathered, near_weights, t, s, t_count)
    first_member = z % group == 0

    def ordered(a, b):
        return jnp.concatenate([jnp.where(first_member, a, b), jnp.where(first_member, b, a)], axis=0)

    hidden = ordered(mine[0], other[0]) + residual[: group * columns].astype(jnp.float32)
    for m in range(1, t_count):
        received = swapped(ordered(mine[1][m - 1], other[1][m - 1]), "tp", m)
        hidden = hidden + received.astype(jnp.float32)
    gain_part = picked(norm_gain.reshape(slots, group * columns), pair, 0)
    scaled = jnp.concatenate([(hidden * gain_part[:, None]).astype(jnp.bfloat16), residual[group * columns :]], axis=0)

    own = {0: scaled}
    pieces = [own] + [{} for m in range(1, t_count)]
    distance = z_count // 2
    while distance:
        held = list(own)
        if distance >= group:
            for m in range(1, t_count):
                pieces[m].update({d: swapped(own[d], "tp", m) for d in held if d not in pieces[m]})
        for d in held:
            own[d + distance] = swapped(own[d], "ep", distance)
        distance //= 2
    for m in range(1, t_count):
        pieces[m].update({d: swapped(own[d], "tp", m) for d in range(0, z_count, group) if d not in pieces[m]})
    late = {d: own[d] for d in own if d % group}
    late, pieces[1:] = lax.optimization_barrier((late, pieces[1:]))
    for m in range(1, t_count):
        pieces[m].update({d: swapped(late[d], "tp", m) for d in late})

    inverse_gain = 1.0 / norm_gain
    inverse_square = inverse_gain * inverse_gain
    coarse = inverse_square.astype(jnp.bfloat16)
    fine = (inverse_square - coarse.astype(jnp.float32)).astype(jnp.bfloat16)
    gain_table = jnp.concatenate([coarse[None], fine[None], jnp.zeros((14, D), jnp.bfloat16)], axis=0)

    total = 0.0
    for m in range(t_count):
        for r in range(slots):
            here = (pair == m) & ((pair ^ t) == r)
            total = total + jnp.where(here, pieces[m][group * r][:width].astype(jnp.float32), 0.0)
    total = total * lax.dynamic_slice_in_dim(inverse_gain, t * width, width, 0)[:, None]
    total = lax.optimization_barrier(total)

    after = None
    for p in range(group):
        part = [[pieces[m][group * r + p] for r in range(slots)] for m in range(t_count)]
        if p:
            part, after = lax.optimization_barrier((part, after))
        activated, share = activate(part, gain_table, experts_in, pair, t, chosen)
        after = activated
        activated = [activated] + [swapped(activated, "tp", m) for m in range(1, t_count)]
        for j, result in enumerate(combine(activated, share, experts_out, t, slots)):
            distance = group * j + p
            result = swapped(result, "ep", distance) if distance else result
            total = total + result.astype(jnp.float32)
    return total.astype(jnp.bfloat16).T


def solution(mesh):
    in_specs = (
        P(("groups", "ep", "sub"), "tp"),
        P(("groups", "ep", "sub"), "tp"),
        P(("groups", "ep", "sub"), "tp"),
        P("tp"),
        P("tp", "ep"),
        P(("groups", "ep", "sub"), None),
        P(),
        P(("ep", "sub"), None, None, "tp"),
        P(("ep", "sub"), None, "tp"),
        P(("groups", "ep", "sub"), None),
        P(("groups", "ep", "sub"), None),
    )
    out_specs = P(("groups", "ep", "sub"), "tp")
    return jax.shard_map(local, mesh=mesh, in_specs=in_specs, out_specs=out_specs, check_vma=False)
```

```python
import jax
import jax.numpy as jnp
from jax import lax
from jax.experimental import pallas as pl
from jax.experimental.pallas import tpu as pltpu
from jax.sharding import PartitionSpec as P

D = 2880
HD = 64
WIN = 128
TOP = 4
VMEM_BYTES = 16 * 1024 * 1024


def shifted(block, axis, distance):
    devices = range(lax.axis_size(axis))
    route = [(i - distance, i) for i in devices if i - distance in devices]
    return lax.ppermute(block, axis, route)


def swapped(block, axis, distance):
    return lax.ppermute(block, axis, [(i, i ^ distance) for i in range(lax.axis_size(axis))])


def picked(blocks, index, axis):
    return lax.dynamic_index_in_dim(blocks, index, axis, keepdims=False)


def in_vmem(count):
    return [pl.BlockSpec(memory_space=pltpu.VMEM)] * count


def in_smem():
    return pl.BlockSpec(memory_space=pltpu.SMEM)


def cost(flops, bytes_accessed):
    return pl.CostEstimate(flops=flops, bytes_accessed=bytes_accessed, transcendentals=0)


def dot(left, right):
    return jnp.dot(left, right, preferred_element_type=jnp.float32)


def aligned(size):
    return size % 16 == 0


def fetches(source, target, arrived, cuts):
    return [
        pltpu.make_async_copy(source.at[cut], target.at[cut], arrived.at[index]) for index, cut in enumerate(cuts)
    ]


def cuts_of(lead, size, count):
    count = count if size % (16 * count) == 0 else 1
    step = size // count
    return [(*at, pl.ds(i * step, step)) for at in lead for i in range(count)]


def params():
    return pltpu.CompilerParams(vmem_limit_bytes=VMEM_BYTES)


def attention_kernel(place_ref, sink_ref, q_ref, earlier_ref, k_ref, v_ref, routes_ref, scores_ref, out_ref):
    width = q_ref.shape[1]
    numbers = [routes_ref[...], scores_ref[...] // 256, scores_ref[...] % 256]
    numbers.append(jnp.zeros((out_ref.shape[0] - width - 3 * TOP, q_ref.shape[0]), jnp.int32))
    out_ref[width:, :] = jnp.concatenate(numbers, axis=0).astype(jnp.float32).astype(jnp.bfloat16)
    rows = q_ref.shape[0]
    kv_count = k_ref.shape[1] // HD
    pairs = q_ref.shape[1] // (2 * HD * kv_count)
    key = lax.broadcasted_iota(jnp.int32, (rows, rows), 0)
    query = lax.broadcasted_iota(jnp.int32, (rows, rows), 1)
    before = key > query
    shut = before & (place_ref[0] == 1)
    blank = jnp.zeros((2 * rows, HD), jnp.bfloat16)
    values = jnp.concatenate(
        [
            block.astype(jnp.float32).T.astype(jnp.bfloat16)
            for block in (earlier_ref[:, kv_count * HD :], v_ref[...])
        ],
        axis=1,
    )
    for g in range(kv_count):
        head = slice(g * HD, (g + 1) * HD)
        keys = jnp.concatenate([earlier_ref[:, head], k_ref[:, head]], axis=0) * jnp.bfloat16(HD ** (-0.5))
        keys = jnp.concatenate(
            [jnp.concatenate([keys, blank], axis=1), jnp.concatenate([blank, keys], axis=1)], axis=0
        )
        for i in range(pairs):
            start = (g * pairs + i) * 2 * HD
            products = lax.dot_general(
                keys,
                q_ref[:, start : start + 2 * HD],
                (((1,), (1,)), ((), ())),
                preferred_element_type=jnp.float32,
            )
            weights = []
            for side in range(2):
                sink = sink_ref[(g * pairs + i) * 2 + side]
                part = products[side * 2 * rows : (side + 1) * 2 * rows]
                scores = jnp.where(before, part[:rows], part[rows:])
                scores = jnp.where(shut, -1e30, scores)
                largest = jnp.maximum(jnp.max(scores, axis=0, keepdims=True), sink)
                numerator = jnp.exp(scores - largest)
                denominator = jnp.sum(numerator, axis=0, keepdims=True) + jnp.exp(sink - largest)
                numerator = numerator * (1.0 / denominator)
                weights.append(
                    jnp.concatenate(
                        [
                            jnp.where(before, numerator, 0.0).astype(jnp.bfloat16),
                            jnp.where(before, 0.0, numerator).astype(jnp.bfloat16),
                        ],
                        axis=0,
                    )
                )
            result = dot(values[head], jnp.concatenate(weights, axis=1)).astype(jnp.bfloat16)
            out_ref[start : start + HD, :] = result[:, :rows]
            out_ref[start + HD : start + 2 * HD, :] = result[:, rows:]


def attention(queries, earlier, key_rows, value_rows, sink_logits, first, routes, scores):
    rows, width = queries.shape
    return pl.pallas_call(
        attention_kernel,
        out_shape=jax.ShapeDtypeStruct((width + 16, rows), jnp.bfloat16),
        in_specs=[in_smem(), in_smem()] + in_vmem(6),
        out_specs=in_vmem(1)[0],
        compiler_params=params(),
        cost_estimate=cost(8 * rows * rows * width, 6 * rows * width),
        name="attention",
    )(first, sink_logits, queries, earlier, key_rows, value_rows, routes, scores)


def flip(arrays):
    def kernel(*refs):
        for i in range(len(arrays)):
            refs[len(arrays) + i][...] = refs[i][...].T

    return pl.pallas_call(
        kernel,
        out_shape=tuple(jax.ShapeDtypeStruct(a.shape[::-1], a.dtype) for a in arrays),
        in_specs=in_vmem(len(arrays)),
        out_specs=tuple(in_vmem(len(arrays))),
        compiler_params=params(),
        cost_estimate=cost(0, 4 * sum(a.size for a in arrays)),
        name="flip",
    )(*arrays)


def project(attended, weights, t, s, t_count):
    slots = len(attended)
    rows = attended[0].shape[1]
    columns, depth = weights[0].shape
    shares = len(weights)
    width = shares * depth

    def kernel(place_ref, *refs):
        attended_refs = refs[:slots]
        weight_refs = refs[slots : slots + shares]
        kept_ref, sent_ref, total = refs[slots + shares :]
        t, s = place_ref[0], place_ref[1]
        result = 0.0
        for u in range(shares):
            span = pl.ds(pl.multiple_of((s ^ u) * depth, 128), depth)
            block = jnp.concatenate([ref[span, :] for ref in attended_refs], axis=1)
            result = result + dot(weight_refs[u][...], block)
        total[...] = result
        for m in range(t_count):
            block = total[:, pl.ds(pl.multiple_of((t ^ m) * rows, 128), rows)]
            if m == 0:
                kept_ref[...] = block
            else:
                sent_ref[m - 1] = block.astype(jnp.bfloat16)

    return pl.pallas_call(
        kernel,
        out_shape=(
            jax.ShapeDtypeStruct((columns, rows), jnp.float32),
            jax.ShapeDtypeStruct((t_count - 1, columns, rows), jnp.bfloat16),
        ),
        in_specs=[in_smem()] + in_vmem(slots + shares),
        out_specs=tuple(in_vmem(2)),
        scratch_shapes=[pltpu.VMEM((columns, slots * rows), jnp.float32)],
        compiler_params=params(),
        cost_estimate=cost(2 * slots * rows * width * columns, 2 * width * columns),
        name="project",
    )(jnp.stack([t, s]).astype(jnp.int32), *attended, *weights)


def activate(pieces, gain_table, weights, pair, t, chosen, ahead):
    slots = len(pieces)
    height, rows = pieces[0][0].shape
    depth = D // slots
    lanes = slots * rows
    experts = len(weights)
    units = weights[0].shape[1]
    cuts = cuts_of([(0,), (1,)], units, 3)

    def kernel(place_ref, *refs):
        piece_refs = refs[: slots * slots]
        table_ref = refs[slots * slots]
        weight_refs = refs[slots * slots + 1 : slots * slots + 1 + experts]
        out_ref, share_ref, rows_ref, stage_ref, routes_ref, held_ref, arrived = refs[
            slots * slots + 1 + experts + len(ahead) :
        ]
        copies = [
            fetches(weight_refs[e], held_ref.at[e - 1], arrived.at[e - 1], cuts) for e in range(1, experts)
        ]
        for copy in sum(copies, []):
            copy.start()
        for m in range(slots):
            for r in range(slots):
                lane = pl.ds(pl.multiple_of((place_ref[1] ^ r ^ m) * rows, 128), rows)
                index = place_ref[0] ^ r
                piece_ref = piece_refs[m * slots + r]
                block = piece_ref[:depth, :]
                if aligned(depth):
                    rows_ref[pl.ds(pl.multiple_of(index * depth, 16), depth), lane] = block
                else:
                    stage_ref[index, :, lane] = block
                if not r:
                    routes_ref[:, lane] = piece_ref[depth:, :]
        if not aligned(depth):
            for index in range(slots):
                rows_ref[index * depth : (index + 1) * depth, :] = stage_ref[index]
        routes = routes_ref[...].astype(jnp.float32)
        scores = routes[TOP : 2 * TOP] * 256.0 + routes[2 * TOP : 3 * TOP]
        scores = scores / jnp.sum(scores, axis=0, keepdims=True)
        for e in range(experts):
            mine = routes[:TOP] == place_ref[2 + e].astype(jnp.float32)
            share_ref[e : e + 1, :] = jnp.sum(jnp.where(mine, scores, 0.0), axis=0, keepdims=True)
        plain = rows_ref[...].astype(jnp.float32)
        square = jnp.sum(dot(table_ref[...], (plain * plain).astype(jnp.bfloat16)), axis=0, keepdims=True)
        scale = lax.rsqrt(square / D + 1e-05)
        for e in range(experts):
            if e:
                for copy in copies[e - 1]:
                    copy.wait()
            weight_ref = held_ref.at[e - 1] if e else weight_refs[0]
            gate = dot(weight_ref[0], rows_ref[...]) * scale
            up = dot(weight_ref[1], rows_ref[...]) * scale
            out_ref[e] = ((up + 1.0) * gate * jax.nn.sigmoid(1.702 * gate)).astype(jnp.bfloat16)

    flat = [piece for part in pieces for piece in part]
    return pl.pallas_call(
        kernel,
        out_shape=(
            jax.ShapeDtypeStruct((experts, units, lanes), jnp.bfloat16),
            jax.ShapeDtypeStruct((experts, lanes), jnp.float32),
        ),
        in_specs=[in_smem()]
        + in_vmem(len(flat) + 2)
        + [pl.BlockSpec(memory_space=pl.ANY)] * (experts - 1)
        + in_vmem(len(ahead)),
        out_specs=tuple(in_vmem(2)),
        scratch_shapes=[
            pltpu.VMEM((D, lanes), jnp.bfloat16),
            pltpu.VMEM((1, 16, 128) if aligned(depth) else (slots, depth, lanes), jnp.bfloat16),
            pltpu.VMEM((height - depth, lanes), jnp.bfloat16),
            pltpu.VMEM((max(1, experts - 1), 2, units, D), jnp.bfloat16),
            pltpu.SemaphoreType.DMA((max(1, experts - 1), len(cuts))),
        ],
        compiler_params=params(),
        cost_estimate=cost(4 * experts * lanes * D * units, 4 * experts * D * units),
        name="activate",
    )(jnp.stack([pair, t] + chosen).astype(jnp.int32), *flat, gain_table, *weights, *ahead)


def ready(table, ahead):
    def kernel(table_ref, ahead_ref, out_ref):
        out_ref[...] = table_ref[...]

    return pl.pallas_call(
        kernel,
        out_shape=jax.ShapeDtypeStruct(table.shape, table.dtype),
        in_specs=in_vmem(2),
        out_specs=in_vmem(1)[0],
        compiler_params=params(),
        cost_estimate=cost(0, 4 * table.size),
        name="ready",
    )(table, ahead)


def combine(activated, share, weights, t, slots):
    t_count = len(activated)
    experts, units, lanes = activated[0].shape
    width = weights[0].shape[0]
    rows = lanes // slots

    def kernel(t_ref, *refs):
        activated_refs = refs[:t_count]
        share_ref = refs[t_count]
        weight_refs = refs[t_count + 1 : t_count + 1 + experts]
        *out_refs, all_ref, stage_ref = refs[t_count + 1 + experts :]
        for u in range(t_count):
            index = t_ref[0] ^ u
            if aligned(units):
                all_ref[:, pl.ds(pl.multiple_of(index * units, 16), units), :] = activated_refs[u][...]
            else:
                stage_ref[index] = activated_refs[u][...]
        if not aligned(units):
            for index in range(t_count):
                all_ref[:, index * units : (index + 1) * units, :] = stage_ref[index]
        total = 0.0
        for e in range(experts):
            result = dot(weight_refs[e][...], all_ref[e]).astype(jnp.bfloat16).astype(jnp.float32)
            total = total + share_ref[e : e + 1, :] * result
        for j in range(slots):
            out_refs[j][...] = total[:, j * rows : (j + 1) * rows].astype(jnp.bfloat16)

    return pl.pallas_call(
        kernel,
        out_shape=tuple(jax.ShapeDtypeStruct((width, rows), jnp.bfloat16) for _ in range(slots)),
        in_specs=[in_smem()] + in_vmem(t_count + 1 + experts),
        out_specs=tuple(in_vmem(slots)),
        scratch_shapes=[
            pltpu.VMEM((experts, t_count * units, lanes), jnp.bfloat16),
            pltpu.VMEM((1, 1, 16, 128) if aligned(units) else (t_count, experts, units, lanes), jnp.bfloat16),
        ],
        compiler_params=params(),
        cost_estimate=cost(
            2 * experts * lanes * t_count * units * width, 2 * experts * t_count * units * width
        ),
        name="combine",
    )(t.reshape(1), *activated, share, *weights)


def local(
    queries,
    key_rows,
    value_rows,
    sink_logits,
    out_weight,
    residual,
    norm_gain,
    expert_in,
    expert_out,
    routes,
    route_scores,
):
    rows = queries.shape[0]
    z_count, t_count, s_count = lax.axis_size("ep"), lax.axis_size("tp"), lax.axis_size("sub")
    z, t, s = (lax.axis_index(name).astype(jnp.int32) for name in ("ep", "tp", "sub"))
    columns = out_weight.shape[1]
    width = expert_out.shape[2]
    slots = t_count
    group = z_count // slots
    pair = z // group

    paired = jnp.concatenate([key_rows, value_rows], axis=1)
    earlier = shifted(paired, ("ep", "sub"), 1)
    out_weight = out_weight.T
    depth = out_weight.shape[1] // s_count
    near = lax.dynamic_slice_in_dim(out_weight, s * depth, depth, 1)
    residual = picked(residual.T.reshape(slots, group * columns, rows), pair ^ t, 0)
    earlier, near, residual, expert_in, expert_out = lax.optimization_barrier(
        (earlier, near, residual, expert_in, expert_out)
    )

    near = swapped(near, "ep", 1)

    route = [
        (i * t_count + k, (i ^ (group * k)) * t_count + k) for i in range(z_count) for k in range(t_count)
    ]
    residual = lax.ppermute(residual, ("ep", "tp"), route)

    expert_in = expert_in[0].transpose(0, 2, 1)
    expert_out = expert_out[0]
    experts_in = [expert_in] + [swapped(expert_in, "sub", e) for e in range(1, s_count)]
    experts_out = [expert_out] + [swapped(expert_out, "sub", e) for e in range(1, s_count)]
    chosen = [z * s_count + (s ^ e) for e in range(s_count)]

    first = (lax.axis_index(("ep", "sub")) == 0).astype(jnp.int32).reshape(1)
    attended = attention(
        queries, earlier, key_rows, value_rows, sink_logits, first, routes.T, route_scores.T
    )
    gathered = [attended] + [swapped(attended, "ep", group * j) for j in range(1, slots)]
    experts_out, _ = lax.optimization_barrier((experts_out, attended))
    experts_out = flip(experts_out)

    gathered, near, residual, experts_out = lax.optimization_barrier((gathered, near, residual, experts_out))
    near_weights = [near] + [swapped(near, "sub", u) for u in range(1, s_count)]
    mine = project(gathered, [out_weight], t, s * 0, t_count)
    other = project(gathered, near_weights, t, s, t_count)
    first_member = z % group == 0

    def ordered(a, b):
        return jnp.concatenate([jnp.where(first_member, a, b), jnp.where(first_member, b, a)], axis=0)

    kept_routes = gathered[0][queries.shape[1] :]
    for j in range(1, slots):
        kept_routes = jnp.where(t == j, gathered[j][queries.shape[1] :], kept_routes)
    hidden = ordered(mine[0], other[0]) + residual.astype(jnp.float32)
    for m in range(1, t_count):
        received = swapped(ordered(mine[1][m - 1], other[1][m - 1]), "tp", m)
        hidden = hidden + received.astype(jnp.float32)
    gain_part = picked(norm_gain.reshape(slots, group * columns), pair, 0)
    scaled = jnp.concatenate([(hidden * gain_part[:, None]).astype(jnp.bfloat16), kept_routes], axis=0)

    own = {0: scaled}
    pieces = [own] + [{} for m in range(1, t_count)]
    distance = z_count // 2
    while distance:
        held = list(own)
        if distance >= group:
            for m in range(1, t_count):
                pieces[m].update({d: swapped(own[d], "tp", m) for d in held if d not in pieces[m]})
        for d in held:
            own[d + distance] = swapped(own[d], "ep", distance)
        distance //= 2
    for m in range(1, t_count):
        pieces[m].update({d: swapped(own[d], "tp", m) for d in range(0, z_count, group) if d not in pieces[m]})
    late = {d: own[d] for d in own if d % group}
    late, pieces[1:] = lax.optimization_barrier((late, pieces[1:]))
    for m in range(1, t_count):
        pieces[m].update({d: swapped(late[d], "tp", m) for d in late})

    inverse_gain = 1.0 / norm_gain
    inverse_square = inverse_gain * inverse_gain
    coarse = inverse_square.astype(jnp.bfloat16)
    fine = (inverse_square - coarse.astype(jnp.float32)).astype(jnp.bfloat16)
    gain_table = jnp.concatenate([coarse[None], fine[None], jnp.zeros((14, D), jnp.bfloat16)], axis=0)

    gain_table, _ = lax.optimization_barrier((gain_table, scaled))
    gain_table = ready(gain_table, expert_in)

    total = 0.0
    for m in range(t_count):
        for r in range(slots):
            here = (pair == m) & ((pair ^ t) == r)
            total = total + jnp.where(here, pieces[m][group * r][:width].astype(jnp.float32), 0.0)
    total = total * lax.dynamic_slice_in_dim(inverse_gain, t * width, width, 0)[:, None]
    total = lax.optimization_barrier(total)

    after = None
    for p in range(group):
        part = [[pieces[m][group * r + p] for r in range(slots)] for m in range(t_count)]
        if p:
            part, after = lax.optimization_barrier((part, after))
        activated, share = activate(
            part, gain_table, experts_in, pair, t, chosen, experts_out if p == group - 1 else []
        )
        after = activated
        activated = [activated] + [swapped(activated, "tp", m) for m in range(1, t_count)]
        for j, result in enumerate(combine(activated, share, experts_out, t, slots)):
            distance = group * j + p
            result = swapped(result, "ep", distance) if distance else result
            total = total + result.astype(jnp.float32)
    return total.astype(jnp.bfloat16).T


def solution(mesh):
    in_specs = (
        P(("groups", "ep", "sub"), "tp"),
        P(("groups", "ep", "sub"), "tp"),
        P(("groups", "ep", "sub"), "tp"),
        P("tp"),
        P("tp", "ep"),
        P(("groups", "ep", "sub"), None),
        P(),
        P(("ep", "sub"), None, None, "tp"),
        P(("ep", "sub"), None, "tp"),
        P(("groups", "ep", "sub"), None),
        P(("groups", "ep", "sub"), None),
    )
    out_specs = P(("groups", "ep", "sub"), "tp")
    return jax.shard_map(local, mesh=mesh, in_specs=in_specs, out_specs=out_specs, check_vma=False)
```

```python
import jax
import jax.numpy as jnp
from jax import lax
from jax.experimental import pallas as pl
from jax.experimental.pallas import tpu as pltpu
from jax.sharding import PartitionSpec as P

D = 2880
HD = 64
WIN = 128
TOP = 4
MIB = 1024 * 1024


def shifted(block, axis, distance):
    devices = range(lax.axis_size(axis))
    route = [(i - distance, i) for i in devices if i - distance in devices]
    return lax.ppermute(block, axis, route)


def swapped(block, axis, distance):
    return lax.ppermute(block, axis, [(i, i ^ distance) for i in range(lax.axis_size(axis))])


def picked(blocks, index, axis):
    return lax.dynamic_index_in_dim(blocks, index, axis, keepdims=False)


def in_vmem(count):
    return [pl.BlockSpec(memory_space=pltpu.VMEM)] * count


def in_smem():
    return pl.BlockSpec(memory_space=pltpu.SMEM)


def cost(flops, bytes_accessed):
    return pl.CostEstimate(flops=flops, bytes_accessed=bytes_accessed, transcendentals=0)


def dot(left, right):
    return jnp.dot(left, right, preferred_element_type=jnp.float32)


def aligned(size):
    return size % 16 == 0


def fetches(source, target, arrived, cuts):
    return [
        pltpu.make_async_copy(source.at[cut], target.at[cut], arrived.at[index]) for index, cut in enumerate(cuts)
    ]


def cuts_of(lead, size, count):
    count = count if size % (16 * count) == 0 else 1
    step = size // count
    return [(*at, pl.ds(i * step, step)) for at in lead for i in range(count)]


def params(mebibytes):
    return pltpu.CompilerParams(vmem_limit_bytes=int(mebibytes * MIB))


def attention_kernel(
    place_ref, sink_ref, q_ref, earlier_ref, k_ref, v_ref, routes_ref, scores_ref, residual_ref, out_ref
):
    width = q_ref.shape[1]
    numbers = [routes_ref[...], scores_ref[...] // 256, scores_ref[...] % 256]
    numbers.append(jnp.zeros((16 - 3 * TOP, q_ref.shape[0]), jnp.int32))
    out_ref[width : width + 16, :] = jnp.concatenate(numbers, axis=0).astype(jnp.float32).astype(jnp.bfloat16)
    out_ref[width + 16 :, :] = residual_ref[place_ref[1]]
    rows = q_ref.shape[0]
    kv_count = k_ref.shape[1] // HD
    pairs = q_ref.shape[1] // (2 * HD * kv_count)
    key = lax.broadcasted_iota(jnp.int32, (rows, rows), 0)
    query = lax.broadcasted_iota(jnp.int32, (rows, rows), 1)
    before = key > query
    shut = before & (place_ref[0] == 1)
    blank = jnp.zeros((2 * rows, HD), jnp.bfloat16)
    values = jnp.concatenate(
        [
            block.astype(jnp.float32).T.astype(jnp.bfloat16)
            for block in (earlier_ref[:, kv_count * HD :], v_ref[...])
        ],
        axis=1,
    )
    for g in range(kv_count):
        head = slice(g * HD, (g + 1) * HD)
        keys = jnp.concatenate([earlier_ref[:, head], k_ref[:, head]], axis=0) * jnp.bfloat16(HD ** (-0.5))
        keys = jnp.concatenate(
            [jnp.concatenate([keys, blank], axis=1), jnp.concatenate([blank, keys], axis=1)], axis=0
        )
        for i in range(pairs):
            start = (g * pairs + i) * 2 * HD
            products = lax.dot_general(
                keys,
                q_ref[:, start : start + 2 * HD],
                (((1,), (1,)), ((), ())),
                preferred_element_type=jnp.float32,
            )
            weights = []
            for side in range(2):
                sink = sink_ref[(g * pairs + i) * 2 + side]
                part = products[side * 2 * rows : (side + 1) * 2 * rows]
                scores = jnp.where(before, part[:rows], part[rows:])
                scores = jnp.where(shut, -1e30, scores)
                largest = jnp.maximum(jnp.max(scores, axis=0, keepdims=True), sink)
                numerator = jnp.exp(scores - largest)
                denominator = jnp.sum(numerator, axis=0, keepdims=True) + jnp.exp(sink - largest)
                numerator = numerator * (1.0 / denominator)
                weights.append(
                    jnp.concatenate(
                        [
                            jnp.where(before, numerator, 0.0).astype(jnp.bfloat16),
                            jnp.where(before, 0.0, numerator).astype(jnp.bfloat16),
                        ],
                        axis=0,
                    )
                )
            result = dot(values[head], jnp.concatenate(weights, axis=1)).astype(jnp.bfloat16)
            out_ref[start : start + HD, :] = result[:, :rows]
            out_ref[start + HD : start + 2 * HD, :] = result[:, rows:]


def attention(queries, earlier, key_rows, value_rows, sink_logits, place, routes, scores, residual):
    rows, width = queries.shape
    return pl.pallas_call(
        attention_kernel,
        out_shape=jax.ShapeDtypeStruct((width + 16 + residual.shape[1], rows), jnp.bfloat16),
        in_specs=[in_smem(), in_smem()] + in_vmem(7),
        out_specs=in_vmem(1)[0],
        compiler_params=params(8),
        cost_estimate=cost(8 * rows * rows * width, 6 * rows * width),
        name="attention",
    )(place, sink_logits, queries, earlier, key_rows, value_rows, routes, scores, residual)


def flip(arrays):
    def kernel(*refs):
        for i in range(len(arrays)):
            refs[len(arrays) + i][...] = refs[i][...].T

    return pl.pallas_call(
        kernel,
        out_shape=tuple(jax.ShapeDtypeStruct(a.shape[::-1], a.dtype) for a in arrays),
        in_specs=in_vmem(len(arrays)),
        out_specs=tuple(in_vmem(len(arrays))),
        compiler_params=params(12),
        cost_estimate=cost(0, 4 * sum(a.size for a in arrays)),
        name="flip",
    )(*arrays)


def project(attended, weights, residual, has_share, t, s, t_count):
    slots = len(attended)
    rows = attended[0].shape[1]
    columns, depth = weights[0].shape
    shares = len(weights)
    width = shares * depth

    def kernel(place_ref, *refs):
        attended_refs = refs[:slots]
        weight_refs = refs[slots : slots + shares]
        residual_ref, kept_ref, sent_ref, total = refs[slots + shares :]
        t, s = place_ref[0], place_ref[1]
        result = 0.0
        for u in range(shares):
            span = pl.ds(pl.multiple_of((s ^ u) * depth, 128), depth)
            block = jnp.concatenate([ref[span, :] for ref in attended_refs], axis=1)
            result = result + dot(weight_refs[u][...], block)
        total[...] = result

        @pl.when(place_ref[2] == 1)
        def _():
            for j in range(slots):
                share = attended_refs[j][width + 16 :, :] if j else residual_ref[...]
                if share.shape[0] == columns:
                    total[:, j * rows : (j + 1) * rows] += share.astype(jnp.float32)

        for m in range(t_count):
            block = total[:, pl.ds(pl.multiple_of((t ^ m) * rows, 128), rows)]
            if m == 0:
                kept_ref[...] = block
            else:
                sent_ref[m - 1] = block.astype(jnp.bfloat16)

    return pl.pallas_call(
        kernel,
        out_shape=(
            jax.ShapeDtypeStruct((columns, rows), jnp.float32),
            jax.ShapeDtypeStruct((t_count - 1, columns, rows), jnp.bfloat16),
        ),
        in_specs=[in_smem()] + in_vmem(slots + shares + 1),
        out_specs=tuple(in_vmem(2)),
        scratch_shapes=[pltpu.VMEM((columns, slots * rows), jnp.float32)],
        compiler_params=params(8),
        cost_estimate=cost(2 * slots * rows * width * columns, 2 * width * columns),
        name="project",
    )(jnp.stack([t, s, has_share]).astype(jnp.int32), *attended, *weights, residual)


def activate(pieces, gain_table, weights, pair, t, chosen):
    slots = len(pieces)
    height, rows = pieces[0][0].shape
    depth = D // slots
    lanes = slots * rows
    experts = len(weights)
    units = weights[0].shape[1]
    cuts = cuts_of([(0,), (1,)], units, 3)

    def kernel(place_ref, *refs):
        piece_refs = refs[: slots * slots]
        table_ref = refs[slots * slots]
        weight_refs = refs[slots * slots + 1 : slots * slots + 1 + experts]
        out_ref, share_ref, rows_ref, stage_ref, routes_ref, held_ref, arrived = refs[
            slots * slots + 1 + experts :
        ]
        copies = [
            fetches(weight_refs[e], held_ref.at[e - 1], arrived.at[e - 1], cuts) for e in range(1, experts)
        ]
        for copy in sum(copies, []):
            copy.start()
        for m in range(slots):
            for r in range(slots):
                lane = pl.ds(pl.multiple_of((place_ref[1] ^ r ^ m) * rows, 128), rows)
                index = place_ref[0] ^ r
                piece_ref = piece_refs[m * slots + r]
                block = piece_ref[:depth, :]
                if aligned(depth):
                    rows_ref[pl.ds(pl.multiple_of(index * depth, 16), depth), lane] = block
                else:
                    stage_ref[index, :, lane] = block
                if not r:
                    routes_ref[:, lane] = piece_ref[depth:, :]
        if not aligned(depth):
            for index in range(slots):
                rows_ref[index * depth : (index + 1) * depth, :] = stage_ref[index]
        routes = routes_ref[...].astype(jnp.float32)
        scores = routes[TOP : 2 * TOP] * 256.0 + routes[2 * TOP : 3 * TOP]
        scores = scores / jnp.sum(scores, axis=0, keepdims=True)
        for e in range(experts):
            mine = routes[:TOP] == place_ref[2 + e].astype(jnp.float32)
            share_ref[e : e + 1, :] = jnp.sum(jnp.where(mine, scores, 0.0), axis=0, keepdims=True)
        plain = rows_ref[...].astype(jnp.float32)
        square = jnp.sum(dot(table_ref[...], (plain * plain).astype(jnp.bfloat16)), axis=0, keepdims=True)
        scale = lax.rsqrt(square / D + 1e-05)
        for e in range(experts):
            if e:
                for copy in copies[e - 1]:
                    copy.wait()
            weight_ref = held_ref.at[e - 1] if e else weight_refs[0]
            gate = dot(weight_ref[0], rows_ref[...]) * scale
            up = dot(weight_ref[1], rows_ref[...]) * scale
            out_ref[e] = ((up + 1.0) * gate * jax.nn.sigmoid(1.702 * gate)).astype(jnp.bfloat16)

    flat = [piece for part in pieces for piece in part]
    return pl.pallas_call(
        kernel,
        out_shape=(
            jax.ShapeDtypeStruct((experts, units, lanes), jnp.bfloat16),
            jax.ShapeDtypeStruct((experts, lanes), jnp.float32),
        ),
        in_specs=[in_smem()]
        + in_vmem(len(flat) + 2)
        + [pl.BlockSpec(memory_space=pl.ANY)] * (experts - 1),
        out_specs=tuple(in_vmem(2)),
        scratch_shapes=[
            pltpu.VMEM((D, lanes), jnp.bfloat16),
            pltpu.VMEM((1, 16, 128) if aligned(depth) else (slots, depth, lanes), jnp.bfloat16),
            pltpu.VMEM((height - depth, lanes), jnp.bfloat16),
            pltpu.VMEM((max(1, experts - 1), 2, units, D), jnp.bfloat16),
            pltpu.SemaphoreType.DMA((max(1, experts - 1), len(cuts))),
        ],
        compiler_params=params(13 if aligned(depth) else 16),
        cost_estimate=cost(4 * experts * lanes * D * units, 4 * experts * D * units),
        name="activate",
    )(jnp.stack([pair, t] + chosen).astype(jnp.int32), *flat, gain_table, *weights)


def ready(table, ahead):
    def kernel(table_ref, ahead_ref, out_ref):
        out_ref[...] = table_ref[...]

    return pl.pallas_call(
        kernel,
        out_shape=jax.ShapeDtypeStruct(table.shape, table.dtype),
        in_specs=in_vmem(2),
        out_specs=in_vmem(1)[0],
        compiler_params=params(4),
        cost_estimate=cost(0, 4 * table.size),
        name="ready",
    )(table, ahead)


def combine(activated, share, weights, t, slots):
    t_count = len(activated)
    experts, units, lanes = activated[0].shape
    width = weights[0].shape[0]
    rows = lanes // slots

    def kernel(t_ref, *refs):
        activated_refs = refs[:t_count]
        share_ref = refs[t_count]
        weight_refs = refs[t_count + 1 : t_count + 1 + experts]
        *out_refs, all_ref, stage_ref = refs[t_count + 1 + experts :]
        for u in range(t_count):
            index = t_ref[0] ^ u
            if aligned(units):
                all_ref[:, pl.ds(pl.multiple_of(index * units, 16), units), :] = activated_refs[u][...]
            else:
                stage_ref[index] = activated_refs[u][...]
        if not aligned(units):
            for index in range(t_count):
                all_ref[:, index * units : (index + 1) * units, :] = stage_ref[index]
        total = 0.0
        for e in range(experts):
            result = dot(weight_refs[e][...], all_ref[e]).astype(jnp.bfloat16).astype(jnp.float32)
            total = total + share_ref[e : e + 1, :] * result
        for j in range(slots):
            out_refs[j][...] = total[:, j * rows : (j + 1) * rows].astype(jnp.bfloat16)

    return pl.pallas_call(
        kernel,
        out_shape=tuple(jax.ShapeDtypeStruct((width, rows), jnp.bfloat16) for _ in range(slots)),
        in_specs=[in_smem()] + in_vmem(t_count + 1 + experts),
        out_specs=tuple(in_vmem(slots)),
        scratch_shapes=[
            pltpu.VMEM((experts, t_count * units, lanes), jnp.bfloat16),
            pltpu.VMEM((1, 1, 16, 128) if aligned(units) else (t_count, experts, units, lanes), jnp.bfloat16),
        ],
        compiler_params=params(7 if aligned(units) else 16),
        cost_estimate=cost(
            2 * experts * lanes * t_count * units * width, 2 * experts * t_count * units * width
        ),
        name="combine",
    )(t.reshape(1), *activated, share, *weights)


def local(
    queries,
    key_rows,
    value_rows,
    sink_logits,
    out_weight,
    residual,
    norm_gain,
    expert_in,
    expert_out,
    routes,
    route_scores,
):
    rows = queries.shape[0]
    z_count, t_count, s_count = lax.axis_size("ep"), lax.axis_size("tp"), lax.axis_size("sub")
    z, t, s = (lax.axis_index(name).astype(jnp.int32) for name in ("ep", "tp", "sub"))
    columns = out_weight.shape[1]
    width = expert_out.shape[2]
    slots = t_count
    group = z_count // slots
    pair = z // group

    paired = jnp.concatenate([key_rows, value_rows], axis=1)
    earlier = shifted(paired, ("ep", "sub"), 1)
    out_weight = out_weight.T
    depth = out_weight.shape[1] // s_count
    near = lax.dynamic_slice_in_dim(out_weight, s * depth, depth, 1)
    shared = slots == 2 and group == t_count and aligned(columns)
    residual = residual.T.reshape(slots * group, columns, rows)
    kept_residual = picked(residual.reshape(slots, group * columns, rows), pair ^ t, 0)
    earlier, near, expert_in, expert_out = lax.optimization_barrier((earlier, near, expert_in, expert_out))

    near = swapped(near, "ep", 1)

    if not shared:
        route = [
            (i * t_count + k, (i ^ (group * k)) * t_count + k) for i in range(z_count) for k in range(t_count)
        ]
        kept_residual = lax.ppermute(kept_residual, ("ep", "tp"), route)

    expert_in = expert_in[0].transpose(0, 2, 1)
    expert_out = expert_out[0]
    experts_in = [expert_in] + [swapped(expert_in, "sub", e) for e in range(1, s_count)]
    experts_out = [expert_out] + [swapped(expert_out, "sub", e) for e in range(1, s_count)]
    chosen = [z * s_count + (s ^ e) for e in range(s_count)]

    first = (lax.axis_index(("ep", "sub")) == 0).astype(jnp.int32)
    below = residual if shared else residual[:, :16]
    place = jnp.stack([first, (pair ^ 1) * group + t if shared else first * 0])
    attended = attention(
        queries, earlier, key_rows, value_rows, sink_logits, place, routes.T, route_scores.T, below
    )
    gathered = [attended] + [swapped(attended, "ep", group * j) for j in range(1, slots)]
    experts_out, _ = lax.optimization_barrier((experts_out, attended))
    experts_out = flip(experts_out)

    gathered, near, experts_out = lax.optimization_barrier((gathered, near, experts_out))
    near_weights = [near] + [swapped(near, "sub", u) for u in range(1, s_count)]
    own_share = picked(residual, pair * group + t, 0) if shared else below[0]
    member = z % group
    mine = project(gathered, [out_weight], own_share, (t == member) & shared, t, s * 0, t_count)
    other = project(gathered, near_weights, own_share, (t == member ^ 1) & shared, t, s, t_count)
    first_member = z % group == 0

    def ordered(a, b):
        return jnp.concatenate([jnp.where(first_member, a, b), jnp.where(first_member, b, a)], axis=0)

    span = slice(queries.shape[1], queries.shape[1] + 16)
    kept_routes = gathered[0][span]
    for j in range(1, slots):
        kept_routes = jnp.where(t == j, gathered[j][span], kept_routes)
    hidden = ordered(mine[0], other[0])
    if not shared:
        hidden = hidden + kept_residual.astype(jnp.float32)
    for m in range(1, t_count):
        received = swapped(ordered(mine[1][m - 1], other[1][m - 1]), "tp", m)
        hidden = hidden + received.astype(jnp.float32)
    gain_part = picked(norm_gain.reshape(slots, group * columns), pair, 0)
    scaled = jnp.concatenate([(hidden * gain_part[:, None]).astype(jnp.bfloat16), kept_routes], axis=0)

    own = {0: scaled}
    pieces = [own] + [{} for m in range(1, t_count)]
    distance = z_count // 2
    while distance:
        held = list(own)
        if distance >= group:
            for m in range(1, t_count):
                pieces[m].update({d: swapped(own[d], "tp", m) for d in held if d not in pieces[m]})
        for d in held:
            own[d + distance] = swapped(own[d], "ep", distance)
        distance //= 2
    for m in range(1, t_count):
        pieces[m].update({d: swapped(own[d], "tp", m) for d in range(0, z_count, group) if d not in pieces[m]})
    late = {d: own[d] for d in own if d % group}
    late, pieces[1:] = lax.optimization_barrier((late, pieces[1:]))
    for m in range(1, t_count):
        pieces[m].update({d: swapped(late[d], "tp", m) for d in late})

    inverse_gain = 1.0 / norm_gain
    inverse_square = inverse_gain * inverse_gain
    coarse = inverse_square.astype(jnp.bfloat16)
    fine = (inverse_square - coarse.astype(jnp.float32)).astype(jnp.bfloat16)
    gain_table = jnp.concatenate([coarse[None], fine[None], jnp.zeros((14, D), jnp.bfloat16)], axis=0)

    gain_table, _ = lax.optimization_barrier((gain_table, scaled))
    gain_table = ready(gain_table, expert_in)

    total = 0.0
    for m in range(t_count):
        for r in range(slots):
            here = (pair == m) & ((pair ^ t) == r)
            total = total + jnp.where(here, pieces[m][group * r][:width].astype(jnp.float32), 0.0)
    total = total * lax.dynamic_slice_in_dim(inverse_gain, t * width, width, 0)[:, None]
    total = lax.optimization_barrier(total)

    after = None
    for p in range(group):
        part = [[pieces[m][group * r + p] for r in range(slots)] for m in range(t_count)]
        if p:
            part, after = lax.optimization_barrier((part, after))
        activated, share = activate(part, gain_table, experts_in, pair, t, chosen)
        after = activated
        activated = [activated] + [swapped(activated, "tp", m) for m in range(1, t_count)]
        for j, result in enumerate(combine(activated, share, experts_out, t, slots)):
            distance = group * j + p
            result = swapped(result, "ep", distance) if distance else result
            total = total + result.astype(jnp.float32)
    return total.astype(jnp.bfloat16).T


def solution(mesh):
    in_specs = (
        P(("groups", "ep", "sub"), "tp"),
        P(("groups", "ep", "sub"), "tp"),
        P(("groups", "ep", "sub"), "tp"),
        P("tp"),
        P("tp", "ep"),
        P(("groups", "ep", "sub"), None),
        P(),
        P(("ep", "sub"), None, None, "tp"),
        P(("ep", "sub"), None, "tp"),
        P(("groups", "ep", "sub"), None),
        P(("groups", "ep", "sub"), None),
    )
    out_specs = P(("groups", "ep", "sub"), "tp")
    return jax.shard_map(local, mesh=mesh, in_specs=in_specs, out_specs=out_specs, check_vma=False)
```

```python
import jax
import jax.numpy as jnp
from jax import lax
from jax.experimental import pallas as pl
from jax.experimental.pallas import tpu as pltpu
from jax.sharding import PartitionSpec as P

D = 2880
HD = 64
WIN = 128
TOP = 4
MIB = 1024 * 1024


def shifted(block, axis, distance):
    devices = range(lax.axis_size(axis))
    route = [(i - distance, i) for i in devices if i - distance in devices]
    return lax.ppermute(block, axis, route)


def swapped(block, axis, distance):
    return lax.ppermute(block, axis, [(i, i ^ distance) for i in range(lax.axis_size(axis))])


def picked(blocks, index, axis):
    return lax.dynamic_index_in_dim(blocks, index, axis, keepdims=False)


def in_vmem(count):
    return [pl.BlockSpec(memory_space=pltpu.VMEM)] * count


def in_smem():
    return pl.BlockSpec(memory_space=pltpu.SMEM)


def cost(flops, bytes_accessed):
    return pl.CostEstimate(flops=flops, bytes_accessed=bytes_accessed, transcendentals=0)


def dot(left, right):
    return jnp.dot(left, right, preferred_element_type=jnp.float32)


def aligned(size):
    return size % 16 == 0


def fetches(source, target, arrived, cuts):
    return [
        pltpu.make_async_copy(source.at[cut], target.at[cut], arrived.at[index]) for index, cut in enumerate(cuts)
    ]


def cuts_of(lead, size, count):
    count = count if size % (16 * count) == 0 else 1
    step = size // count
    return [(*at, pl.ds(i * step, step)) for at in lead for i in range(count)]


def params(mebibytes):
    return pltpu.CompilerParams(vmem_limit_bytes=int(mebibytes * MIB))


def attention_kernel(
    place_ref, sink_ref, q_ref, earlier_ref, k_ref, v_ref, routes_ref, scores_ref, residual_ref, out_ref
):
    width = q_ref.shape[1]
    numbers = [routes_ref[...], scores_ref[...] // 256, scores_ref[...] % 256]
    numbers.append(jnp.zeros((16 - 3 * TOP, q_ref.shape[0]), jnp.int32))
    out_ref[width : width + 16, :] = jnp.concatenate(numbers, axis=0).astype(jnp.float32).astype(jnp.bfloat16)
    out_ref[width + 16 :, :] = residual_ref[place_ref[1]]
    rows = q_ref.shape[0]
    kv_count = k_ref.shape[1] // HD
    pairs = q_ref.shape[1] // (2 * HD * kv_count)
    key = lax.broadcasted_iota(jnp.int32, (rows, rows), 0)
    query = lax.broadcasted_iota(jnp.int32, (rows, rows), 1)
    before = key > query
    shut = before & (place_ref[0] == 1)
    blank = jnp.zeros((2 * rows, HD), jnp.bfloat16)
    values = jnp.concatenate(
        [
            block.astype(jnp.float32).T.astype(jnp.bfloat16)
            for block in (earlier_ref[:, kv_count * HD :], v_ref[...])
        ],
        axis=1,
    )
    for g in range(kv_count):
        head = slice(g * HD, (g + 1) * HD)
        keys = jnp.concatenate([earlier_ref[:, head], k_ref[:, head]], axis=0) * jnp.bfloat16(HD ** (-0.5))
        keys = jnp.concatenate(
            [jnp.concatenate([keys, blank], axis=1), jnp.concatenate([blank, keys], axis=1)], axis=0
        )
        for i in range(pairs):
            start = (g * pairs + i) * 2 * HD
            products = lax.dot_general(
                keys,
                q_ref[:, start : start + 2 * HD],
                (((1,), (1,)), ((), ())),
                preferred_element_type=jnp.float32,
            )
            weights = []
            for side in range(2):
                sink = sink_ref[(g * pairs + i) * 2 + side]
                part = products[side * 2 * rows : (side + 1) * 2 * rows]
                scores = jnp.where(before, part[:rows], part[rows:])
                scores = jnp.where(shut, -1e30, scores)
                largest = jnp.maximum(jnp.max(scores, axis=0, keepdims=True), sink)
                numerator = jnp.exp(scores - largest)
                denominator = jnp.sum(numerator, axis=0, keepdims=True) + jnp.exp(sink - largest)
                numerator = numerator * (1.0 / denominator)
                weights.append(
                    jnp.concatenate(
                        [
                            jnp.where(before, numerator, 0.0).astype(jnp.bfloat16),
                            jnp.where(before, 0.0, numerator).astype(jnp.bfloat16),
                        ],
                        axis=0,
                    )
                )
            result = dot(values[head], jnp.concatenate(weights, axis=1)).astype(jnp.bfloat16)
            out_ref[start : start + HD, :] = result[:, :rows]
            out_ref[start + HD : start + 2 * HD, :] = result[:, rows:]


def attention(queries, earlier, key_rows, value_rows, sink_logits, place, routes, scores, residual):
    rows, width = queries.shape
    return pl.pallas_call(
        attention_kernel,
        out_shape=jax.ShapeDtypeStruct((width + 16 + residual.shape[1], rows), jnp.bfloat16),
        in_specs=[in_smem(), in_smem()] + in_vmem(7),
        out_specs=in_vmem(1)[0],
        compiler_params=params(8),
        cost_estimate=cost(8 * rows * rows * width, 6 * rows * width),
        name="attention",
    )(place, sink_logits, queries, earlier, key_rows, value_rows, routes, scores, residual)


def flip(arrays):
    def kernel(*refs):
        for i in range(len(arrays)):
            refs[len(arrays) + i][...] = refs[i][...].T

    return pl.pallas_call(
        kernel,
        out_shape=tuple(jax.ShapeDtypeStruct(a.shape[::-1], a.dtype) for a in arrays),
        in_specs=in_vmem(len(arrays)),
        out_specs=tuple(in_vmem(len(arrays))),
        compiler_params=params(12),
        cost_estimate=cost(0, 4 * sum(a.size for a in arrays)),
        name="flip",
    )(*arrays)


def project(attended, weights, residual, has_share, t, s, t_count):
    slots = len(attended)
    rows = attended[0].shape[1]
    columns, depth = weights[0].shape
    shares = len(weights)
    width = shares * depth

    def kernel(place_ref, *refs):
        attended_refs = refs[:slots]
        weight_refs = refs[slots : slots + shares]
        residual_ref, kept_ref, sent_ref, total = refs[slots + shares :]
        t, s = place_ref[0], place_ref[1]
        result = 0.0
        for u in range(shares):
            span = pl.ds(pl.multiple_of((s ^ u) * depth, 128), depth)
            block = jnp.concatenate([ref[span, :] for ref in attended_refs], axis=1)
            result = result + dot(weight_refs[u][...], block)
        total[...] = result

        @pl.when(place_ref[2] == 1)
        def _():
            for j in range(slots):
                share = attended_refs[j][width + 16 :, :] if j else residual_ref[...]
                if share.shape[0] == columns:
                    total[:, j * rows : (j + 1) * rows] += share.astype(jnp.float32)

        for m in range(t_count):
            block = total[:, pl.ds(pl.multiple_of((t ^ m) * rows, 128), rows)]
            if m == 0:
                kept_ref[...] = block
            else:
                sent_ref[m - 1] = block.astype(jnp.bfloat16)

    return pl.pallas_call(
        kernel,
        out_shape=(
            jax.ShapeDtypeStruct((columns, rows), jnp.float32),
            jax.ShapeDtypeStruct((t_count - 1, columns, rows), jnp.bfloat16),
        ),
        in_specs=[in_smem()] + in_vmem(slots + shares + 1),
        out_specs=tuple(in_vmem(2)),
        scratch_shapes=[pltpu.VMEM((columns, slots * rows), jnp.float32)],
        compiler_params=params(8),
        cost_estimate=cost(2 * slots * rows * width * columns, 2 * width * columns),
        name="project",
    )(jnp.stack([t, s, has_share]).astype(jnp.int32), *attended, *weights, residual)


def activate(pieces, gain_table, weights, pair, t, chosen):
    slots = len(pieces)
    height, rows = pieces[0][0].shape
    depth = D // slots
    lanes = slots * rows
    experts = len(weights)
    units = weights[0].shape[1]
    cuts = cuts_of([(0,), (1,)], units, 3)

    def kernel(place_ref, *refs):
        piece_refs = refs[: slots * slots]
        table_ref = refs[slots * slots]
        weight_refs = refs[slots * slots + 1 : slots * slots + 1 + experts]
        out_ref, share_ref, rows_ref, stage_ref, routes_ref, held_ref, arrived = refs[
            slots * slots + 1 + experts :
        ]
        copies = [
            fetches(weight_refs[e], held_ref.at[e - 1], arrived.at[e - 1], cuts) for e in range(1, experts)
        ]
        for copy in sum(copies, []):
            copy.start()
        for m in range(slots):
            for r in range(slots):
                lane = pl.ds(pl.multiple_of((place_ref[1] ^ r ^ m) * rows, 128), rows)
                index = place_ref[0] ^ r
                piece_ref = piece_refs[m * slots + r]
                block = piece_ref[:depth, :]
                if aligned(depth):
                    rows_ref[pl.ds(pl.multiple_of(index * depth, 16), depth), lane] = block
                else:
                    stage_ref[index, :, lane] = block
                if not r:
                    routes_ref[:, lane] = piece_ref[depth:, :]
        if not aligned(depth):
            for index in range(slots):
                rows_ref[index * depth : (index + 1) * depth, :] = stage_ref[index]
        routes = routes_ref[...].astype(jnp.float32)
        scores = routes[TOP : 2 * TOP] * 256.0 + routes[2 * TOP : 3 * TOP]
        scores = scores / jnp.sum(scores, axis=0, keepdims=True)
        for e in range(experts):
            mine = routes[:TOP] == place_ref[2 + e].astype(jnp.float32)
            share_ref[e : e + 1, :] = jnp.sum(jnp.where(mine, scores, 0.0), axis=0, keepdims=True)
        plain = rows_ref[...].astype(jnp.float32)
        square = jnp.sum(dot(table_ref[...], (plain * plain).astype(jnp.bfloat16)), axis=0, keepdims=True)
        scale = lax.rsqrt(square / D + 1e-05)
        for e in range(experts):
            if e:
                for copy in copies[e - 1]:
                    copy.wait()
            weight_ref = held_ref.at[e - 1] if e else weight_refs[0]
            gate = dot(weight_ref[0], rows_ref[...]) * scale
            up = dot(weight_ref[1], rows_ref[...]) * scale
            out_ref[e] = ((up + 1.0) * gate * jax.nn.sigmoid(1.702 * gate)).astype(jnp.bfloat16)

    flat = [piece for part in pieces for piece in part]
    return pl.pallas_call(
        kernel,
        out_shape=(
            jax.ShapeDtypeStruct((experts, units, lanes), jnp.bfloat16),
            jax.ShapeDtypeStruct((experts, lanes), jnp.float32),
        ),
        in_specs=[in_smem()]
        + in_vmem(len(flat) + 2)
        + [pl.BlockSpec(memory_space=pl.ANY)] * (experts - 1),
        out_specs=tuple(in_vmem(2)),
        scratch_shapes=[
            pltpu.VMEM((D, lanes), jnp.bfloat16),
            pltpu.VMEM((1, 16, 128) if aligned(depth) else (slots, depth, lanes), jnp.bfloat16),
            pltpu.VMEM((height - depth, lanes), jnp.bfloat16),
            pltpu.VMEM((max(1, experts - 1), 2, units, D), jnp.bfloat16),
            pltpu.SemaphoreType.DMA((max(1, experts - 1), len(cuts))),
        ],
        compiler_params=params(13 if aligned(depth) else 16),
        cost_estimate=cost(4 * experts * lanes * D * units, 4 * experts * D * units),
        name="activate",
    )(jnp.stack([pair, t] + chosen).astype(jnp.int32), *flat, gain_table, *weights)


def combine(activated, share, weights, t, slots):
    t_count = len(activated)
    experts, units, lanes = activated[0].shape
    width = weights[0].shape[0]
    rows = lanes // slots

    def kernel(t_ref, *refs):
        activated_refs = refs[:t_count]
        share_ref = refs[t_count]
        weight_refs = refs[t_count + 1 : t_count + 1 + experts]
        *out_refs, all_ref, stage_ref = refs[t_count + 1 + experts :]
        for u in range(t_count):
            index = t_ref[0] ^ u
            if aligned(units):
                all_ref[:, pl.ds(pl.multiple_of(index * units, 16), units), :] = activated_refs[u][...]
            else:
                stage_ref[index] = activated_refs[u][...]
        if not aligned(units):
            for index in range(t_count):
                all_ref[:, index * units : (index + 1) * units, :] = stage_ref[index]
        total = 0.0
        for e in range(experts):
            result = dot(weight_refs[e][...], all_ref[e]).astype(jnp.bfloat16).astype(jnp.float32)
            total = total + share_ref[e : e + 1, :] * result
        for j in range(slots):
            out_refs[j][...] = total[:, j * rows : (j + 1) * rows].astype(jnp.bfloat16)

    return pl.pallas_call(
        kernel,
        out_shape=tuple(jax.ShapeDtypeStruct((width, rows), jnp.bfloat16) for _ in range(slots)),
        in_specs=[in_smem()] + in_vmem(t_count + 1 + experts),
        out_specs=tuple(in_vmem(slots)),
        scratch_shapes=[
            pltpu.VMEM((experts, t_count * units, lanes), jnp.bfloat16),
            pltpu.VMEM((1, 1, 16, 128) if aligned(units) else (t_count, experts, units, lanes), jnp.bfloat16),
        ],
        compiler_params=params(7 if aligned(units) else 16),
        cost_estimate=cost(
            2 * experts * lanes * t_count * units * width, 2 * experts * t_count * units * width
        ),
        name="combine",
    )(t.reshape(1), *activated, share, *weights)


def local(
    queries,
    key_rows,
    value_rows,
    sink_logits,
    out_weight,
    residual,
    norm_gain,
    expert_in,
    expert_out,
    routes,
    route_scores,
):
    rows = queries.shape[0]
    z_count, t_count, s_count = lax.axis_size("ep"), lax.axis_size("tp"), lax.axis_size("sub")
    z, t, s = (lax.axis_index(name).astype(jnp.int32) for name in ("ep", "tp", "sub"))
    columns = out_weight.shape[1]
    width = expert_out.shape[2]
    slots = t_count
    group = z_count // slots
    pair = z // group

    paired = jnp.concatenate([key_rows, value_rows], axis=1)
    earlier = shifted(paired, ("ep", "sub"), 1)
    out_weight = out_weight.T
    depth = out_weight.shape[1] // s_count
    near = lax.dynamic_slice_in_dim(out_weight, s * depth, depth, 1)
    shared = slots == 2 and group == t_count and aligned(columns)
    residual = residual.T.reshape(slots * group, columns, rows)
    kept_residual = picked(residual.reshape(slots, group * columns, rows), pair ^ t, 0)
    earlier, near, expert_in, expert_out = lax.optimization_barrier((earlier, near, expert_in, expert_out))

    near = swapped(near, "ep", 1)

    if not shared:
        route = [
            (i * t_count + k, (i ^ (group * k)) * t_count + k) for i in range(z_count) for k in range(t_count)
        ]
        kept_residual = lax.ppermute(kept_residual, ("ep", "tp"), route)

    expert_in = expert_in[0].transpose(0, 2, 1)
    expert_out = expert_out[0]
    experts_in = [expert_in] + [swapped(expert_in, "sub", e) for e in range(1, s_count)]
    experts_out = [expert_out] + [swapped(expert_out, "sub", e) for e in range(1, s_count)]
    chosen = [z * s_count + (s ^ e) for e in range(s_count)]

    first = (lax.axis_index(("ep", "sub")) == 0).astype(jnp.int32)
    below = residual if shared else residual[:, :16]
    place = jnp.stack([first, (pair ^ 1) * group + t if shared else first * 0])
    attended = attention(
        queries, earlier, key_rows, value_rows, sink_logits, place, routes.T, route_scores.T, below
    )
    gathered = [attended] + [swapped(attended, "ep", group * j) for j in range(1, slots)]
    experts_out, _ = lax.optimization_barrier((experts_out, attended))
    experts_out = flip(experts_out)

    own_share = picked(residual, pair * group + t, 0) if shared else below[0]
    own_share, _ = lax.optimization_barrier((own_share, attended))
    gathered, near, experts_out, own_share = lax.optimization_barrier((gathered, near, experts_out, own_share))
    near_weights = [near] + [swapped(near, "sub", u) for u in range(1, s_count)]
    member = z % group
    mine = project(gathered, [out_weight], own_share, (t == member) & shared, t, s * 0, t_count)
    other = project(gathered, near_weights, own_share, (t == member ^ 1) & shared, t, s, t_count)
    first_member = z % group == 0

    def ordered(a, b):
        return jnp.concatenate([jnp.where(first_member, a, b), jnp.where(first_member, b, a)], axis=0)

    span = slice(queries.shape[1], queries.shape[1] + 16)
    kept_routes = gathered[0][span]
    for j in range(1, slots):
        kept_routes = jnp.where(t == j, gathered[j][span], kept_routes)
    hidden = ordered(mine[0], other[0])
    if not shared:
        hidden = hidden + kept_residual.astype(jnp.float32)
    for m in range(1, t_count):
        received = swapped(ordered(mine[1][m - 1], other[1][m - 1]), "tp", m)
        hidden = hidden + received.astype(jnp.float32)
    gain_part = picked(norm_gain.reshape(slots, group * columns), pair, 0)
    scaled = jnp.concatenate([(hidden * gain_part[:, None]).astype(jnp.bfloat16), kept_routes], axis=0)

    own = {0: scaled}
    pieces = [own] + [{0: swapped(scaled, "tp", m)} for m in range(1, t_count)]
    distance = z_count // 2
    while distance >= group:
        own.update({d + distance: swapped(own[d], "ep", distance) for d in list(own)})
        distance //= 2
    again, pieces[1:] = lax.optimization_barrier((scaled, pieces[1:]))
    own[1] = swapped(again, "ep", 1)
    own, pieces[1:] = lax.optimization_barrier((own, pieces[1:]))
    pieces[0] = own
    for d in range(group, z_count, group):
        own[d + 1] = swapped(own[d], "ep", 1)
        for m in range(1, t_count):
            pieces[m][d] = swapped(own[d], "tp", m)
    for m in range(1, t_count):
        pieces[m][1] = swapped(pieces[m][0], "ep", 1)
        for d in range(group, z_count, group):
            pieces[m][d + 1] = swapped(own[d + 1], "tp", m)

    inverse_gain = 1.0 / norm_gain
    inverse_square = inverse_gain * inverse_gain
    coarse = inverse_square.astype(jnp.bfloat16)
    fine = (inverse_square - coarse.astype(jnp.float32)).astype(jnp.bfloat16)
    gain_table = jnp.concatenate([coarse[None], fine[None], jnp.zeros((14, D), jnp.bfloat16)], axis=0)

    total = 0.0
    for m in range(t_count):
        for r in range(slots):
            here = (pair == m) & ((pair ^ t) == r)
            total = total + jnp.where(here, pieces[m][group * r][:width].astype(jnp.float32), 0.0)
    total = total * lax.dynamic_slice_in_dim(inverse_gain, t * width, width, 0)[:, None]
    total = lax.optimization_barrier(total)

    after = None
    for p in range(group):
        part = [[pieces[m][group * r + p] for r in range(slots)] for m in range(t_count)]
        if p:
            part, after = lax.optimization_barrier((part, after))
        activated, share = activate(part, gain_table, experts_in, pair, t, chosen)
        after = activated
        activated = [activated] + [swapped(activated, "tp", m) for m in range(1, t_count)]
        for j, result in enumerate(combine(activated, share, experts_out, t, slots)):
            distance = group * j + p
            result = swapped(result, "ep", distance) if distance else result
            total = total + result.astype(jnp.float32)
    return total.astype(jnp.bfloat16).T


def solution(mesh):
    in_specs = (
        P(("groups", "ep", "sub"), "tp"),
        P(("groups", "ep", "sub"), "tp"),
        P(("groups", "ep", "sub"), "tp"),
        P("tp"),
        P("tp", "ep"),
        P(("groups", "ep", "sub"), None),
        P(),
        P(("ep", "sub"), None, None, "tp"),
        P(("ep", "sub"), None, "tp"),
        P(("groups", "ep", "sub"), None),
        P(("groups", "ep", "sub"), None),
    )
    out_specs = P(("groups", "ep", "sub"), "tp")
    return jax.shard_map(local, mesh=mesh, in_specs=in_specs, out_specs=out_specs, check_vma=False)
```

```python
import jax
import jax.numpy as jnp
from jax import lax
from jax.experimental import pallas as pl
from jax.experimental.pallas import tpu as pltpu
from jax.sharding import PartitionSpec as P

D = 2880
HD = 64
WIN = 128
TOP = 4
MIB = 1024 * 1024


def shifted(block, axis, distance):
    devices = range(lax.axis_size(axis))
    route = [(i - distance, i) for i in devices if i - distance in devices]
    return lax.ppermute(block, axis, route)


def swapped(block, axis, distance):
    return lax.ppermute(block, axis, [(i, i ^ distance) for i in range(lax.axis_size(axis))])


def picked(blocks, index, axis):
    return lax.dynamic_index_in_dim(blocks, index, axis, keepdims=False)


def in_vmem(count):
    return [pl.BlockSpec(memory_space=pltpu.VMEM)] * count


def in_smem():
    return pl.BlockSpec(memory_space=pltpu.SMEM)


def cost(flops, bytes_accessed):
    return pl.CostEstimate(flops=flops, bytes_accessed=bytes_accessed, transcendentals=0)


def dot(left, right):
    return jnp.dot(left, right, preferred_element_type=jnp.float32)


def aligned(size):
    return size % 16 == 0


def fetches(source, target, arrived, cuts):
    return [
        pltpu.make_async_copy(source.at[cut], target.at[cut], arrived.at[index]) for index, cut in enumerate(cuts)
    ]


def cuts_of(lead, size, count):
    count = count if size % (16 * count) == 0 else 1
    step = size // count
    return [(*at, pl.ds(i * step, step)) for at in lead for i in range(count)]


def params(mebibytes):
    return pltpu.CompilerParams(vmem_limit_bytes=int(mebibytes * MIB))


def attention_kernel(
    place_ref, sink_ref, q_ref, earlier_ref, k_ref, v_ref, routes_ref, scores_ref, residual_ref, out_ref
):
    width = q_ref.shape[1]
    numbers = [routes_ref[...], scores_ref[...] // 256, scores_ref[...] % 256]
    numbers.append(jnp.zeros((16 - 3 * TOP, q_ref.shape[0]), jnp.int32))
    out_ref[width : width + 16, :] = jnp.concatenate(numbers, axis=0).astype(jnp.float32).astype(jnp.bfloat16)
    out_ref[width + 16 :, :] = residual_ref[place_ref[1]]
    rows = q_ref.shape[0]
    kv_count = k_ref.shape[1] // HD
    pairs = q_ref.shape[1] // (2 * HD * kv_count)
    key = lax.broadcasted_iota(jnp.int32, (rows, rows), 0)
    query = lax.broadcasted_iota(jnp.int32, (rows, rows), 1)
    before = key > query
    shut = before & (place_ref[0] == 1)
    blank = jnp.zeros((2 * rows, HD), jnp.bfloat16)
    values = jnp.concatenate(
        [
            block.astype(jnp.float32).T.astype(jnp.bfloat16)
            for block in (earlier_ref[:, kv_count * HD :], v_ref[...])
        ],
        axis=1,
    )
    for g in range(kv_count):
        head = slice(g * HD, (g + 1) * HD)
        keys = jnp.concatenate([earlier_ref[:, head], k_ref[:, head]], axis=0) * jnp.bfloat16(HD ** (-0.5))
        keys = jnp.concatenate(
            [jnp.concatenate([keys, blank], axis=1), jnp.concatenate([blank, keys], axis=1)], axis=0
        )
        for i in range(pairs):
            start = (g * pairs + i) * 2 * HD
            products = lax.dot_general(
                keys,
                q_ref[:, start : start + 2 * HD],
                (((1,), (1,)), ((), ())),
                preferred_element_type=jnp.float32,
            )
            weights = []
            for side in range(2):
                sink = sink_ref[(g * pairs + i) * 2 + side]
                part = products[side * 2 * rows : (side + 1) * 2 * rows]
                scores = jnp.where(before, part[:rows], part[rows:])
                scores = jnp.where(shut, -1e30, scores)
                largest = jnp.maximum(jnp.max(scores, axis=0, keepdims=True), sink)
                numerator = jnp.exp(scores - largest)
                denominator = jnp.sum(numerator, axis=0, keepdims=True) + jnp.exp(sink - largest)
                numerator = numerator * (1.0 / denominator)
                weights.append(
                    jnp.concatenate(
                        [
                            jnp.where(before, numerator, 0.0).astype(jnp.bfloat16),
                            jnp.where(before, 0.0, numerator).astype(jnp.bfloat16),
                        ],
                        axis=0,
                    )
                )
            result = dot(values[head], jnp.concatenate(weights, axis=1)).astype(jnp.bfloat16)
            out_ref[start : start + HD, :] = result[:, :rows]
            out_ref[start + HD : start + 2 * HD, :] = result[:, rows:]


def attention(queries, earlier, key_rows, value_rows, sink_logits, place, routes, scores, residual):
    rows, width = queries.shape
    return pl.pallas_call(
        attention_kernel,
        out_shape=jax.ShapeDtypeStruct((width + 16 + residual.shape[1], rows), jnp.bfloat16),
        in_specs=[in_smem(), in_smem()] + in_vmem(7),
        out_specs=in_vmem(1)[0],
        compiler_params=params(8),
        cost_estimate=cost(8 * rows * rows * width, 6 * rows * width),
        name="attention",
    )(place, sink_logits, queries, earlier, key_rows, value_rows, routes, scores, residual)


def flip(arrays):
    def kernel(*refs):
        for i in range(len(arrays)):
            refs[len(arrays) + i][...] = refs[i][...].T

    return pl.pallas_call(
        kernel,
        out_shape=tuple(jax.ShapeDtypeStruct(a.shape[::-1], a.dtype) for a in arrays),
        in_specs=in_vmem(len(arrays)),
        out_specs=tuple(in_vmem(len(arrays))),
        compiler_params=params(12),
        cost_estimate=cost(0, 4 * sum(a.size for a in arrays)),
        name="flip",
    )(*arrays)


def project(attended, weights, residual, has_share, t, s, t_count):
    slots = len(attended)
    rows = attended[0].shape[1]
    columns, depth = weights[0].shape
    shares = len(weights)
    width = shares * depth

    def kernel(place_ref, *refs):
        attended_refs = refs[:slots]
        weight_refs = refs[slots : slots + shares]
        residual_ref, kept_ref, sent_ref, total = refs[slots + shares :]
        t, s = place_ref[0], place_ref[1]
        result = 0.0
        for u in range(shares):
            span = pl.ds(pl.multiple_of((s ^ u) * depth, 128), depth)
            block = jnp.concatenate([ref[span, :] for ref in attended_refs], axis=1)
            result = result + dot(weight_refs[u][...], block)
        total[...] = result

        @pl.when(place_ref[2] == 1)
        def _():
            for j in range(slots):
                share = attended_refs[j][width + 16 :, :] if j else residual_ref[...]
                if share.shape[0] == columns:
                    total[:, j * rows : (j + 1) * rows] += share.astype(jnp.float32)

        for m in range(t_count):
            block = total[:, pl.ds(pl.multiple_of((t ^ m) * rows, 128), rows)]
            if m == 0:
                kept_ref[...] = block
            else:
                sent_ref[m - 1] = block.astype(jnp.bfloat16)

    return pl.pallas_call(
        kernel,
        out_shape=(
            jax.ShapeDtypeStruct((columns, rows), jnp.float32),
            jax.ShapeDtypeStruct((t_count - 1, columns, rows), jnp.bfloat16),
        ),
        in_specs=[in_smem()] + in_vmem(slots + shares + 1),
        out_specs=tuple(in_vmem(2)),
        scratch_shapes=[pltpu.VMEM((columns, slots * rows), jnp.float32)],
        compiler_params=params(8),
        cost_estimate=cost(2 * slots * rows * width * columns, 2 * width * columns),
        name="project",
    )(jnp.stack([t, s, has_share]).astype(jnp.int32), *attended, *weights, residual)


def activate(pieces, gain_table, weights, pair, t, chosen):
    slots = len(pieces)
    height, rows = pieces[0][0].shape
    depth = D // slots
    lanes = slots * rows
    experts = len(weights)
    units = weights[0].shape[1]
    cuts = cuts_of([(0,), (1,)], units, 3)

    def kernel(place_ref, *refs):
        piece_refs = refs[: slots * slots]
        table_ref = refs[slots * slots]
        weight_refs = refs[slots * slots + 1 : slots * slots + 1 + experts]
        out_ref, share_ref, rows_ref, stage_ref, routes_ref, held_ref, arrived = refs[
            slots * slots + 1 + experts :
        ]
        copies = [
            fetches(weight_refs[e], held_ref.at[e - 1], arrived.at[e - 1], cuts) for e in range(1, experts)
        ]
        for copy in sum(copies, []):
            copy.start()
        for m in range(slots):
            for r in range(slots):
                lane = pl.ds(pl.multiple_of((place_ref[1] ^ r ^ m) * rows, 128), rows)
                index = place_ref[0] ^ r
                piece_ref = piece_refs[m * slots + r]
                block = piece_ref[:depth, :]
                if aligned(depth):
                    rows_ref[pl.ds(pl.multiple_of(index * depth, 16), depth), lane] = block
                else:
                    stage_ref[index, :, lane] = block
                if not r:
                    routes_ref[:, lane] = piece_ref[depth:, :]
        if not aligned(depth):
            for index in range(slots):
                rows_ref[index * depth : (index + 1) * depth, :] = stage_ref[index]
        routes = routes_ref[...].astype(jnp.float32)
        scores = routes[TOP : 2 * TOP] * 256.0 + routes[2 * TOP : 3 * TOP]
        scores = scores / jnp.sum(scores, axis=0, keepdims=True)
        for e in range(experts):
            mine = routes[:TOP] == place_ref[2 + e].astype(jnp.float32)
            share_ref[e : e + 1, :] = jnp.sum(jnp.where(mine, scores, 0.0), axis=0, keepdims=True)
        plain = rows_ref[...].astype(jnp.float32)
        square = jnp.sum(dot(table_ref[...], (plain * plain).astype(jnp.bfloat16)), axis=0, keepdims=True)
        scale = lax.rsqrt(square / D + 1e-05)
        for e in range(experts):
            if e:
                for copy in copies[e - 1]:
                    copy.wait()
            weight_ref = held_ref.at[e - 1] if e else weight_refs[0]
            gate = dot(weight_ref[0], rows_ref[...]) * scale
            up = dot(weight_ref[1], rows_ref[...]) * scale
            out_ref[e] = ((up + 1.0) * gate * jax.nn.sigmoid(1.702 * gate)).astype(jnp.bfloat16)

    flat = [piece for part in pieces for piece in part]
    return pl.pallas_call(
        kernel,
        out_shape=(
            jax.ShapeDtypeStruct((experts, units, lanes), jnp.bfloat16),
            jax.ShapeDtypeStruct((experts, lanes), jnp.float32),
        ),
        in_specs=[in_smem()]
        + in_vmem(len(flat) + 2)
        + [pl.BlockSpec(memory_space=pl.ANY)] * (experts - 1),
        out_specs=tuple(in_vmem(2)),
        scratch_shapes=[
            pltpu.VMEM((D, lanes), jnp.bfloat16),
            pltpu.VMEM((1, 16, 128) if aligned(depth) else (slots, depth, lanes), jnp.bfloat16),
            pltpu.VMEM((height - depth, lanes), jnp.bfloat16),
            pltpu.VMEM((max(1, experts - 1), 2, units, D), jnp.bfloat16),
            pltpu.SemaphoreType.DMA((max(1, experts - 1), len(cuts))),
        ],
        compiler_params=params(13 if aligned(depth) else 16),
        cost_estimate=cost(4 * experts * lanes * D * units, 4 * experts * D * units),
        name="activate",
    )(jnp.stack([pair, t] + chosen).astype(jnp.int32), *flat, gain_table, *weights)


def combine(activated, share, weights, t, slots):
    t_count = len(activated)
    experts, units, lanes = activated[0].shape
    width = weights[0].shape[0]
    rows = lanes // slots

    def kernel(t_ref, *refs):
        activated_refs = refs[:t_count]
        share_ref = refs[t_count]
        weight_refs = refs[t_count + 1 : t_count + 1 + experts]
        *out_refs, all_ref, stage_ref = refs[t_count + 1 + experts :]
        for u in range(t_count):
            index = t_ref[0] ^ u
            if aligned(units):
                all_ref[:, pl.ds(pl.multiple_of(index * units, 16), units), :] = activated_refs[u][...]
            else:
                stage_ref[index] = activated_refs[u][...]
        if not aligned(units):
            for index in range(t_count):
                all_ref[:, index * units : (index + 1) * units, :] = stage_ref[index]
        total = 0.0
        for e in range(experts):
            result = dot(weight_refs[e][...], all_ref[e]).astype(jnp.bfloat16).astype(jnp.float32)
            total = total + share_ref[e : e + 1, :] * result
        for j in range(slots):
            out_refs[j][...] = total[:, j * rows : (j + 1) * rows].astype(jnp.bfloat16)

    return pl.pallas_call(
        kernel,
        out_shape=tuple(jax.ShapeDtypeStruct((width, rows), jnp.bfloat16) for _ in range(slots)),
        in_specs=[in_smem()] + in_vmem(t_count + 1 + experts),
        out_specs=tuple(in_vmem(slots)),
        scratch_shapes=[
            pltpu.VMEM((experts, t_count * units, lanes), jnp.bfloat16),
            pltpu.VMEM((1, 1, 16, 128) if aligned(units) else (t_count, experts, units, lanes), jnp.bfloat16),
        ],
        compiler_params=params(7 if aligned(units) else 16),
        cost_estimate=cost(
            2 * experts * lanes * t_count * units * width, 2 * experts * t_count * units * width
        ),
        name="combine",
    )(t.reshape(1), *activated, share, *weights)


def local(
    queries,
    key_rows,
    value_rows,
    sink_logits,
    out_weight,
    residual,
    norm_gain,
    expert_in,
    expert_out,
    routes,
    route_scores,
):
    rows = queries.shape[0]
    z_count, t_count, s_count = lax.axis_size("ep"), lax.axis_size("tp"), lax.axis_size("sub")
    z, t, s = (lax.axis_index(name).astype(jnp.int32) for name in ("ep", "tp", "sub"))
    columns = out_weight.shape[1]
    width = expert_out.shape[2]
    slots = t_count
    group = z_count // slots
    pair = z // group

    paired = jnp.concatenate([key_rows, value_rows], axis=1)
    earlier = shifted(paired, ("ep", "sub"), 1)
    out_weight = out_weight.T
    depth = out_weight.shape[1] // s_count
    near = lax.dynamic_slice_in_dim(out_weight, s * depth, depth, 1)
    shared = slots == 2 and group == t_count and aligned(columns)
    residual = residual.T.reshape(slots * group, columns, rows)
    kept_residual = picked(residual.reshape(slots, group * columns, rows), pair ^ t, 0)
    earlier, near, expert_in, expert_out = lax.optimization_barrier((earlier, near, expert_in, expert_out))

    near = swapped(near, "ep", 1)

    if not shared:
        route = [
            (i * t_count + k, (i ^ (group * k)) * t_count + k) for i in range(z_count) for k in range(t_count)
        ]
        kept_residual = lax.ppermute(kept_residual, ("ep", "tp"), route)

    expert_in = expert_in[0].transpose(0, 2, 1)
    expert_out = expert_out[0]
    experts_in = [expert_in] + [swapped(expert_in, "sub", e) for e in range(1, s_count)]
    experts_out = [expert_out] + [swapped(expert_out, "sub", e) for e in range(1, s_count)]
    chosen = [z * s_count + (s ^ e) for e in range(s_count)]

    first = (lax.axis_index(("ep", "sub")) == 0).astype(jnp.int32)
    below = residual if shared else residual[:, :16]
    place = jnp.stack([first, (pair ^ 1) * group + t if shared else first * 0])
    attended = attention(
        queries, earlier, key_rows, value_rows, sink_logits, place, routes.T, route_scores.T, below
    )
    gathered = [attended] + [swapped(attended, "ep", group * j) for j in range(1, slots)]
    own_share = picked(residual, pair * group + t, 0) if shared else below[0]
    own_share, _ = lax.optimization_barrier((own_share, attended))
    gathered, near, own_share, experts_out = lax.optimization_barrier((gathered, near, own_share, experts_out))
    near_weights = [near] + [swapped(near, "sub", u) for u in range(1, s_count)]
    member = z % group
    mine = project(gathered, [out_weight], own_share, (t == member) & shared, t, s * 0, t_count)
    other = project(gathered, near_weights, own_share, (t == member ^ 1) & shared, t, s, t_count)
    first_member = z % group == 0

    def ordered(a, b):
        return jnp.concatenate([jnp.where(first_member, a, b), jnp.where(first_member, b, a)], axis=0)

    span = slice(queries.shape[1], queries.shape[1] + 16)
    kept_routes = gathered[0][span]
    for j in range(1, slots):
        kept_routes = jnp.where(t == j, gathered[j][span], kept_routes)
    hidden = ordered(mine[0], other[0])
    if not shared:
        hidden = hidden + kept_residual.astype(jnp.float32)
    for m in range(1, t_count):
        received = swapped(ordered(mine[1][m - 1], other[1][m - 1]), "tp", m)
        hidden = hidden + received.astype(jnp.float32)
    gain_part = picked(norm_gain.reshape(slots, group * columns), pair, 0)
    scaled = jnp.concatenate([(hidden * gain_part[:, None]).astype(jnp.bfloat16), kept_routes], axis=0)

    own = {0: scaled}
    pieces = [own] + [{} for m in range(1, t_count)]
    distance = z_count // 2
    while distance:
        held = list(own)
        if distance >= group:
            for m in range(1, t_count):
                pieces[m].update({d: swapped(own[d], "tp", m) for d in held if d not in pieces[m]})
        for d in held:
            own[d + distance] = swapped(own[d], "ep", distance)
        distance //= 2
    for m in range(1, t_count):
        pieces[m].update({d: swapped(own[d], "tp", m) for d in range(0, z_count, group) if d not in pieces[m]})
    late = {d: own[d] for d in own if d % group}
    late, pieces[1:] = lax.optimization_barrier((late, pieces[1:]))
    for m in range(1, t_count):
        pieces[m].update({d: swapped(late[d], "tp", m) for d in late})

    inverse_gain = 1.0 / norm_gain
    inverse_square = inverse_gain * inverse_gain
    coarse = inverse_square.astype(jnp.bfloat16)
    fine = (inverse_square - coarse.astype(jnp.float32)).astype(jnp.bfloat16)
    gain_table = jnp.concatenate([coarse[None], fine[None], jnp.zeros((14, D), jnp.bfloat16)], axis=0)

    total = 0.0
    for m in range(t_count):
        for r in range(slots):
            here = (pair == m) & ((pair ^ t) == r)
            total = total + jnp.where(here, pieces[m][group * r][:width].astype(jnp.float32), 0.0)
    total = total * lax.dynamic_slice_in_dim(inverse_gain, t * width, width, 0)[:, None]
    total = lax.optimization_barrier(total)

    units = []
    for p in range(group):
        part = [[pieces[m][group * r + p] for r in range(slots)] for m in range(t_count)]
        if units:
            part, _ = lax.optimization_barrier((part, units[-1][0][0]))
        activated, share = activate(part, gain_table, experts_in, pair, t, chosen)
        units.append(([activated] + [swapped(activated, "tp", m) for m in range(1, t_count)], share))

    experts_out, _ = lax.optimization_barrier((experts_out, units[-1][0][0]))
    experts_out = flip(experts_out)
    for p in range(group):
        activated, share = units[p]
        for j, result in enumerate(combine(activated, share, experts_out, t, slots)):
            distance = group * j + p
            result = swapped(result, "ep", distance) if distance else result
            total = total + result.astype(jnp.float32)
    return total.astype(jnp.bfloat16).T


def solution(mesh):
    in_specs = (
        P(("groups", "ep", "sub"), "tp"),
        P(("groups", "ep", "sub"), "tp"),
        P(("groups", "ep", "sub"), "tp"),
        P("tp"),
        P("tp", "ep"),
        P(("groups", "ep", "sub"), None),
        P(),
        P(("ep", "sub"), None, None, "tp"),
        P(("ep", "sub"), None, "tp"),
        P(("groups", "ep", "sub"), None),
        P(("groups", "ep", "sub"), None),
    )
    out_specs = P(("groups", "ep", "sub"), "tp")
    return jax.shard_map(local, mesh=mesh, in_specs=in_specs, out_specs=out_specs, check_vma=False)
```

```python
import jax
import jax.numpy as jnp
from jax import lax
from jax.experimental import pallas as pl
from jax.experimental.pallas import tpu as pltpu
from jax.sharding import PartitionSpec as P

D = 2880
HD = 64
WIN = 128
TOP = 4
MIB = 1024 * 1024


def shifted(block, axis, distance):
    devices = range(lax.axis_size(axis))
    route = [(i - distance, i) for i in devices if i - distance in devices]
    return lax.ppermute(block, axis, route)


def swapped(block, axis, distance):
    return lax.ppermute(block, axis, [(i, i ^ distance) for i in range(lax.axis_size(axis))])


def picked(blocks, index, axis):
    return lax.dynamic_index_in_dim(blocks, index, axis, keepdims=False)


def in_vmem(count):
    return [pl.BlockSpec(memory_space=pltpu.VMEM)] * count


def in_smem():
    return pl.BlockSpec(memory_space=pltpu.SMEM)


def cost(flops, bytes_accessed):
    return pl.CostEstimate(flops=flops, bytes_accessed=bytes_accessed, transcendentals=0)


def dot(left, right):
    return jnp.dot(left, right, preferred_element_type=jnp.float32)


def aligned(size):
    return size % 16 == 0


def fetches(source, target, arrived, cuts):
    return [
        pltpu.make_async_copy(source.at[cut], target.at[cut], arrived.at[index]) for index, cut in enumerate(cuts)
    ]


def cuts_of(lead, size, count):
    count = count if size % (16 * count) == 0 else 1
    step = size // count
    return [(*at, pl.ds(i * step, step)) for at in lead for i in range(count)]


def params(mebibytes):
    return pltpu.CompilerParams(vmem_limit_bytes=int(mebibytes * MIB))


def attention_kernel(
    place_ref, sink_ref, q_ref, earlier_ref, k_ref, v_ref, routes_ref, scores_ref, residual_ref, out_ref
):
    width = q_ref.shape[1]
    numbers = [routes_ref[...], scores_ref[...] // 256, scores_ref[...] % 256]
    numbers.append(jnp.zeros((16 - 3 * TOP, q_ref.shape[0]), jnp.int32))
    out_ref[width : width + 16, :] = jnp.concatenate(numbers, axis=0).astype(jnp.float32).astype(jnp.bfloat16)
    out_ref[width + 16 :, :] = residual_ref[place_ref[1]]
    rows = q_ref.shape[0]
    kv_count = k_ref.shape[1] // HD
    pairs = q_ref.shape[1] // (2 * HD * kv_count)
    key = lax.broadcasted_iota(jnp.int32, (rows, rows), 0)
    query = lax.broadcasted_iota(jnp.int32, (rows, rows), 1)
    before = key > query
    shut = before & (place_ref[0] == 1)
    blank = jnp.zeros((2 * rows, HD), jnp.bfloat16)
    values = jnp.concatenate(
        [
            block.astype(jnp.float32).T.astype(jnp.bfloat16)
            for block in (earlier_ref[:, kv_count * HD :], v_ref[...])
        ],
        axis=1,
    )
    for g in range(kv_count):
        head = slice(g * HD, (g + 1) * HD)
        keys = jnp.concatenate([earlier_ref[:, head], k_ref[:, head]], axis=0) * jnp.bfloat16(HD ** (-0.5))
        keys = jnp.concatenate(
            [jnp.concatenate([keys, blank], axis=1), jnp.concatenate([blank, keys], axis=1)], axis=0
        )
        for i in range(pairs):
            start = (g * pairs + i) * 2 * HD
            products = lax.dot_general(
                keys,
                q_ref[:, start : start + 2 * HD],
                (((1,), (1,)), ((), ())),
                preferred_element_type=jnp.float32,
            )
            weights = []
            for side in range(2):
                sink = sink_ref[(g * pairs + i) * 2 + side]
                part = products[side * 2 * rows : (side + 1) * 2 * rows]
                scores = jnp.where(before, part[:rows], part[rows:])
                scores = jnp.where(shut, -1e30, scores)
                largest = jnp.maximum(jnp.max(scores, axis=0, keepdims=True), sink)
                numerator = jnp.exp(scores - largest)
                denominator = jnp.sum(numerator, axis=0, keepdims=True) + jnp.exp(sink - largest)
                numerator = numerator * (1.0 / denominator)
                weights.append(
                    jnp.concatenate(
                        [
                            jnp.where(before, numerator, 0.0).astype(jnp.bfloat16),
                            jnp.where(before, 0.0, numerator).astype(jnp.bfloat16),
                        ],
                        axis=0,
                    )
                )
            result = dot(values[head], jnp.concatenate(weights, axis=1)).astype(jnp.bfloat16)
            out_ref[start : start + HD, :] = result[:, :rows]
            out_ref[start + HD : start + 2 * HD, :] = result[:, rows:]


def attention(queries, earlier, key_rows, value_rows, sink_logits, place, routes, scores, residual):
    rows, width = queries.shape
    return pl.pallas_call(
        attention_kernel,
        out_shape=jax.ShapeDtypeStruct((width + 16 + residual.shape[1], rows), jnp.bfloat16),
        in_specs=[in_smem(), in_smem()] + in_vmem(7),
        out_specs=in_vmem(1)[0],
        compiler_params=params(8),
        cost_estimate=cost(8 * rows * rows * width, 6 * rows * width),
        name="attention",
    )(place, sink_logits, queries, earlier, key_rows, value_rows, routes, scores, residual)


def flip(arrays):
    def kernel(*refs):
        for i in range(len(arrays)):
            refs[len(arrays) + i][...] = refs[i][...].T

    return pl.pallas_call(
        kernel,
        out_shape=tuple(jax.ShapeDtypeStruct(a.shape[::-1], a.dtype) for a in arrays),
        in_specs=in_vmem(len(arrays)),
        out_specs=tuple(in_vmem(len(arrays))),
        compiler_params=params(12),
        cost_estimate=cost(0, 4 * sum(a.size for a in arrays)),
        name="flip",
    )(*arrays)


def fetched(weight):
    cuts = cuts_of([(k,) for k in range(weight.shape[0])], weight.shape[1], 3)

    def kernel(weight_ref, out_ref, arrived):
        copies = fetches(weight_ref, out_ref, arrived, cuts)
        for copy in copies:
            copy.start()
        for copy in copies:
            copy.wait()

    return pl.pallas_call(
        kernel,
        out_shape=jax.ShapeDtypeStruct(weight.shape, weight.dtype),
        in_specs=[pl.BlockSpec(memory_space=pl.ANY)],
        out_specs=in_vmem(1)[0],
        scratch_shapes=[pltpu.SemaphoreType.DMA((len(cuts),))],
        compiler_params=params(2),
        cost_estimate=cost(0, 4 * weight.size),
        name="fetched",
    )(weight)


def project(attended, weights, residual, has_share, t, s, t_count):
    slots = len(attended)
    rows = attended[0].shape[1]
    columns, depth = weights[0].shape
    shares = len(weights)
    width = shares * depth

    def kernel(place_ref, *refs):
        attended_refs = refs[:slots]
        weight_refs = refs[slots : slots + shares]
        residual_ref, kept_ref, sent_ref, total = refs[slots + shares :]
        t, s = place_ref[0], place_ref[1]
        result = 0.0
        for u in range(shares):
            span = pl.ds(pl.multiple_of((s ^ u) * depth, 128), depth)
            block = jnp.concatenate([ref[span, :] for ref in attended_refs], axis=1)
            result = result + dot(weight_refs[u][...], block)
        total[...] = result

        @pl.when(place_ref[2] == 1)
        def _():
            for j in range(slots):
                share = attended_refs[j][width + 16 :, :] if j else residual_ref[...]
                if share.shape[0] == columns:
                    total[:, j * rows : (j + 1) * rows] += share.astype(jnp.float32)

        for m in range(t_count):
            block = total[:, pl.ds(pl.multiple_of((t ^ m) * rows, 128), rows)]
            if m == 0:
                kept_ref[...] = block
            else:
                sent_ref[m - 1] = block.astype(jnp.bfloat16)

    return pl.pallas_call(
        kernel,
        out_shape=(
            jax.ShapeDtypeStruct((columns, rows), jnp.float32),
            jax.ShapeDtypeStruct((t_count - 1, columns, rows), jnp.bfloat16),
        ),
        in_specs=[in_smem()] + in_vmem(slots + shares + 1),
        out_specs=tuple(in_vmem(2)),
        scratch_shapes=[pltpu.VMEM((columns, slots * rows), jnp.float32)],
        compiler_params=params(8),
        cost_estimate=cost(2 * slots * rows * width * columns, 2 * width * columns),
        name="project",
    )(jnp.stack([t, s, has_share]).astype(jnp.int32), *attended, *weights, residual)


def activate(pieces, gain_table, weights, pair, t, chosen):
    slots = len(pieces)
    height, rows = pieces[0][0].shape
    depth = D // slots
    lanes = slots * rows
    experts = len(weights)
    units = weights[0].shape[1]
    cuts = cuts_of([(0,), (1,)], units, 3)

    def kernel(place_ref, *refs):
        piece_refs = refs[: slots * slots]
        table_ref = refs[slots * slots]
        weight_refs = refs[slots * slots + 1 : slots * slots + 1 + experts]
        out_ref, share_ref, rows_ref, stage_ref, routes_ref, held_ref, arrived = refs[
            slots * slots + 1 + experts :
        ]
        copies = [
            fetches(weight_refs[e], held_ref.at[e - 1], arrived.at[e - 1], cuts) for e in range(1, experts)
        ]
        for copy in sum(copies, []):
            copy.start()
        for m in range(slots):
            for r in range(slots):
                lane = pl.ds(pl.multiple_of((place_ref[1] ^ r ^ m) * rows, 128), rows)
                index = place_ref[0] ^ r
                piece_ref = piece_refs[m * slots + r]
                block = piece_ref[:depth, :]
                if aligned(depth):
                    rows_ref[pl.ds(pl.multiple_of(index * depth, 16), depth), lane] = block
                else:
                    stage_ref[index, :, lane] = block
                if not r:
                    routes_ref[:, lane] = piece_ref[depth:, :]
        if not aligned(depth):
            for index in range(slots):
                rows_ref[index * depth : (index + 1) * depth, :] = stage_ref[index]
        routes = routes_ref[...].astype(jnp.float32)
        scores = routes[TOP : 2 * TOP] * 256.0 + routes[2 * TOP : 3 * TOP]
        scores = scores / jnp.sum(scores, axis=0, keepdims=True)
        for e in range(experts):
            mine = routes[:TOP] == place_ref[2 + e].astype(jnp.float32)
            share_ref[e : e + 1, :] = jnp.sum(jnp.where(mine, scores, 0.0), axis=0, keepdims=True)
        plain = rows_ref[...].astype(jnp.float32)
        square = jnp.sum(dot(table_ref[...], (plain * plain).astype(jnp.bfloat16)), axis=0, keepdims=True)
        scale = lax.rsqrt(square / D + 1e-05)
        for e in range(experts):
            if e:
                for copy in copies[e - 1]:
                    copy.wait()
            weight_ref = held_ref.at[e - 1] if e else weight_refs[0]
            gate = dot(weight_ref[0], rows_ref[...]) * scale
            up = dot(weight_ref[1], rows_ref[...]) * scale
            out_ref[e] = ((up + 1.0) * gate * jax.nn.sigmoid(1.702 * gate)).astype(jnp.bfloat16)

    flat = [piece for part in pieces for piece in part]
    return pl.pallas_call(
        kernel,
        out_shape=(
            jax.ShapeDtypeStruct((experts, units, lanes), jnp.bfloat16),
            jax.ShapeDtypeStruct((experts, lanes), jnp.float32),
        ),
        in_specs=[in_smem()]
        + in_vmem(len(flat) + 2)
        + [pl.BlockSpec(memory_space=pl.ANY)] * (experts - 1),
        out_specs=tuple(in_vmem(2)),
        scratch_shapes=[
            pltpu.VMEM((D, lanes), jnp.bfloat16),
            pltpu.VMEM((1, 16, 128) if aligned(depth) else (slots, depth, lanes), jnp.bfloat16),
            pltpu.VMEM((height - depth, lanes), jnp.bfloat16),
            pltpu.VMEM((max(1, experts - 1), 2, units, D), jnp.bfloat16),
            pltpu.SemaphoreType.DMA((max(1, experts - 1), len(cuts))),
        ],
        compiler_params=params(13 if aligned(depth) else 16),
        cost_estimate=cost(4 * experts * lanes * D * units, 4 * experts * D * units),
        name="activate",
    )(jnp.stack([pair, t] + chosen).astype(jnp.int32), *flat, gain_table, *weights)


def combine(activated, share, weights, t, slots):
    t_count = len(activated)
    experts, units, lanes = activated[0].shape
    width = weights[0].shape[0]
    rows = lanes // slots

    def kernel(t_ref, *refs):
        activated_refs = refs[:t_count]
        share_ref = refs[t_count]
        weight_refs = refs[t_count + 1 : t_count + 1 + experts]
        *out_refs, all_ref, stage_ref = refs[t_count + 1 + experts :]
        for u in range(t_count):
            index = t_ref[0] ^ u
            if aligned(units):
                all_ref[:, pl.ds(pl.multiple_of(index * units, 16), units), :] = activated_refs[u][...]
            else:
                stage_ref[index] = activated_refs[u][...]
        if not aligned(units):
            for index in range(t_count):
                all_ref[:, index * units : (index + 1) * units, :] = stage_ref[index]
        total = 0.0
        for e in range(experts):
            result = dot(weight_refs[e][...], all_ref[e]).astype(jnp.bfloat16).astype(jnp.float32)
            total = total + share_ref[e : e + 1, :] * result
        for j in range(slots):
            out_refs[j][...] = total[:, j * rows : (j + 1) * rows].astype(jnp.bfloat16)

    return pl.pallas_call(
        kernel,
        out_shape=tuple(jax.ShapeDtypeStruct((width, rows), jnp.bfloat16) for _ in range(slots)),
        in_specs=[in_smem()] + in_vmem(t_count + 1 + experts),
        out_specs=tuple(in_vmem(slots)),
        scratch_shapes=[
            pltpu.VMEM((experts, t_count * units, lanes), jnp.bfloat16),
            pltpu.VMEM((1, 1, 16, 128) if aligned(units) else (t_count, experts, units, lanes), jnp.bfloat16),
        ],
        compiler_params=params(7 if aligned(units) else 16),
        cost_estimate=cost(
            2 * experts * lanes * t_count * units * width, 2 * experts * t_count * units * width
        ),
        name="combine",
    )(t.reshape(1), *activated, share, *weights)


def local(
    queries,
    key_rows,
    value_rows,
    sink_logits,
    out_weight,
    residual,
    norm_gain,
    expert_in,
    expert_out,
    routes,
    route_scores,
):
    rows = queries.shape[0]
    z_count, t_count, s_count = lax.axis_size("ep"), lax.axis_size("tp"), lax.axis_size("sub")
    z, t, s = (lax.axis_index(name).astype(jnp.int32) for name in ("ep", "tp", "sub"))
    columns = out_weight.shape[1]
    width = expert_out.shape[2]
    slots = t_count
    group = z_count // slots
    pair = z // group

    paired = jnp.concatenate([key_rows, value_rows], axis=1)
    earlier = shifted(paired, ("ep", "sub"), 1)
    out_weight = out_weight.T
    depth = out_weight.shape[1] // s_count
    near = lax.dynamic_slice_in_dim(out_weight, s * depth, depth, 1)
    shared = slots == 2 and group == t_count and aligned(columns)
    residual = residual.T.reshape(slots * group, columns, rows)
    kept_residual = picked(residual.reshape(slots, group * columns, rows), pair ^ t, 0)
    earlier, near, expert_in, expert_out = lax.optimization_barrier((earlier, near, expert_in, expert_out))

    near = swapped(near, "ep", 1)

    if not shared:
        route = [
            (i * t_count + k, (i ^ (group * k)) * t_count + k) for i in range(z_count) for k in range(t_count)
        ]
        kept_residual = lax.ppermute(kept_residual, ("ep", "tp"), route)

    expert_in = expert_in[0].transpose(0, 2, 1)
    expert_out = expert_out[0]
    experts_in = [expert_in] + [swapped(expert_in, "sub", e) for e in range(1, s_count)]
    experts_out = [expert_out] + [swapped(expert_out, "sub", e) for e in range(1, s_count)]
    chosen = [z * s_count + (s ^ e) for e in range(s_count)]

    first = (lax.axis_index(("ep", "sub")) == 0).astype(jnp.int32)
    below = residual if shared else residual[:, :16]
    place = jnp.stack([first, (pair ^ 1) * group + t if shared else first * 0])
    attended = attention(
        queries, earlier, key_rows, value_rows, sink_logits, place, routes.T, route_scores.T, below
    )
    gathered = [attended] + [swapped(attended, "ep", group * j) for j in range(1, slots)]
    own_share = picked(residual, pair * group + t, 0) if shared else below[0]
    own_share, _ = lax.optimization_barrier((own_share, attended))
    gathered, near, own_share, experts_out = lax.optimization_barrier((gathered, near, own_share, experts_out))
    near_weights = [near] + [swapped(near, "sub", u) for u in range(1, s_count)]
    member = z % group
    mine = project(gathered, [out_weight], own_share, (t == member) & shared, t, s * 0, t_count)
    other = project(gathered, near_weights, own_share, (t == member ^ 1) & shared, t, s, t_count)
    first_member = z % group == 0

    def ordered(a, b):
        return jnp.concatenate([jnp.where(first_member, a, b), jnp.where(first_member, b, a)], axis=0)

    span = slice(queries.shape[1], queries.shape[1] + 16)
    kept_routes = gathered[0][span]
    for j in range(1, slots):
        kept_routes = jnp.where(t == j, gathered[j][span], kept_routes)
    hidden = ordered(mine[0], other[0])
    if not shared:
        hidden = hidden + kept_residual.astype(jnp.float32)
    for m in range(1, t_count):
        received = swapped(ordered(mine[1][m - 1], other[1][m - 1]), "tp", m)
        hidden = hidden + received.astype(jnp.float32)
    gain_part = picked(norm_gain.reshape(slots, group * columns), pair, 0)
    scaled = jnp.concatenate([(hidden * gain_part[:, None]).astype(jnp.bfloat16), kept_routes], axis=0)

    own = {0: scaled}
    pieces = [own] + [{} for m in range(1, t_count)]
    distance = z_count // 2
    while distance:
        held = list(own)
        if distance >= group:
            for m in range(1, t_count):
                pieces[m].update({d: swapped(own[d], "tp", m) for d in held if d not in pieces[m]})
        for d in held:
            own[d + distance] = swapped(own[d], "ep", distance)
        distance //= 2
    for m in range(1, t_count):
        pieces[m].update({d: swapped(own[d], "tp", m) for d in range(0, z_count, group) if d not in pieces[m]})
    late = {d: own[d] for d in own if d % group and d != 1}
    late, pieces[1:] = lax.optimization_barrier((late, pieces[1:]))
    for m in range(1, t_count):
        pieces[m].update({d: swapped(late[d], "tp", m) for d in late})

    weight, _ = lax.optimization_barrier((experts_in[0], own[group]))
    experts_in[0] = fetched(weight)
    odd, _ = lax.optimization_barrier((own[1], experts_in[0]))
    for m in range(1, t_count):
        pieces[m][1] = swapped(odd, "tp", m)

    inverse_gain = 1.0 / norm_gain
    inverse_square = inverse_gain * inverse_gain
    coarse = inverse_square.astype(jnp.bfloat16)
    fine = (inverse_square - coarse.astype(jnp.float32)).astype(jnp.bfloat16)
    gain_table = jnp.concatenate([coarse[None], fine[None], jnp.zeros((14, D), jnp.bfloat16)], axis=0)

    total = 0.0
    for m in range(t_count):
        for r in range(slots):
            here = (pair == m) & ((pair ^ t) == r)
            total = total + jnp.where(here, pieces[m][group * r][:width].astype(jnp.float32), 0.0)
    total = total * lax.dynamic_slice_in_dim(inverse_gain, t * width, width, 0)[:, None]
    total = lax.optimization_barrier(total)

    units = []
    for p in range(group):
        part = [[pieces[m][group * r + p] for r in range(slots)] for m in range(t_count)]
        if units:
            part, _ = lax.optimization_barrier((part, units[-1][0][0]))
        activated, share = activate(part, gain_table, experts_in, pair, t, chosen)
        units.append(([activated] + [swapped(activated, "tp", m) for m in range(1, t_count)], share))

    experts_out, _ = lax.optimization_barrier((experts_out, units[-1][0][0]))
    experts_out = flip(experts_out)
    for p in range(group):
        activated, share = units[p]
        for j, result in enumerate(combine(activated, share, experts_out, t, slots)):
            distance = group * j + p
            result = swapped(result, "ep", distance) if distance else result
            total = total + result.astype(jnp.float32)
    return total.astype(jnp.bfloat16).T


def solution(mesh):
    in_specs = (
        P(("groups", "ep", "sub"), "tp"),
        P(("groups", "ep", "sub"), "tp"),
        P(("groups", "ep", "sub"), "tp"),
        P("tp"),
        P("tp", "ep"),
        P(("groups", "ep", "sub"), None),
        P(),
        P(("ep", "sub"), None, None, "tp"),
        P(("ep", "sub"), None, "tp"),
        P(("groups", "ep", "sub"), None),
        P(("groups", "ep", "sub"), None),
    )
    out_specs = P(("groups", "ep", "sub"), "tp")
    return jax.shard_map(local, mesh=mesh, in_specs=in_specs, out_specs=out_specs, check_vma=False)
```

```python
import jax
import jax.numpy as jnp
from jax import lax
from jax.experimental import pallas as pl
from jax.experimental.pallas import tpu as pltpu
from jax.sharding import PartitionSpec as P

D = 2880
HD = 64
WIN = 128
TOP = 4
MIB = 1024 * 1024


def shifted(block, axis, distance):
    devices = range(lax.axis_size(axis))
    route = [(i - distance, i) for i in devices if i - distance in devices]
    return lax.ppermute(block, axis, route)


def swapped(block, axis, distance):
    return lax.ppermute(block, axis, [(i, i ^ distance) for i in range(lax.axis_size(axis))])


def picked(blocks, index, axis):
    return lax.dynamic_index_in_dim(blocks, index, axis, keepdims=False)


def in_vmem(count):
    return [pl.BlockSpec(memory_space=pltpu.VMEM)] * count


def in_smem():
    return pl.BlockSpec(memory_space=pltpu.SMEM)


def cost(flops, bytes_accessed):
    return pl.CostEstimate(flops=flops, bytes_accessed=bytes_accessed, transcendentals=0)


def dot(left, right):
    return jnp.dot(left, right, preferred_element_type=jnp.float32)


def aligned(size):
    return size % 16 == 0


def fetches(source, target, arrived, cuts):
    return [
        pltpu.make_async_copy(source.at[cut], target.at[cut], arrived.at[index]) for index, cut in enumerate(cuts)
    ]


def cuts_of(lead, size, count):
    count = count if size % (16 * count) == 0 else 1
    step = size // count
    return [(*at, pl.ds(i * step, step)) for at in lead for i in range(count)]


def params(mebibytes):
    return pltpu.CompilerParams(vmem_limit_bytes=int(mebibytes * MIB))


def attention_kernel(
    place_ref, sink_ref, q_ref, earlier_ref, k_ref, v_ref, routes_ref, scores_ref, residual_ref, out_ref
):
    width = q_ref.shape[1]
    numbers = [routes_ref[...], scores_ref[...] // 256, scores_ref[...] % 256]
    numbers.append(jnp.zeros((16 - 3 * TOP, q_ref.shape[0]), jnp.int32))
    out_ref[width : width + 16, :] = jnp.concatenate(numbers, axis=0).astype(jnp.float32).astype(jnp.bfloat16)
    out_ref[width + 16 :, :] = residual_ref[place_ref[1]]
    rows = q_ref.shape[0]
    kv_count = k_ref.shape[1] // HD
    pairs = q_ref.shape[1] // (2 * HD * kv_count)
    key = lax.broadcasted_iota(jnp.int32, (rows, rows), 0)
    query = lax.broadcasted_iota(jnp.int32, (rows, rows), 1)
    before = key > query
    shut = before & (place_ref[0] == 1)
    blank = jnp.zeros((2 * rows, HD), jnp.bfloat16)
    values = jnp.concatenate(
        [
            block.astype(jnp.float32).T.astype(jnp.bfloat16)
            for block in (earlier_ref[:, kv_count * HD :], v_ref[...])
        ],
        axis=1,
    )
    for g in range(kv_count):
        head = slice(g * HD, (g + 1) * HD)
        keys = jnp.concatenate([earlier_ref[:, head], k_ref[:, head]], axis=0) * jnp.bfloat16(HD ** (-0.5))
        keys = jnp.concatenate(
            [jnp.concatenate([keys, blank], axis=1), jnp.concatenate([blank, keys], axis=1)], axis=0
        )
        for i in range(pairs):
            start = (g * pairs + i) * 2 * HD
            products = lax.dot_general(
                keys,
                q_ref[:, start : start + 2 * HD],
                (((1,), (1,)), ((), ())),
                preferred_element_type=jnp.float32,
            )
            weights = []
            for side in range(2):
                sink = sink_ref[(g * pairs + i) * 2 + side]
                part = products[side * 2 * rows : (side + 1) * 2 * rows]
                scores = jnp.where(before, part[:rows], part[rows:])
                scores = jnp.where(shut, -1e30, scores)
                largest = jnp.maximum(jnp.max(scores, axis=0, keepdims=True), sink)
                numerator = jnp.exp(scores - largest)
                denominator = jnp.sum(numerator, axis=0, keepdims=True) + jnp.exp(sink - largest)
                numerator = numerator * (1.0 / denominator)
                weights.append(
                    jnp.concatenate(
                        [
                            jnp.where(before, numerator, 0.0).astype(jnp.bfloat16),
                            jnp.where(before, 0.0, numerator).astype(jnp.bfloat16),
                        ],
                        axis=0,
                    )
                )
            result = dot(values[head], jnp.concatenate(weights, axis=1)).astype(jnp.bfloat16)
            out_ref[start : start + HD, :] = result[:, :rows]
            out_ref[start + HD : start + 2 * HD, :] = result[:, rows:]


def attention(queries, earlier, key_rows, value_rows, sink_logits, place, routes, scores, residual):
    rows, width = queries.shape
    return pl.pallas_call(
        attention_kernel,
        out_shape=jax.ShapeDtypeStruct((width + 16 + residual.shape[1], rows), jnp.bfloat16),
        in_specs=[in_smem(), in_smem()] + in_vmem(7),
        out_specs=in_vmem(1)[0],
        compiler_params=params(8),
        cost_estimate=cost(8 * rows * rows * width, 6 * rows * width),
        name="attention",
    )(place, sink_logits, queries, earlier, key_rows, value_rows, routes, scores, residual)


def flip(arrays):
    def kernel(*refs):
        for i in range(len(arrays)):
            refs[len(arrays) + i][...] = refs[i][...].T

    return pl.pallas_call(
        kernel,
        out_shape=tuple(jax.ShapeDtypeStruct(a.shape[::-1], a.dtype) for a in arrays),
        in_specs=in_vmem(len(arrays)),
        out_specs=tuple(in_vmem(len(arrays))),
        compiler_params=params(12),
        cost_estimate=cost(0, 4 * sum(a.size for a in arrays)),
        name="flip",
    )(*arrays)


def fetched(weight):
    cuts = cuts_of([(k,) for k in range(weight.shape[0])], weight.shape[1], 3)

    def kernel(weight_ref, out_ref, arrived):
        copies = fetches(weight_ref, out_ref, arrived, cuts)
        for copy in copies:
            copy.start()
        for copy in copies:
            copy.wait()

    return pl.pallas_call(
        kernel,
        out_shape=jax.ShapeDtypeStruct(weight.shape, weight.dtype),
        in_specs=[pl.BlockSpec(memory_space=pl.ANY)],
        out_specs=in_vmem(1)[0],
        scratch_shapes=[pltpu.SemaphoreType.DMA((len(cuts),))],
        compiler_params=params(2),
        cost_estimate=cost(0, 4 * weight.size),
        name="fetched",
    )(weight)


def project(attended, weights, residual, has_share, t, s, t_count):
    slots = len(attended)
    rows = attended[0].shape[1]
    columns, depth = weights[0].shape
    shares = len(weights)
    width = shares * depth

    def kernel(place_ref, *refs):
        attended_refs = refs[:slots]
        weight_refs = refs[slots : slots + shares]
        residual_ref, kept_ref, sent_ref, total = refs[slots + shares :]
        t, s = place_ref[0], place_ref[1]
        result = 0.0
        for u in range(shares):
            span = pl.ds(pl.multiple_of((s ^ u) * depth, 128), depth)
            block = jnp.concatenate([ref[span, :] for ref in attended_refs], axis=1)
            result = result + dot(weight_refs[u][...], block)
        total[...] = result

        @pl.when(place_ref[2] == 1)
        def _():
            for j in range(slots):
                share = attended_refs[j][width + 16 :, :] if j else residual_ref[...]
                if share.shape[0] == columns:
                    total[:, j * rows : (j + 1) * rows] += share.astype(jnp.float32)

        for m in range(t_count):
            block = total[:, pl.ds(pl.multiple_of((t ^ m) * rows, 128), rows)]
            if m == 0:
                kept_ref[...] = block
            else:
                sent_ref[m - 1] = block.astype(jnp.bfloat16)

    return pl.pallas_call(
        kernel,
        out_shape=(
            jax.ShapeDtypeStruct((columns, rows), jnp.float32),
            jax.ShapeDtypeStruct((t_count - 1, columns, rows), jnp.bfloat16),
        ),
        in_specs=[in_smem()] + in_vmem(slots + shares + 1),
        out_specs=tuple(in_vmem(2)),
        scratch_shapes=[pltpu.VMEM((columns, slots * rows), jnp.float32)],
        compiler_params=params(8),
        cost_estimate=cost(2 * slots * rows * width * columns, 2 * width * columns),
        name="project",
    )(jnp.stack([t, s, has_share]).astype(jnp.int32), *attended, *weights, residual)


def activate(pieces, gain_table, weights, pair, t, chosen):
    slots = len(pieces)
    height, rows = pieces[0][0].shape
    depth = D // slots
    lanes = slots * rows
    experts = len(weights)
    units = weights[0].shape[1]
    cuts = cuts_of([(0,), (1,)], units, 3)

    def kernel(place_ref, *refs):
        piece_refs = refs[: slots * slots]
        table_ref = refs[slots * slots]
        weight_refs = refs[slots * slots + 1 : slots * slots + 1 + experts]
        out_ref, share_ref, rows_ref, stage_ref, routes_ref, held_ref, arrived = refs[
            slots * slots + 1 + experts :
        ]
        copies = [
            fetches(weight_refs[e], held_ref.at[e - 1], arrived.at[e - 1], cuts) for e in range(1, experts)
        ]
        for copy in sum(copies, []):
            copy.start()
        for m in range(slots):
            for r in range(slots):
                lane = pl.ds(pl.multiple_of((place_ref[1] ^ r ^ m) * rows, 128), rows)
                index = place_ref[0] ^ r
                piece_ref = piece_refs[m * slots + r]
                block = piece_ref[:depth, :]
                if aligned(depth):
                    rows_ref[pl.ds(pl.multiple_of(index * depth, 16), depth), lane] = block
                else:
                    stage_ref[index, :, lane] = block
                if not r:
                    routes_ref[:, lane] = piece_ref[depth:, :]
        if not aligned(depth):
            for index in range(slots):
                rows_ref[index * depth : (index + 1) * depth, :] = stage_ref[index]
        routes = routes_ref[...].astype(jnp.float32)
        scores = routes[TOP : 2 * TOP] * 256.0 + routes[2 * TOP : 3 * TOP]
        scores = scores / jnp.sum(scores, axis=0, keepdims=True)
        for e in range(experts):
            mine = routes[:TOP] == place_ref[2 + e].astype(jnp.float32)
            share_ref[e : e + 1, :] = jnp.sum(jnp.where(mine, scores, 0.0), axis=0, keepdims=True)
        plain = rows_ref[...].astype(jnp.float32)
        square = jnp.sum(dot(table_ref[...], (plain * plain).astype(jnp.bfloat16)), axis=0, keepdims=True)
        scale = lax.rsqrt(square / D + 1e-05)
        for e in range(experts):
            if e:
                for copy in copies[e - 1]:
                    copy.wait()
            weight_ref = held_ref.at[e - 1] if e else weight_refs[0]
            gate = dot(weight_ref[0], rows_ref[...]) * scale
            up = dot(weight_ref[1], rows_ref[...]) * scale
            out_ref[e] = ((up + 1.0) * gate * jax.nn.sigmoid(1.702 * gate)).astype(jnp.bfloat16)

    flat = [piece for part in pieces for piece in part]
    return pl.pallas_call(
        kernel,
        out_shape=(
            jax.ShapeDtypeStruct((experts, units, lanes), jnp.bfloat16),
            jax.ShapeDtypeStruct((experts, lanes), jnp.float32),
        ),
        in_specs=[in_smem()]
        + in_vmem(len(flat) + 2)
        + [pl.BlockSpec(memory_space=pl.ANY)] * (experts - 1),
        out_specs=tuple(in_vmem(2)),
        scratch_shapes=[
            pltpu.VMEM((D, lanes), jnp.bfloat16),
            pltpu.VMEM((1, 16, 128) if aligned(depth) else (slots, depth, lanes), jnp.bfloat16),
            pltpu.VMEM((height - depth, lanes), jnp.bfloat16),
            pltpu.VMEM((max(1, experts - 1), 2, units, D), jnp.bfloat16),
            pltpu.SemaphoreType.DMA((max(1, experts - 1), len(cuts))),
        ],
        compiler_params=params(13 if aligned(depth) else 16),
        cost_estimate=cost(4 * experts * lanes * D * units, 4 * experts * D * units),
        name="activate",
    )(jnp.stack([pair, t] + chosen).astype(jnp.int32), *flat, gain_table, *weights)


def combine(activated, share, weights, t, slots):
    t_count = len(activated)
    experts, units, lanes = activated[0].shape
    width = weights[0].shape[0]
    rows = lanes // slots

    def kernel(t_ref, *refs):
        activated_refs = refs[:t_count]
        share_ref = refs[t_count]
        weight_refs = refs[t_count + 1 : t_count + 1 + experts]
        *out_refs, all_ref, stage_ref = refs[t_count + 1 + experts :]
        for u in range(t_count):
            index = t_ref[0] ^ u
            if aligned(units):
                all_ref[:, pl.ds(pl.multiple_of(index * units, 16), units), :] = activated_refs[u][...]
            else:
                stage_ref[index] = activated_refs[u][...]
        if not aligned(units):
            for index in range(t_count):
                all_ref[:, index * units : (index + 1) * units, :] = stage_ref[index]
        total = 0.0
        for e in range(experts):
            result = dot(weight_refs[e][...], all_ref[e]).astype(jnp.bfloat16).astype(jnp.float32)
            total = total + share_ref[e : e + 1, :] * result
        for j in range(slots):
            out_refs[j][...] = total[:, j * rows : (j + 1) * rows].astype(jnp.bfloat16)

    return pl.pallas_call(
        kernel,
        out_shape=tuple(jax.ShapeDtypeStruct((width, rows), jnp.bfloat16) for _ in range(slots)),
        in_specs=[in_smem()] + in_vmem(t_count + 1 + experts),
        out_specs=tuple(in_vmem(slots)),
        scratch_shapes=[
            pltpu.VMEM((experts, t_count * units, lanes), jnp.bfloat16),
            pltpu.VMEM((1, 1, 16, 128) if aligned(units) else (t_count, experts, units, lanes), jnp.bfloat16),
        ],
        compiler_params=params(7 if aligned(units) else 16),
        cost_estimate=cost(
            2 * experts * lanes * t_count * units * width, 2 * experts * t_count * units * width
        ),
        name="combine",
    )(t.reshape(1), *activated, share, *weights)


def local(
    queries,
    key_rows,
    value_rows,
    sink_logits,
    out_weight,
    residual,
    norm_gain,
    expert_in,
    expert_out,
    routes,
    route_scores,
):
    rows = queries.shape[0]
    z_count, t_count, s_count = lax.axis_size("ep"), lax.axis_size("tp"), lax.axis_size("sub")
    z, t, s = (lax.axis_index(name).astype(jnp.int32) for name in ("ep", "tp", "sub"))
    columns = out_weight.shape[1]
    width = expert_out.shape[2]
    slots = t_count
    group = z_count // slots
    pair = z // group

    paired = jnp.concatenate([key_rows, value_rows], axis=1)
    earlier = shifted(paired, ("ep", "sub"), 1)
    out_weight = out_weight.T
    depth = out_weight.shape[1] // s_count
    near = lax.dynamic_slice_in_dim(out_weight, s * depth, depth, 1)
    shared = slots == 2 and group == t_count and aligned(columns)
    residual = residual.T.reshape(slots * group, columns, rows)
    kept_residual = picked(residual.reshape(slots, group * columns, rows), pair ^ t, 0)
    earlier, near, expert_in, expert_out = lax.optimization_barrier((earlier, near, expert_in, expert_out))

    near = swapped(near, "ep", 1)

    if not shared:
        route = [
            (i * t_count + k, (i ^ (group * k)) * t_count + k) for i in range(z_count) for k in range(t_count)
        ]
        kept_residual = lax.ppermute(kept_residual, ("ep", "tp"), route)

    expert_in = expert_in[0].transpose(0, 2, 1)
    expert_out = expert_out[0]
    experts_in = [expert_in] + [swapped(expert_in, "sub", e) for e in range(1, s_count)]
    experts_out = [expert_out] + [swapped(expert_out, "sub", e) for e in range(1, s_count)]
    chosen = [z * s_count + (s ^ e) for e in range(s_count)]

    first = (lax.axis_index(("ep", "sub")) == 0).astype(jnp.int32)
    below = residual if shared else residual[:, :16]
    place = jnp.stack([first, (pair ^ 1) * group + t if shared else first * 0])
    attended = attention(
        queries, earlier, key_rows, value_rows, sink_logits, place, routes.T, route_scores.T, below
    )
    gathered = [attended] + [swapped(attended, "ep", group * j) for j in range(1, slots)]
    own_share = picked(residual, pair * group + t, 0) if shared else below[0]
    own_share, _ = lax.optimization_barrier((own_share, attended))
    gathered, near, own_share, experts_out = lax.optimization_barrier((gathered, near, own_share, experts_out))
    near_weights = [near] + [swapped(near, "sub", u) for u in range(1, s_count)]
    member = z % group
    mine = project(gathered, [out_weight], own_share, (t == member) & shared, t, s * 0, t_count)
    other = project(gathered, near_weights, own_share, (t == member ^ 1) & shared, t, s, t_count)
    first_member = z % group == 0

    def ordered(a, b):
        return jnp.concatenate([jnp.where(first_member, a, b), jnp.where(first_member, b, a)], axis=0)

    span = slice(queries.shape[1], queries.shape[1] + 16)
    kept_routes = gathered[0][span]
    for j in range(1, slots):
        kept_routes = jnp.where(t == j, gathered[j][span], kept_routes)
    hidden = ordered(mine[0], other[0])
    if not shared:
        hidden = hidden + kept_residual.astype(jnp.float32)
    for m in range(1, t_count):
        received = swapped(ordered(mine[1][m - 1], other[1][m - 1]), "tp", m)
        hidden = hidden + received.astype(jnp.float32)
    gain_part = picked(norm_gain.reshape(slots, group * columns), pair, 0)
    scaled = jnp.concatenate([(hidden * gain_part[:, None]).astype(jnp.bfloat16), kept_routes], axis=0)

    own = {0: scaled}
    pieces = [own] + [{} for m in range(1, t_count)]
    distance = z_count // 2
    while distance:
        held = list(own)
        if distance >= group:
            for m in range(1, t_count):
                pieces[m].update({d: swapped(own[d], "tp", m) for d in held if d not in pieces[m]})
        for d in held:
            own[d + distance] = swapped(own[d], "ep", distance)
        distance //= 2
    for m in range(1, t_count):
        pieces[m].update({d: swapped(own[d], "tp", m) for d in range(0, z_count, group) if d not in pieces[m]})
        pieces[m].update({d: swapped(own[d], "tp", m) for d in own if d % group and d != 1})

    weight, _ = lax.optimization_barrier((experts_in[0], own[group]))
    experts_in[0] = fetched(weight)
    handed, _ = lax.optimization_barrier(([part[0] for part in pieces[1:]], [experts_in[0], own[1]]))
    for m in range(1, t_count):
        pieces[m][1] = swapped(handed[m - 1], "ep", 1)

    inverse_gain = 1.0 / norm_gain
    inverse_square = inverse_gain * inverse_gain
    coarse = inverse_square.astype(jnp.bfloat16)
    fine = (inverse_square - coarse.astype(jnp.float32)).astype(jnp.bfloat16)
    gain_table = jnp.concatenate([coarse[None], fine[None], jnp.zeros((14, D), jnp.bfloat16)], axis=0)

    total = 0.0
    for m in range(t_count):
        for r in range(slots):
            here = (pair == m) & ((pair ^ t) == r)
            total = total + jnp.where(here, pieces[m][group * r][:width].astype(jnp.float32), 0.0)
    total = total * lax.dynamic_slice_in_dim(inverse_gain, t * width, width, 0)[:, None]
    total = lax.optimization_barrier(total)

    units = []
    for p in range(group):
        part = [[pieces[m][group * r + p] for r in range(slots)] for m in range(t_count)]
        if units:
            part, _ = lax.optimization_barrier((part, units[-1][0][0]))
        activated, share = activate(part, gain_table, experts_in, pair, t, chosen)
        units.append(([activated] + [swapped(activated, "tp", m) for m in range(1, t_count)], share))

    experts_out, _ = lax.optimization_barrier((experts_out, units[-1][0][0]))
    experts_out = flip(experts_out)
    for p in range(group):
        activated, share = units[p]
        for j, result in enumerate(combine(activated, share, experts_out, t, slots)):
            distance = group * j + p
            result = swapped(result, "ep", distance) if distance else result
            total = total + result.astype(jnp.float32)
    return total.astype(jnp.bfloat16).T


def solution(mesh):
    in_specs = (
        P(("groups", "ep", "sub"), "tp"),
        P(("groups", "ep", "sub"), "tp"),
        P(("groups", "ep", "sub"), "tp"),
        P("tp"),
        P("tp", "ep"),
        P(("groups", "ep", "sub"), None),
        P(),
        P(("ep", "sub"), None, None, "tp"),
        P(("ep", "sub"), None, "tp"),
        P(("groups", "ep", "sub"), None),
        P(("groups", "ep", "sub"), None),
    )
    out_specs = P(("groups", "ep", "sub"), "tp")
    return jax.shard_map(local, mesh=mesh, in_specs=in_specs, out_specs=out_specs, check_vma=False)
```

```python
import jax
import jax.numpy as jnp
from jax import lax
from jax.experimental import pallas as pl
from jax.experimental.pallas import tpu as pltpu
from jax.sharding import PartitionSpec as P

D = 2880
HD = 64
WIN = 128
TOP = 4
MIB = 1024 * 1024


def shifted(block, axis, distance):
    devices = range(lax.axis_size(axis))
    route = [(i - distance, i) for i in devices if i - distance in devices]
    return lax.ppermute(block, axis, route)


def swapped(block, axis, distance):
    return lax.ppermute(block, axis, [(i, i ^ distance) for i in range(lax.axis_size(axis))])


def picked(blocks, index, axis):
    return lax.dynamic_index_in_dim(blocks, index, axis, keepdims=False)


def in_vmem(count):
    return [pl.BlockSpec(memory_space=pltpu.VMEM)] * count


def in_smem():
    return pl.BlockSpec(memory_space=pltpu.SMEM)


def cost(flops, bytes_accessed):
    return pl.CostEstimate(flops=flops, bytes_accessed=bytes_accessed, transcendentals=0)


def dot(left, right):
    return jnp.dot(left, right, preferred_element_type=jnp.float32)


def aligned(size):
    return size % 16 == 0


def fetches(source, target, arrived, cuts):
    return [
        pltpu.make_async_copy(source.at[cut], target.at[cut], arrived.at[index]) for index, cut in enumerate(cuts)
    ]


def cuts_of(lead, size, count):
    count = count if size % (16 * count) == 0 else 1
    step = size // count
    return [(*at, pl.ds(i * step, step)) for at in lead for i in range(count)]


def params(mebibytes):
    return pltpu.CompilerParams(vmem_limit_bytes=int(mebibytes * MIB))


def attention_kernel(
    place_ref, sink_ref, q_ref, earlier_ref, k_ref, v_ref, routes_ref, scores_ref, residual_ref, out_ref
):
    width = q_ref.shape[1]
    numbers = [routes_ref[...], scores_ref[...] // 256, scores_ref[...] % 256]
    numbers.append(jnp.zeros((16 - 3 * TOP, q_ref.shape[0]), jnp.int32))
    out_ref[width : width + 16, :] = jnp.concatenate(numbers, axis=0).astype(jnp.float32).astype(jnp.bfloat16)
    out_ref[width + 16 :, :] = residual_ref[place_ref[1]]
    rows = q_ref.shape[0]
    kv_count = k_ref.shape[1] // HD
    pairs = q_ref.shape[1] // (2 * HD * kv_count)
    key = lax.broadcasted_iota(jnp.int32, (rows, rows), 0)
    query = lax.broadcasted_iota(jnp.int32, (rows, rows), 1)
    before = key > query
    shut = before & (place_ref[0] == 1)
    blank = jnp.zeros((2 * rows, HD), jnp.bfloat16)
    values = jnp.concatenate(
        [
            block.astype(jnp.float32).T.astype(jnp.bfloat16)
            for block in (earlier_ref[:, kv_count * HD :], v_ref[...])
        ],
        axis=1,
    )
    for g in range(kv_count):
        head = slice(g * HD, (g + 1) * HD)
        keys = jnp.concatenate([earlier_ref[:, head], k_ref[:, head]], axis=0) * jnp.bfloat16(HD ** (-0.5))
        keys = jnp.concatenate(
            [jnp.concatenate([keys, blank], axis=1), jnp.concatenate([blank, keys], axis=1)], axis=0
        )
        for i in range(pairs):
            start = (g * pairs + i) * 2 * HD
            products = lax.dot_general(
                keys,
                q_ref[:, start : start + 2 * HD],
                (((1,), (1,)), ((), ())),
                preferred_element_type=jnp.float32,
            )
            weights = []
            for side in range(2):
                sink = sink_ref[(g * pairs + i) * 2 + side]
                part = products[side * 2 * rows : (side + 1) * 2 * rows]
                scores = jnp.where(before, part[:rows], part[rows:])
                scores = jnp.where(shut, -1e30, scores)
                largest = jnp.maximum(jnp.max(scores, axis=0, keepdims=True), sink)
                numerator = jnp.exp(scores - largest)
                denominator = jnp.sum(numerator, axis=0, keepdims=True) + jnp.exp(sink - largest)
                numerator = numerator * (1.0 / denominator)
                weights.append(
                    jnp.concatenate(
                        [
                            jnp.where(before, numerator, 0.0).astype(jnp.bfloat16),
                            jnp.where(before, 0.0, numerator).astype(jnp.bfloat16),
                        ],
                        axis=0,
                    )
                )
            result = dot(values[head], jnp.concatenate(weights, axis=1)).astype(jnp.bfloat16)
            out_ref[start : start + HD, :] = result[:, :rows]
            out_ref[start + HD : start + 2 * HD, :] = result[:, rows:]


def attention(queries, earlier, key_rows, value_rows, sink_logits, place, routes, scores, residual):
    rows, width = queries.shape
    return pl.pallas_call(
        attention_kernel,
        out_shape=jax.ShapeDtypeStruct((width + 16 + residual.shape[1], rows), jnp.bfloat16),
        in_specs=[in_smem(), in_smem()] + in_vmem(7),
        out_specs=in_vmem(1)[0],
        compiler_params=params(8),
        cost_estimate=cost(8 * rows * rows * width, 6 * rows * width),
        name="attention",
    )(place, sink_logits, queries, earlier, key_rows, value_rows, routes, scores, residual)


def flip(arrays, t, t_count):
    units, width = arrays[0].shape[0] // t_count, arrays[0].shape[1]
    count = len(arrays)

    def kernel(t_ref, *refs):
        for i in range(count):
            for u in range(t_count):
                refs[count + i * t_count + u][...] = refs[i][t_ref[0] ^ u].T

    out = pl.pallas_call(
        kernel,
        out_shape=tuple(jax.ShapeDtypeStruct((width, units), arrays[0].dtype) for _ in range(count * t_count)),
        in_specs=[in_smem()] + in_vmem(count),
        out_specs=tuple(in_vmem(count * t_count)),
        compiler_params=params(12),
        cost_estimate=cost(0, 4 * sum(a.size for a in arrays)),
        name="flip",
    )(t.reshape(1), *[a.reshape(t_count, units, width) for a in arrays])
    return [out[i * t_count : (i + 1) * t_count] for i in range(count)]


def fetched(weight):
    cuts = cuts_of([(k,) for k in range(weight.shape[0])], weight.shape[1], 3)

    def kernel(weight_ref, out_ref, arrived):
        copies = fetches(weight_ref, out_ref, arrived, cuts)
        for copy in copies:
            copy.start()
        for copy in copies:
            copy.wait()

    return pl.pallas_call(
        kernel,
        out_shape=jax.ShapeDtypeStruct(weight.shape, weight.dtype),
        in_specs=[pl.BlockSpec(memory_space=pl.ANY)],
        out_specs=in_vmem(1)[0],
        scratch_shapes=[pltpu.SemaphoreType.DMA((len(cuts),))],
        compiler_params=params(2),
        cost_estimate=cost(0, 4 * weight.size),
        name="fetched",
    )(weight)


def project(attended, weights, residual, has_share, t, s, t_count):
    slots = len(attended)
    rows = attended[0].shape[1]
    columns, depth = weights[0].shape
    shares = len(weights)
    width = shares * depth

    def kernel(place_ref, *refs):
        attended_refs = refs[:slots]
        weight_refs = refs[slots : slots + shares]
        residual_ref, kept_ref, sent_ref, total = refs[slots + shares :]
        t, s = place_ref[0], place_ref[1]
        result = 0.0
        for u in range(shares):
            span = pl.ds(pl.multiple_of((s ^ u) * depth, 128), depth)
            block = jnp.concatenate([ref[span, :] for ref in attended_refs], axis=1)
            result = result + dot(weight_refs[u][...], block)
        total[...] = result

        @pl.when(place_ref[2] == 1)
        def _():
            for j in range(slots):
                share = attended_refs[j][width + 16 :, :] if j else residual_ref[...]
                if share.shape[0] == columns:
                    total[:, j * rows : (j + 1) * rows] += share.astype(jnp.float32)

        for m in range(t_count):
            block = total[:, pl.ds(pl.multiple_of((t ^ m) * rows, 128), rows)]
            if m == 0:
                kept_ref[...] = block
            else:
                sent_ref[m - 1] = block.astype(jnp.bfloat16)

    return pl.pallas_call(
        kernel,
        out_shape=(
            jax.ShapeDtypeStruct((columns, rows), jnp.float32),
            jax.ShapeDtypeStruct((t_count - 1, columns, rows), jnp.bfloat16),
        ),
        in_specs=[in_smem()] + in_vmem(slots + shares + 1),
        out_specs=tuple(in_vmem(2)),
        scratch_shapes=[pltpu.VMEM((columns, slots * rows), jnp.float32)],
        compiler_params=params(8),
        cost_estimate=cost(2 * slots * rows * width * columns, 2 * width * columns),
        name="project",
    )(jnp.stack([t, s, has_share]).astype(jnp.int32), *attended, *weights, residual)


def activate(pieces, gain_table, weights, pair, t, chosen):
    slots = len(pieces)
    height, rows = pieces[0][0].shape
    depth = D // slots
    lanes = slots * rows
    experts = len(weights)
    units = weights[0].shape[1]
    cuts = cuts_of([(0,), (1,)], units, 3)

    def kernel(place_ref, *refs):
        piece_refs = refs[: slots * slots]
        table_ref = refs[slots * slots]
        weight_refs = refs[slots * slots + 1 : slots * slots + 1 + experts]
        out_ref, share_ref, rows_ref, stage_ref, routes_ref, held_ref, arrived = refs[
            slots * slots + 1 + experts :
        ]
        copies = [
            fetches(weight_refs[e], held_ref.at[e - 1], arrived.at[e - 1], cuts) for e in range(1, experts)
        ]
        for copy in sum(copies, []):
            copy.start()
        for m in range(slots):
            for r in range(slots):
                lane = pl.ds(pl.multiple_of((place_ref[1] ^ r ^ m) * rows, 128), rows)
                index = place_ref[0] ^ r
                piece_ref = piece_refs[m * slots + r]
                block = piece_ref[:depth, :]
                if aligned(depth):
                    rows_ref[pl.ds(pl.multiple_of(index * depth, 16), depth), lane] = block
                else:
                    stage_ref[index, :, lane] = block
                if not r:
                    routes_ref[:, lane] = piece_ref[depth:, :]
        if not aligned(depth):
            for index in range(slots):
                rows_ref[index * depth : (index + 1) * depth, :] = stage_ref[index]
        routes = routes_ref[...].astype(jnp.float32)
        scores = routes[TOP : 2 * TOP] * 256.0 + routes[2 * TOP : 3 * TOP]
        scores = scores / jnp.sum(scores, axis=0, keepdims=True)
        for e in range(experts):
            mine = routes[:TOP] == place_ref[2 + e].astype(jnp.float32)
            share_ref[e : e + 1, :] = jnp.sum(jnp.where(mine, scores, 0.0), axis=0, keepdims=True)
        plain = rows_ref[...].astype(jnp.float32)
        square = jnp.sum(dot(table_ref[...], (plain * plain).astype(jnp.bfloat16)), axis=0, keepdims=True)
        scale = lax.rsqrt(square / D + 1e-05)
        for e in range(experts):
            if e:
                for copy in copies[e - 1]:
                    copy.wait()
            weight_ref = held_ref.at[e - 1] if e else weight_refs[0]
            gate = dot(weight_ref[0], rows_ref[...]) * scale
            up = dot(weight_ref[1], rows_ref[...]) * scale
            out_ref[e] = ((up + 1.0) * gate * jax.nn.sigmoid(1.702 * gate)).astype(jnp.bfloat16)

    flat = [piece for part in pieces for piece in part]
    return pl.pallas_call(
        kernel,
        out_shape=(
            jax.ShapeDtypeStruct((experts, units, lanes), jnp.bfloat16),
            jax.ShapeDtypeStruct((experts, lanes), jnp.float32),
        ),
        in_specs=[in_smem()]
        + in_vmem(len(flat) + 2)
        + [pl.BlockSpec(memory_space=pl.ANY)] * (experts - 1),
        out_specs=tuple(in_vmem(2)),
        scratch_shapes=[
            pltpu.VMEM((D, lanes), jnp.bfloat16),
            pltpu.VMEM((1, 16, 128) if aligned(depth) else (slots, depth, lanes), jnp.bfloat16),
            pltpu.VMEM((height - depth, lanes), jnp.bfloat16),
            pltpu.VMEM((max(1, experts - 1), 2, units, D), jnp.bfloat16),
            pltpu.SemaphoreType.DMA((max(1, experts - 1), len(cuts))),
        ],
        compiler_params=params(13 if aligned(depth) else 16),
        cost_estimate=cost(4 * experts * lanes * D * units, 4 * experts * D * units),
        name="activate",
    )(jnp.stack([pair, t] + chosen).astype(jnp.int32), *flat, gain_table, *weights)


def own_part(activated, weights):
    experts, units, lanes = activated.shape
    width = weights[0].shape[0]

    def kernel(activated_ref, *refs):
        for e in range(experts):
            refs[experts][e] = dot(refs[e][...], activated_ref[e])

    return pl.pallas_call(
        kernel,
        out_shape=jax.ShapeDtypeStruct((experts, width, lanes), jnp.float32),
        in_specs=in_vmem(1 + experts),
        out_specs=in_vmem(1)[0],
        compiler_params=params(7 if aligned(units) else 16),
        cost_estimate=cost(2 * experts * lanes * units * width, 2 * experts * units * width),
        name="own_part",
    )(activated, *weights)


def combine(part, activated, share, weights, slots):
    others = len(activated)
    experts, units, lanes = activated[0].shape
    width = part.shape[1]
    rows = lanes // slots

    def kernel(part_ref, share_ref, *refs):
        activated_refs, weight_refs = refs[:others], refs[others : others + others * experts]
        out_refs = refs[others + others * experts :]
        total = 0.0
        for e in range(experts):
            result = part_ref[e]
            for u in range(others):
                result = result + dot(weight_refs[u * experts + e][...], activated_refs[u][e])
            total = total + share_ref[e : e + 1, :] * result.astype(jnp.bfloat16).astype(jnp.float32)
        for j in range(slots):
            out_refs[j][...] = total[:, j * rows : (j + 1) * rows].astype(jnp.bfloat16)

    return pl.pallas_call(
        kernel,
        out_shape=tuple(jax.ShapeDtypeStruct((width, rows), jnp.bfloat16) for _ in range(slots)),
        in_specs=in_vmem(2 + others + others * experts),
        out_specs=tuple(in_vmem(slots)),
        compiler_params=params(8 if aligned(units) else 16),
        cost_estimate=cost(4 * experts * lanes * others * units * width, 4 * experts * others * units * width),
        name="combine",
    )(part, share, *activated, *[w for unit in weights for w in unit])


def local(
    queries,
    key_rows,
    value_rows,
    sink_logits,
    out_weight,
    residual,
    norm_gain,
    expert_in,
    expert_out,
    routes,
    route_scores,
):
    rows = queries.shape[0]
    z_count, t_count, s_count = lax.axis_size("ep"), lax.axis_size("tp"), lax.axis_size("sub")
    z, t, s = (lax.axis_index(name).astype(jnp.int32) for name in ("ep", "tp", "sub"))
    columns = out_weight.shape[1]
    width = expert_out.shape[2]
    slots = t_count
    group = z_count // slots
    pair = z // group

    paired = jnp.concatenate([key_rows, value_rows], axis=1)
    earlier = shifted(paired, ("ep", "sub"), 1)
    out_weight = out_weight.T
    depth = out_weight.shape[1] // s_count
    near = lax.dynamic_slice_in_dim(out_weight, s * depth, depth, 1)
    shared = slots == 2 and group == t_count and aligned(columns)
    residual = residual.T.reshape(slots * group, columns, rows)
    kept_residual = picked(residual.reshape(slots, group * columns, rows), pair ^ t, 0)
    earlier, near, expert_in, expert_out = lax.optimization_barrier((earlier, near, expert_in, expert_out))

    near = swapped(near, "ep", 1)

    if not shared:
        route = [
            (i * t_count + k, (i ^ (group * k)) * t_count + k) for i in range(z_count) for k in range(t_count)
        ]
        kept_residual = lax.ppermute(kept_residual, ("ep", "tp"), route)

    expert_in = expert_in[0].transpose(0, 2, 1)
    expert_out = expert_out[0]
    experts_in = [expert_in] + [swapped(expert_in, "sub", e) for e in range(1, s_count)]
    experts_out = [expert_out] + [swapped(expert_out, "sub", e) for e in range(1, s_count)]
    chosen = [z * s_count + (s ^ e) for e in range(s_count)]

    first = (lax.axis_index(("ep", "sub")) == 0).astype(jnp.int32)
    below = residual if shared else residual[:, :16]
    place = jnp.stack([first, (pair ^ 1) * group + t if shared else first * 0])
    attended = attention(
        queries, earlier, key_rows, value_rows, sink_logits, place, routes.T, route_scores.T, below
    )
    gathered = [attended] + [swapped(attended, "ep", group * j) for j in range(1, slots)]
    own_share = picked(residual, pair * group + t, 0) if shared else below[0]
    own_share, _ = lax.optimization_barrier((own_share, attended))
    gathered, near, own_share, experts_out = lax.optimization_barrier((gathered, near, own_share, experts_out))
    near_weights = [near] + [swapped(near, "sub", u) for u in range(1, s_count)]
    member = z % group
    mine = project(gathered, [out_weight], own_share, (t == member) & shared, t, s * 0, t_count)
    other = project(gathered, near_weights, own_share, (t == member ^ 1) & shared, t, s, t_count)
    first_member = z % group == 0

    def ordered(a, b):
        return jnp.concatenate([jnp.where(first_member, a, b), jnp.where(first_member, b, a)], axis=0)

    span = slice(queries.shape[1], queries.shape[1] + 16)
    kept_routes = gathered[0][span]
    for j in range(1, slots):
        kept_routes = jnp.where(t == j, gathered[j][span], kept_routes)
    hidden = ordered(mine[0], other[0])
    if not shared:
        hidden = hidden + kept_residual.astype(jnp.float32)
    for m in range(1, t_count):
        received = swapped(ordered(mine[1][m - 1], other[1][m - 1]), "tp", m)
        hidden = hidden + received.astype(jnp.float32)
    gain_part = picked(norm_gain.reshape(slots, group * columns), pair, 0)
    scaled = jnp.concatenate([(hidden * gain_part[:, None]).astype(jnp.bfloat16), kept_routes], axis=0)

    own = {0: scaled}
    pieces = [own] + [{} for m in range(1, t_count)]
    distance = z_count // 2
    while distance:
        held = list(own)
        if distance >= group:
            for m in range(1, t_count):
                pieces[m].update({d: swapped(own[d], "tp", m) for d in held if d not in pieces[m]})
        for d in held:
            own[d + distance] = swapped(own[d], "ep", distance)
        distance //= 2
    for m in range(1, t_count):
        pieces[m].update({d: swapped(own[d], "tp", m) for d in range(0, z_count, group) if d not in pieces[m]})
        pieces[m].update({d: swapped(own[d], "tp", m) for d in own if d % group and d != 1})

    weight, _ = lax.optimization_barrier((experts_in[0], own[group]))
    experts_in[0] = fetched(weight)
    handed, _ = lax.optimization_barrier(([part[0] for part in pieces[1:]], [experts_in[0], own[1]]))
    for m in range(1, t_count):
        pieces[m][1] = swapped(handed[m - 1], "ep", 1)

    inverse_gain = 1.0 / norm_gain
    inverse_square = inverse_gain * inverse_gain
    coarse = inverse_square.astype(jnp.bfloat16)
    fine = (inverse_square - coarse.astype(jnp.float32)).astype(jnp.bfloat16)
    gain_table = jnp.concatenate([coarse[None], fine[None], jnp.zeros((14, D), jnp.bfloat16)], axis=0)

    total = 0.0
    for m in range(t_count):
        for r in range(slots):
            here = (pair == m) & ((pair ^ t) == r)
            total = total + jnp.where(here, pieces[m][group * r][:width].astype(jnp.float32), 0.0)
    total = total * lax.dynamic_slice_in_dim(inverse_gain, t * width, width, 0)[:, None]
    total = lax.optimization_barrier(total)

    units = []
    for p in range(group):
        part = [[pieces[m][group * r + p] for r in range(slots)] for m in range(t_count)]
        if units:
            part, _ = lax.optimization_barrier((part, units[-1][0][0]))
        activated, share = activate(part, gain_table, experts_in, pair, t, chosen)
        units.append(([activated] + [swapped(activated, "tp", m) for m in range(1, t_count)], share))

    experts_out, _ = lax.optimization_barrier((experts_out, units[-1][0][0]))
    flipped = flip(experts_out, t, t_count)
    others = [[weight[u] for weight in flipped] for u in range(1, t_count)]
    results = None
    for p in range(group):
        activated, share = units[p]
        mine = activated[0]
        if results is not None:
            mine, _ = lax.optimization_barrier((mine, results[0]))
        part = own_part(mine, [weight[0] for weight in flipped])
        results = combine(part, activated[1:], share, others, slots)
        for j, result in enumerate(results):
            distance = group * j + p
            result = swapped(result, "ep", distance) if distance else result
            total = total + result.astype(jnp.float32)
        total = lax.optimization_barrier(total) if p < group - 1 else total
    return total.astype(jnp.bfloat16).T


def solution(mesh):
    in_specs = (
        P(("groups", "ep", "sub"), "tp"),
        P(("groups", "ep", "sub"), "tp"),
        P(("groups", "ep", "sub"), "tp"),
        P("tp"),
        P("tp", "ep"),
        P(("groups", "ep", "sub"), None),
        P(),
        P(("ep", "sub"), None, None, "tp"),
        P(("ep", "sub"), None, "tp"),
        P(("groups", "ep", "sub"), None),
        P(("groups", "ep", "sub"), None),
    )
    out_specs = P(("groups", "ep", "sub"), "tp")
    return jax.shard_map(local, mesh=mesh, in_specs=in_specs, out_specs=out_specs, check_vma=False)
```

```python
import jax
import jax.numpy as jnp
from jax import lax
from jax.experimental import pallas as pl
from jax.experimental.pallas import tpu as pltpu
from jax.sharding import PartitionSpec as P

D = 2880
HD = 64
WIN = 128
TOP = 4
MIB = 1024 * 1024


def shifted(block, axis, distance):
    devices = range(lax.axis_size(axis))
    route = [(i - distance, i) for i in devices if i - distance in devices]
    return lax.ppermute(block, axis, route)


def swapped(block, axis, distance):
    return lax.ppermute(block, axis, [(i, i ^ distance) for i in range(lax.axis_size(axis))])


def picked(blocks, index, axis):
    return lax.dynamic_index_in_dim(blocks, index, axis, keepdims=False)


def in_vmem(count):
    return [pl.BlockSpec(memory_space=pltpu.VMEM)] * count


def in_smem():
    return pl.BlockSpec(memory_space=pltpu.SMEM)


def cost(flops, bytes_accessed):
    return pl.CostEstimate(flops=flops, bytes_accessed=bytes_accessed, transcendentals=0)


def dot(left, right):
    return jnp.dot(left, right, preferred_element_type=jnp.float32)


def aligned(size):
    return size % 16 == 0


def fetches(source, target, arrived, cuts):
    return [
        pltpu.make_async_copy(source.at[cut], target.at[cut], arrived.at[index]) for index, cut in enumerate(cuts)
    ]


def cuts_of(lead, size, count):
    count = count if size % (16 * count) == 0 else 1
    step = size // count
    return [(*at, pl.ds(i * step, step)) for at in lead for i in range(count)]


def params(mebibytes):
    return pltpu.CompilerParams(vmem_limit_bytes=int(mebibytes * MIB))


def attention_kernel(
    place_ref, sink_ref, q_ref, earlier_ref, k_ref, v_ref, routes_ref, scores_ref, residual_ref, out_ref
):
    width = q_ref.shape[1]
    numbers = [routes_ref[...], scores_ref[...] // 256, scores_ref[...] % 256]
    numbers.append(jnp.zeros((16 - 3 * TOP, q_ref.shape[0]), jnp.int32))
    out_ref[width : width + 16, :] = jnp.concatenate(numbers, axis=0).astype(jnp.float32).astype(jnp.bfloat16)
    out_ref[width + 16 :, :] = residual_ref[place_ref[1]]
    rows = q_ref.shape[0]
    kv_count = k_ref.shape[1] // HD
    pairs = q_ref.shape[1] // (2 * HD * kv_count)
    key = lax.broadcasted_iota(jnp.int32, (rows, rows), 0)
    query = lax.broadcasted_iota(jnp.int32, (rows, rows), 1)
    before = key > query
    shut = before & (place_ref[0] == 1)
    blank = jnp.zeros((2 * rows, HD), jnp.bfloat16)
    values = jnp.concatenate(
        [
            block.astype(jnp.float32).T.astype(jnp.bfloat16)
            for block in (earlier_ref[:, kv_count * HD :], v_ref[...])
        ],
        axis=1,
    )
    for g in range(kv_count):
        head = slice(g * HD, (g + 1) * HD)
        keys = jnp.concatenate([earlier_ref[:, head], k_ref[:, head]], axis=0) * jnp.bfloat16(HD ** (-0.5))
        keys = jnp.concatenate(
            [jnp.concatenate([keys, blank], axis=1), jnp.concatenate([blank, keys], axis=1)], axis=0
        )
        for i in range(pairs):
            start = (g * pairs + i) * 2 * HD
            products = lax.dot_general(
                keys,
                q_ref[:, start : start + 2 * HD],
                (((1,), (1,)), ((), ())),
                preferred_element_type=jnp.float32,
            )
            weights = []
            for side in range(2):
                sink = sink_ref[(g * pairs + i) * 2 + side]
                part = products[side * 2 * rows : (side + 1) * 2 * rows]
                scores = jnp.where(before, part[:rows], part[rows:])
                scores = jnp.where(shut, -1e30, scores)
                largest = jnp.maximum(jnp.max(scores, axis=0, keepdims=True), sink)
                numerator = jnp.exp(scores - largest)
                denominator = jnp.sum(numerator, axis=0, keepdims=True) + jnp.exp(sink - largest)
                numerator = numerator * (1.0 / denominator)
                weights.append(
                    jnp.concatenate(
                        [
                            jnp.where(before, numerator, 0.0).astype(jnp.bfloat16),
                            jnp.where(before, 0.0, numerator).astype(jnp.bfloat16),
                        ],
                        axis=0,
                    )
                )
            result = dot(values[head], jnp.concatenate(weights, axis=1)).astype(jnp.bfloat16)
            out_ref[start : start + HD, :] = result[:, :rows]
            out_ref[start + HD : start + 2 * HD, :] = result[:, rows:]


def attention(queries, earlier, key_rows, value_rows, sink_logits, place, routes, scores, residual):
    rows, width = queries.shape
    return pl.pallas_call(
        attention_kernel,
        out_shape=jax.ShapeDtypeStruct((width + 16 + residual.shape[1], rows), jnp.bfloat16),
        in_specs=[in_smem(), in_smem()] + in_vmem(7),
        out_specs=in_vmem(1)[0],
        compiler_params=params(8),
        cost_estimate=cost(8 * rows * rows * width, 6 * rows * width),
        name="attention",
    )(place, sink_logits, queries, earlier, key_rows, value_rows, routes, scores, residual)


def flip(arrays, t, t_count):
    units, width = arrays[0].shape[0] // t_count, arrays[0].shape[1]
    count = len(arrays)

    def kernel(t_ref, *refs):
        for i in range(count):
            for u in range(t_count):
                refs[count + i * t_count + u][...] = refs[i][t_ref[0] ^ u].T

    out = pl.pallas_call(
        kernel,
        out_shape=tuple(jax.ShapeDtypeStruct((width, units), arrays[0].dtype) for _ in range(count * t_count)),
        in_specs=[in_smem()] + in_vmem(count),
        out_specs=tuple(in_vmem(count * t_count)),
        compiler_params=params(8),
        cost_estimate=cost(0, 4 * sum(a.size for a in arrays)),
        name="flip",
    )(t.reshape(1), *[a.reshape(t_count, units, width) for a in arrays])
    return [out[i * t_count : (i + 1) * t_count] for i in range(count)]


def fetched(weight):
    cuts = cuts_of([(k,) for k in range(weight.shape[0])], weight.shape[1], 3)

    def kernel(weight_ref, out_ref, arrived):
        copies = fetches(weight_ref, out_ref, arrived, cuts)
        for copy in copies:
            copy.start()
        for copy in copies:
            copy.wait()

    return pl.pallas_call(
        kernel,
        out_shape=jax.ShapeDtypeStruct(weight.shape, weight.dtype),
        in_specs=[pl.BlockSpec(memory_space=pl.ANY)],
        out_specs=in_vmem(1)[0],
        scratch_shapes=[pltpu.SemaphoreType.DMA((len(cuts),))],
        compiler_params=params(2),
        cost_estimate=cost(0, 4 * weight.size),
        name="fetched",
    )(weight)


def project(attended, weights, residual, has_share, t, s, t_count):
    slots = len(attended)
    rows = attended[0].shape[1]
    columns, depth = weights[0].shape
    shares = len(weights)
    width = shares * depth

    def kernel(place_ref, *refs):
        attended_refs = refs[:slots]
        weight_refs = refs[slots : slots + shares]
        residual_ref, kept_ref, sent_ref, total = refs[slots + shares :]
        t, s = place_ref[0], place_ref[1]
        result = 0.0
        for u in range(shares):
            span = pl.ds(pl.multiple_of((s ^ u) * depth, 128), depth)
            block = jnp.concatenate([ref[span, :] for ref in attended_refs], axis=1)
            result = result + dot(weight_refs[u][...], block)
        total[...] = result

        @pl.when(place_ref[2] == 1)
        def _():
            for j in range(slots):
                share = attended_refs[j][width + 16 :, :] if j else residual_ref[...]
                if share.shape[0] == columns:
                    total[:, j * rows : (j + 1) * rows] += share.astype(jnp.float32)

        for m in range(t_count):
            block = total[:, pl.ds(pl.multiple_of((t ^ m) * rows, 128), rows)]
            if m == 0:
                kept_ref[...] = block
            else:
                sent_ref[m - 1] = block.astype(jnp.bfloat16)

    return pl.pallas_call(
        kernel,
        out_shape=(
            jax.ShapeDtypeStruct((columns, rows), jnp.float32),
            jax.ShapeDtypeStruct((t_count - 1, columns, rows), jnp.bfloat16),
        ),
        in_specs=[in_smem()] + in_vmem(slots + shares + 1),
        out_specs=tuple(in_vmem(2)),
        scratch_shapes=[pltpu.VMEM((columns, slots * rows), jnp.float32)],
        compiler_params=params(8),
        cost_estimate=cost(2 * slots * rows * width * columns, 2 * width * columns),
        name="project",
    )(jnp.stack([t, s, has_share]).astype(jnp.int32), *attended, *weights, residual)


def activate(pieces, gain_table, weights, pair, t, chosen):
    slots = len(pieces)
    height, rows = pieces[0][0].shape
    depth = D // slots
    lanes = slots * rows
    experts = len(weights)
    units = weights[0].shape[1]
    cuts = cuts_of([(0,), (1,)], units, 3)

    def kernel(place_ref, *refs):
        piece_refs = refs[: slots * slots]
        table_ref = refs[slots * slots]
        weight_refs = refs[slots * slots + 1 : slots * slots + 1 + experts]
        out_ref, share_ref, rows_ref, stage_ref, routes_ref, held_ref, arrived = refs[
            slots * slots + 1 + experts :
        ]
        copies = [
            fetches(weight_refs[e], held_ref.at[e - 1], arrived.at[e - 1], cuts) for e in range(1, experts)
        ]
        for copy in sum(copies, []):
            copy.start()
        for m in range(slots):
            for r in range(slots):
                lane = pl.ds(pl.multiple_of((place_ref[1] ^ r ^ m) * rows, 128), rows)
                index = place_ref[0] ^ r
                piece_ref = piece_refs[m * slots + r]
                block = piece_ref[:depth, :]
                if aligned(depth):
                    rows_ref[pl.ds(pl.multiple_of(index * depth, 16), depth), lane] = block
                else:
                    stage_ref[index, :, lane] = block
                if not r:
                    routes_ref[:, lane] = piece_ref[depth:, :]
        if not aligned(depth):
            for index in range(slots):
                rows_ref[index * depth : (index + 1) * depth, :] = stage_ref[index]
        routes = routes_ref[...].astype(jnp.float32)
        scores = routes[TOP : 2 * TOP] * 256.0 + routes[2 * TOP : 3 * TOP]
        scores = scores / jnp.sum(scores, axis=0, keepdims=True)
        for e in range(experts):
            mine = routes[:TOP] == place_ref[2 + e].astype(jnp.float32)
            share_ref[e : e + 1, :] = jnp.sum(jnp.where(mine, scores, 0.0), axis=0, keepdims=True)
        plain = rows_ref[...].astype(jnp.float32)
        square = jnp.sum(dot(table_ref[...], (plain * plain).astype(jnp.bfloat16)), axis=0, keepdims=True)
        scale = lax.rsqrt(square / D + 1e-05)
        for e in range(experts):
            if e:
                for copy in copies[e - 1]:
                    copy.wait()
            weight_ref = held_ref.at[e - 1] if e else weight_refs[0]
            gate = dot(weight_ref[0], rows_ref[...]) * scale
            up = dot(weight_ref[1], rows_ref[...]) * scale
            out_ref[e] = ((up + 1.0) * gate * jax.nn.sigmoid(1.702 * gate)).astype(jnp.bfloat16)

    flat = [piece for part in pieces for piece in part]
    return pl.pallas_call(
        kernel,
        out_shape=(
            jax.ShapeDtypeStruct((experts, units, lanes), jnp.bfloat16),
            jax.ShapeDtypeStruct((experts, lanes), jnp.float32),
        ),
        in_specs=[in_smem()]
        + in_vmem(len(flat) + 2)
        + [pl.BlockSpec(memory_space=pl.ANY)] * (experts - 1),
        out_specs=tuple(in_vmem(2)),
        scratch_shapes=[
            pltpu.VMEM((D, lanes), jnp.bfloat16),
            pltpu.VMEM((1, 16, 128) if aligned(depth) else (slots, depth, lanes), jnp.bfloat16),
            pltpu.VMEM((height - depth, lanes), jnp.bfloat16),
            pltpu.VMEM((max(1, experts - 1), 2, units, D), jnp.bfloat16),
            pltpu.SemaphoreType.DMA((max(1, experts - 1), len(cuts))),
        ],
        compiler_params=params(12 if aligned(depth) else 16),
        cost_estimate=cost(4 * experts * lanes * D * units, 4 * experts * D * units),
        name="activate",
    )(jnp.stack([pair, t] + chosen).astype(jnp.int32), *flat, gain_table, *weights)


def own_part(activated, weights):
    experts, units, lanes = activated.shape
    width = weights[0].shape[0]

    def kernel(activated_ref, *refs):
        for e in range(experts):
            refs[experts][e] = dot(refs[e][...], activated_ref[e])

    return pl.pallas_call(
        kernel,
        out_shape=jax.ShapeDtypeStruct((experts, width, lanes), jnp.float32),
        in_specs=in_vmem(1 + experts),
        out_specs=in_vmem(1)[0],
        compiler_params=params(4 if aligned(units) else 16),
        cost_estimate=cost(2 * experts * lanes * units * width, 2 * experts * units * width),
        name="own_part",
    )(activated, *weights)


def combine(part, activated, share, weights, slots):
    others = len(activated)
    experts, units, lanes = activated[0].shape
    width = part.shape[1]
    rows = lanes // slots

    def kernel(part_ref, share_ref, *refs):
        activated_refs, weight_refs = refs[:others], refs[others : others + others * experts]
        out_refs = refs[others + others * experts :]
        total = 0.0
        for e in range(experts):
            result = part_ref[e]
            for u in range(others):
                result = result + dot(weight_refs[u * experts + e][...], activated_refs[u][e])
            total = total + share_ref[e : e + 1, :] * result.astype(jnp.bfloat16).astype(jnp.float32)
        for j in range(slots):
            out_refs[j][...] = total[:, j * rows : (j + 1) * rows].astype(jnp.bfloat16)

    return pl.pallas_call(
        kernel,
        out_shape=tuple(jax.ShapeDtypeStruct((width, rows), jnp.bfloat16) for _ in range(slots)),
        in_specs=in_vmem(2 + others + others * experts),
        out_specs=tuple(in_vmem(slots)),
        compiler_params=params(6 if aligned(units) else 16),
        cost_estimate=cost(4 * experts * lanes * others * units * width, 4 * experts * others * units * width),
        name="combine",
    )(part, share, *activated, *[w for unit in weights for w in unit])


def local(
    queries,
    key_rows,
    value_rows,
    sink_logits,
    out_weight,
    residual,
    norm_gain,
    expert_in,
    expert_out,
    routes,
    route_scores,
):
    rows = queries.shape[0]
    z_count, t_count, s_count = lax.axis_size("ep"), lax.axis_size("tp"), lax.axis_size("sub")
    z, t, s = (lax.axis_index(name).astype(jnp.int32) for name in ("ep", "tp", "sub"))
    columns = out_weight.shape[1]
    width = expert_out.shape[2]
    slots = t_count
    group = z_count // slots
    pair = z // group

    paired = jnp.concatenate([key_rows, value_rows], axis=1)
    earlier = shifted(paired, ("ep", "sub"), 1)
    out_weight = out_weight.T
    depth = out_weight.shape[1] // s_count
    near = lax.dynamic_slice_in_dim(out_weight, s * depth, depth, 1)
    shared = slots == 2 and group == t_count and aligned(columns)
    residual = residual.T.reshape(slots * group, columns, rows)
    kept_residual = picked(residual.reshape(slots, group * columns, rows), pair ^ t, 0)
    earlier, near, expert_in, expert_out = lax.optimization_barrier((earlier, near, expert_in, expert_out))

    near = swapped(near, "ep", 1)

    if not shared:
        route = [
            (i * t_count + k, (i ^ (group * k)) * t_count + k) for i in range(z_count) for k in range(t_count)
        ]
        kept_residual = lax.ppermute(kept_residual, ("ep", "tp"), route)

    expert_in = expert_in[0].transpose(0, 2, 1)
    expert_out = expert_out[0]
    experts_in = [expert_in] + [swapped(expert_in, "sub", e) for e in range(1, s_count)]
    experts_out = [expert_out] + [swapped(expert_out, "sub", e) for e in range(1, s_count)]
    chosen = [z * s_count + (s ^ e) for e in range(s_count)]

    first = (lax.axis_index(("ep", "sub")) == 0).astype(jnp.int32)
    below = residual if shared else residual[:, :16]
    place = jnp.stack([first, (pair ^ 1) * group + t if shared else first * 0])
    attended = attention(
        queries, earlier, key_rows, value_rows, sink_logits, place, routes.T, route_scores.T, below
    )
    gathered = [attended] + [swapped(attended, "ep", group * j) for j in range(1, slots)]
    own_share = picked(residual, pair * group + t, 0) if shared else below[0]
    own_share, _ = lax.optimization_barrier((own_share, attended))
    gathered, near, own_share, experts_out = lax.optimization_barrier((gathered, near, own_share, experts_out))
    near_weights = [near] + [swapped(near, "sub", u) for u in range(1, s_count)]
    member = z % group
    mine = project(gathered, [out_weight], own_share, (t == member) & shared, t, s * 0, t_count)
    other = project(gathered, near_weights, own_share, (t == member ^ 1) & shared, t, s, t_count)
    first_member = z % group == 0

    def ordered(a, b):
        return jnp.concatenate([jnp.where(first_member, a, b), jnp.where(first_member, b, a)], axis=0)

    span = slice(queries.shape[1], queries.shape[1] + 16)
    kept_routes = gathered[0][span]
    for j in range(1, slots):
        kept_routes = jnp.where(t == j, gathered[j][span], kept_routes)
    hidden = ordered(mine[0], other[0])
    if not shared:
        hidden = hidden + kept_residual.astype(jnp.float32)
    for m in range(1, t_count):
        received = swapped(ordered(mine[1][m - 1], other[1][m - 1]), "tp", m)
        hidden = hidden + received.astype(jnp.float32)
    gain_part = picked(norm_gain.reshape(slots, group * columns), pair, 0)
    scaled = jnp.concatenate([(hidden * gain_part[:, None]).astype(jnp.bfloat16), kept_routes], axis=0)

    own = {0: scaled}
    pieces = [own] + [{} for m in range(1, t_count)]
    distance = z_count // 2
    while distance:
        held = list(own)
        if distance >= group:
            for m in range(1, t_count):
                pieces[m].update({d: swapped(own[d], "tp", m) for d in held if d not in pieces[m]})
        for d in held:
            own[d + distance] = swapped(own[d], "ep", distance)
        distance //= 2
    for m in range(1, t_count):
        pieces[m].update({d: swapped(own[d], "tp", m) for d in range(0, z_count, group) if d not in pieces[m]})
        pieces[m].update({d: swapped(own[d], "tp", m) for d in own if d % group and d != 1})

    weight, _ = lax.optimization_barrier((experts_in[0], own[group]))
    experts_in[0] = fetched(weight)
    handed, _ = lax.optimization_barrier(([part[0] for part in pieces[1:]], [experts_in[0], own[1]]))
    for m in range(1, t_count):
        pieces[m][1] = swapped(handed[m - 1], "ep", 1)

    inverse_gain = 1.0 / norm_gain
    inverse_square = inverse_gain * inverse_gain
    coarse = inverse_square.astype(jnp.bfloat16)
    fine = (inverse_square - coarse.astype(jnp.float32)).astype(jnp.bfloat16)
    gain_table = jnp.concatenate([coarse[None], fine[None], jnp.zeros((14, D), jnp.bfloat16)], axis=0)

    total = 0.0
    for m in range(t_count):
        for r in range(slots):
            here = (pair == m) & ((pair ^ t) == r)
            total = total + jnp.where(here, pieces[m][group * r][:width].astype(jnp.float32), 0.0)
    total = total * lax.dynamic_slice_in_dim(inverse_gain, t * width, width, 0)[:, None]
    total = lax.optimization_barrier(total)

    units = []
    for p in range(group):
        part = [[pieces[m][group * r + p] for r in range(slots)] for m in range(t_count)]
        if units:
            part, _ = lax.optimization_barrier((part, units[-1][0][0]))
        activated, share = activate(part, gain_table, experts_in, pair, t, chosen)
        units.append(([activated] + [swapped(activated, "tp", m) for m in range(1, t_count)], share))

    experts_out, _ = lax.optimization_barrier((experts_out, units[-1][0][0]))
    flipped = flip(experts_out, t, t_count)
    others = [[weight[u] for weight in flipped] for u in range(1, t_count)]
    results = None
    for p in range(group):
        activated, share = units[p]
        mine = activated[0]
        if results is not None:
            mine, _ = lax.optimization_barrier((mine, results[0]))
        part = own_part(mine, [weight[0] for weight in flipped])
        results = combine(part, activated[1:], share, others, slots)
        for j, result in enumerate(results):
            distance = group * j + p
            result = swapped(result, "ep", distance) if distance else result
            total = total + result.astype(jnp.float32)
        total = lax.optimization_barrier(total) if p < group - 1 else total
    return total.astype(jnp.bfloat16).T


def solution(mesh):
    in_specs = (
        P(("groups", "ep", "sub"), "tp"),
        P(("groups", "ep", "sub"), "tp"),
        P(("groups", "ep", "sub"), "tp"),
        P("tp"),
        P("tp", "ep"),
        P(("groups", "ep", "sub"), None),
        P(),
        P(("ep", "sub"), None, None, "tp"),
        P(("ep", "sub"), None, "tp"),
        P(("groups", "ep", "sub"), None),
        P(("groups", "ep", "sub"), None),
    )
    out_specs = P(("groups", "ep", "sub"), "tp")
    return jax.shard_map(local, mesh=mesh, in_specs=in_specs, out_specs=out_specs, check_vma=False)
```
